32 devices in a mesh: dp: 8 (over z, y), tensor: 4 (over x, core).
Axes of the slice: x: 2, y: 2, z: 4, core: 2. Of those that a mesh axis runs over, the one named last changes fastest.
Arguments:
- tokens: bfloat16 [4096, 1024], P(('dp', 'tensor')), may hold values from -6 to 6
- key_mask: int32 [4096], P('dp'), may hold values 0 or 1
- seq_lengths: int32 [8, 4], P('dp'), may hold values from 0 to 512, as said below
- w_query: bfloat16 [1024, 1024], P('dp', 'tensor'), may hold values from -0.1875 to 0.1875
- b_query: float32 [1024], P('tensor'), may hold values from -3 to 3
- w_key: bfloat16 [1024, 1024], P('dp', 'tensor'), may hold values from -0.1875 to 0.1875
- w_value: bfloat16 [1024, 1024], P('dp', 'tensor'), may hold values from -0.1875 to 0.1875
- b_value: float32 [1024], P('tensor'), may hold values from -0.625 to 0.625
- w_proj: bfloat16 [1024, 1024], P('tensor', 'dp'), may hold values from -1.5 to 1.5
- b_proj: float32 [1024], replicated, may hold values from -1.75 to 1.75
- gain_attn: float32 [1024], replicated, may hold values from 0.1 to 1.9
- shift_attn: float32 [1024], replicated, may hold values from -1.75 to 1.75
- w_inner: bfloat16 [1024, 4096], P('dp', 'tensor'), may hold values from -0.1875 to 0.1875
- b_inner: float32 [4096], P('tensor'), may hold values from -1.75 to 1.75
- w_outer: bfloat16 [4096, 1024], P('tensor', 'dp'), may hold values from -0.09375 to 0.09375
- b_outer: float32 [1024], replicated, may hold values from -1.75 to 1.75
- gain_ffn: float32 [1024], replicated, may hold values from 0.1 to 1.9
- shift_ffn: float32 [1024], replicated, may hold values from -1.75 to 1.75
- out_grad: bfloat16 [4096, 1024], P(('dp', 'tensor')), may hold values from -6 to 6
Outputs:
- layer_out: bfloat16 [4096, 1024], P(('dp', 'tensor'))
- tokens_grad: float32 [4096, 1024], P(('dp', 'tensor'))
- dw_query: float32 [1024, 1024], P('dp', 'tensor')
- db_query: float32 [1024], P('tensor')
- dw_key: float32 [1024, 1024], P('dp', 'tensor')
- dw_value: float32 [1024, 1024], P('dp', 'tensor')
- db_value: float32 [1024], P('tensor')
- dw_proj: float32 [1024, 1024], P('tensor', 'dp')
- db_proj: float32 [1024], replicated
- dgain_attn: float32 [1024], replicated
- dshift_attn: float32 [1024], replicated
- dw_inner: float32 [1024, 4096], P('dp', 'tensor')
- db_inner: float32 [4096], P('tensor')
- dw_outer: float32 [4096, 1024], P('tensor', 'dp')
- db_outer: float32 [1024], replicated
- dgain_ffn: float32 [1024], replicated
- dshift_ffn: float32 [1024], replicated
The draws below stay inside these ranges and needn't reach their ends.
Inputs may be any that keep to these rules, and one draw needn't show every extreme that they name: `seq_lengths`: in every data group the lengths sum to 512 or less; the rows after that sum are padding. In every group one sequence starts at row 96 or earlier and ends after row 3 * 512 // 4 (that row belongs to it); in some group it is the only one and fills all 512 rows.
All inputs are finite; a program needn't handle non-finite values. No bound on the sum of `key_mask` on one device may be relied on, other than what follows from the above.
Results may differ from the reference program's by a relative error of at most 0.015.
Values may be sent and summed in bfloat16 or wider, within the bound.
No kernel may reach another device: no remote copies, remote signals or barrier semaphores. Data moves between devices by JAX's collectives and lax.ppermute only.
A program may use at most 128 MiB of HBM per device.

```python
import jax
import jax.numpy as jnp
from jax import lax

D = 1024
HEADS = 16
HEAD_DIM = 64
FF = 4096
ROWS = 512
SLOTS = 4
TOKENS = 4096
N_DP = 8


def draw_seq_lengths(key, part):
    key = jax.random.fold_in(key, 11)
    key_short, key_pad, key_slot, key_full = jax.random.split(key, 4)
    shorts = jax.random.randint(key_short, (N_DP, SLOTS), 0, ROWS // 16 + 1)
    padding = jax.random.randint(key_pad, (N_DP,), 0, ROWS // 16)
    long_slot = jax.random.randint(key_slot, (N_DP,), 0, SLOTS)
    full_group = jax.random.randint(key_full, (), 0, N_DP)
    is_full = jnp.arange(N_DP) == full_group
    slot_ids = jnp.arange(SLOTS)
    is_long = slot_ids[None, :] == long_slot[:, None]
    shorts = jnp.where(is_long | is_full[:, None], 0, shorts)
    padding = jnp.where(is_full, 0, padding)
    long_len = ROWS - padding - jnp.sum(shorts, axis=1)
    return jnp.where(is_long, long_len[:, None], shorts).astype(jnp.int32)


def place_ends(drawn, rng, least, top_value):
    shape = drawn.shape
    spot = [jax.random.randint(jax.random.fold_in(rng, axis), (), 0, shape[axis]) for axis in range(len(shape))]
    drawn = drawn.at[tuple(spot)].set(least)
    longest = shape.index(max(shape))
    spot[longest] = (spot[longest] + 1) % shape[longest]
    return drawn.at[tuple(spot)].set(top_value)


def strengthened(drawn, own_key, source, target, shards_of, factor):
    owner, partner = [(jnp.arange(drawn.shape[dim]) // (drawn.shape[dim] // shards_of)).reshape([-1 if axis == dim else 1 for axis in range(drawn.ndim)]) for dim in (source, target)]
    chosen = jax.random.permutation(own_key, shards_of)[partner]
    strong = (owner == chosen) | (owner == (partner + shards_of // 2) % shards_of)
    return jnp.where(strong, factor * drawn, drawn)


def shard_levels(key, shape, cuts, smallest, largest):
    loudness, own = 1.0, jax.random.fold_in(key, 6)
    for dim, parts in cuts:
        steps = jnp.exp(jax.random.uniform(jax.random.fold_in(own, dim), (parts,), jnp.float32, smallest / len(cuts), largest / len(cuts)))
        loudness = loudness * jnp.repeat(steps, shape[dim] // parts).reshape([-1 if axis == dim else 1 for axis in range(len(shape))])
    return loudness


def noise(own_key, dims, scale, most, pieces=(), kind=jnp.bfloat16):
    entries = jax.random.normal(own_key, dims, jnp.float32) * scale
    if len(pieces) > 0:
        entries = shard_levels(own_key, dims, pieces, -0.22, 0.18) * entries
    return jnp.clip(entries, min=-most, max=most).astype(kind)


def gaussian_with(stream_key, extent, deviation, reach, shards, heavy, kind=jnp.bfloat16):
    entries = deviation * jax.random.normal(stream_key, extent, jnp.float32)
    if shards:
        entries = entries * shard_levels(stream_key, extent, shards, -0.22, 0.18)
    return jnp.clip(strengthened(entries, jax.random.fold_in(stream_key, 3), *heavy), -reach, reach).astype(kind)


def setup_inputs(seed: int = 0) -> dict:
    arg_keys = jax.random.split(jax.random.key(seed), 20)
    return {
        "tokens": gaussian_with(arg_keys[0], (TOKENS, D), 1.0, 6.0, ((0, 32),), (0, 1, 32, 2.75)),
        "key_mask": place_ends((jax.random.randint(arg_keys[1], (TOKENS,), 0, 8) < 7).astype(jnp.int32), jax.random.fold_in(arg_keys[1], 1), 0, 1),
        "seq_lengths": draw_seq_lengths(jax.random.fold_in(arg_keys[19], 71), 0),
        "w_query": noise(arg_keys[3], (D, D), D ** -0.5, 0.1875, ((0, 8), (1, 4))),
        "b_query": noise(arg_keys[4], (D,), 0.5, 3.0, ((0, 4),), jnp.float32),
        "w_key": noise(arg_keys[5], (D, D), D ** -0.5, 0.1875, ((0, 8), (1, 4))),
        "w_value": noise(arg_keys[6], (D, D), D ** -0.5, 0.1875, ((0, 8), (1, 4))),
        "b_value": noise(arg_keys[7], (D,), 0.1, 0.625, ((0, 4),), jnp.float32),
        "w_proj": noise(arg_keys[8], (D, D), (max(1, D * 8 // ROWS)) ** -0.5, 1.5, ((0, 4), (1, 8))),
        "b_proj": noise(arg_keys[9], (D,), 0.3, 1.75, (), jnp.float32),
        "gain_attn": jnp.clip(1.0 + 0.18 * jax.random.normal(arg_keys[10], (D,), jnp.float32), 0.1, 1.9),
        "shift_attn": noise(arg_keys[11], (D,), 0.3, 1.75, (), jnp.float32),
        "w_inner": noise(arg_keys[12], (D, FF), D ** -0.5, 0.1875, ((0, 8), (1, 4))),
        "b_inner": noise(arg_keys[13], (FF,), 0.3, 1.75, ((0, 4),), jnp.float32),
        "w_outer": noise(arg_keys[14], (FF, D), FF ** -0.5, 0.09375, ((0, 4), (1, 8))),
        "b_outer": noise(arg_keys[15], (D,), 0.3, 1.75, (), jnp.float32),
        "gain_ffn": jnp.clip(1.0 + 0.18 * jax.random.normal(arg_keys[16], (D,), jnp.float32), 0.1, 1.9),
        "shift_ffn": noise(arg_keys[17], (D,), 0.3, 1.75, (), jnp.float32),
        "out_grad": gaussian_with(arg_keys[18], (TOKENS, D), 1.0, 6.0, ((0, 32),), (0, 1, 32, 2.75)),
    }


highest = lax.Precision.HIGHEST
epsilon = 1e-12
masked_fill = -1e+30

@jax.custom_vjp
def low(v):
    return lax.optimization_barrier(v.astype(jnp.bfloat16)).astype(jnp.float32)

@jax.custom_vjp
def low_back(v):
    return v

def low_keep(v):
    return (low(v), None)

def low_pass(kept, grad):
    return (grad,)

def back_keep(v):
    return (v, None)

def back_low(kept, grad):
    return (low(grad),)
low.defvjp(low_keep, low_pass)
low_back.defvjp(back_keep, back_low)

def matmul(left_side, right_side):
    return jnp.dot(left_side, right_side, precision=highest)

def layer_norm(values_in, norm_gain, norm_shift):
    centred = values_in - lax.optimization_barrier(jnp.mean(values_in, axis=-1, keepdims=True))
    spread = lax.optimization_barrier(jnp.mean(centred * centred, axis=-1, keepdims=True))
    return centred * lax.rsqrt(spread + epsilon) * norm_gain + norm_shift

def segment_table(seq_lengths, group_rows):
    slot_ends = jnp.cumsum(seq_lengths, axis=1).astype(jnp.int32)
    places = jnp.arange(group_rows, dtype=jnp.int32)
    return lax.optimization_barrier(jnp.sum((places[None, :, None] >= slot_ends[:, None, :]).astype(jnp.int32), axis=2))

def group_layer(params, packed):
    w_query, b_query, w_key, w_value, b_value, w_proj, b_proj, gain_attn, shift_attn, w_inner, b_inner, w_outer, b_outer, gain_ffn, shift_ffn = params
    group_tokens, segment, key_mask = packed
    group_rows = group_tokens.shape[0]
    head_scale = HEAD_DIM ** (-0.5)
    query_rows = low_back(low((matmul(group_tokens, w_query) + b_query) * head_scale))
    key_rows = low_back(low(matmul(group_tokens, w_key)))
    value_rows = low_back(low(matmul(group_tokens, w_value) + b_value))
    query_heads = query_rows.reshape(group_rows, HEADS, HEAD_DIM)
    key_heads = key_rows.reshape(group_rows, HEADS, HEAD_DIM)
    value_heads = value_rows.reshape(group_rows, HEADS, HEAD_DIM)
    scores = low_back(jnp.einsum('qhd,khd->hqk', query_heads, key_heads, precision=highest))
    places = jnp.arange(group_rows, dtype=jnp.int32)
    allowed = (segment[:, None] == segment[None, :]) & ((key_mask[None, :] == 1) | (places[:, None] == places[None, :]))
    scores = jnp.where(allowed[None], scores, masked_fill)
    row_top = lax.optimization_barrier(jnp.max(scores, axis=2, keepdims=True))
    weights = jnp.exp(scores - row_top)
    attn_probs = low(weights / lax.optimization_barrier(jnp.sum(weights, axis=2, keepdims=True)))
    context = jnp.einsum('hqk,khd->qhd', attn_probs, value_heads, precision=highest)
    context = low_back(low(context.reshape(group_rows, HEADS * HEAD_DIM)))
    attended = low_back(matmul(context, w_proj) + b_proj)
    first_norm = layer_norm(group_tokens + attended, gain_attn, shift_attn)
    hidden = low_back(matmul(low(first_norm), w_inner) + b_inner)
    active = low(jax.nn.gelu(hidden, approximate=False))
    branch = low_back(matmul(active, w_outer) + b_outer)
    second = layer_norm(first_norm + branch, gain_ffn, shift_ffn)
    valid_rows = (segment < SLOTS).astype(second.dtype)
    return second * valid_rows[:, None]

def reference(tokens, key_mask, seq_lengths, w_query, b_query, w_key, w_value, b_value, w_proj, b_proj, gain_attn, shift_attn, w_inner, b_inner, w_outer, b_outer, gain_ffn, shift_ffn, out_grad):
    groups = seq_lengths.shape[0]
    group_rows = tokens.shape[0] // groups
    model_width = tokens.shape[1]
    segments = segment_table(seq_lengths.astype(jnp.int32), group_rows)
    mask_rows = key_mask.astype(jnp.int32).reshape(groups, group_rows)
    params = (w_query.astype(jnp.float32), b_query.astype(jnp.float32), w_key.astype(jnp.float32), w_value.astype(jnp.float32), b_value.astype(jnp.float32), w_proj.astype(jnp.float32), b_proj.astype(jnp.float32), gain_attn.astype(jnp.float32), shift_attn.astype(jnp.float32), w_inner.astype(jnp.float32), b_inner.astype(jnp.float32), w_outer.astype(jnp.float32), b_outer.astype(jnp.float32), gain_ffn.astype(jnp.float32), shift_ffn.astype(jnp.float32))

    def forward(inputs, layer_params):

        def one_group(packed):
            return group_layer(layer_params, packed)
        grouped = inputs.reshape(groups, group_rows, model_width)
        outputs = lax.map(jax.checkpoint(one_group), (grouped, segments, mask_rows))
        return outputs.reshape(groups * group_rows, model_width)
    result, pullback = jax.vjp(forward, tokens.astype(jnp.float32), params)
    tokens_grad, weight_grads = pullback(out_grad.astype(jnp.float32))
    return (result.astype(jnp.bfloat16), tokens_grad, weight_grads[0], weight_grads[1], weight_grads[2], weight_grads[3], weight_grads[4], weight_grads[5], weight_grads[6], weight_grads[7], weight_grads[8], weight_grads[9], weight_grads[10], weight_grads[11], weight_grads[12], weight_grads[13], weight_grads[14])
```

```python
from functools import partial

import jax
import jax.numpy as jnp
from jax import lax
from jax.sharding import PartitionSpec as P

HEAD_DIM = 64


epsilon = 1e-12
masked_fill = -1e30


def layer_norm(values_in, norm_gain, norm_shift):
    centred = values_in - jnp.mean(values_in, axis=-1, keepdims=True)
    spread = jnp.mean(centred * centred, axis=-1, keepdims=True)
    return centred * lax.rsqrt(spread + epsilon) * norm_gain + norm_shift


def matmul(left_side, right_side):
    return jnp.dot(left_side, right_side, preferred_element_type=jnp.float32)


def matmul_nt(left_side, right_side):
    return lax.dot_general(
        left_side, right_side, (((1,), (1,)), ((), ())), preferred_element_type=jnp.float32
    )


def matmul_tn(left_side, right_side):
    return lax.dot_general(
        left_side, right_side, (((0,), (0,)), ((), ())), preferred_element_type=jnp.float32
    )


def swap(block, axis_name, offset):
    count = lax.axis_size(axis_name)
    return lax.ppermute(block, axis_name, [(i, i ^ offset) for i in range(count)])


def after(blocks, marks):
    return lax.optimization_barrier((blocks, marks))[0]


def gather_rows(piece):
    across = swap(piece, "tensor", 2)
    beside = swap(piece, "tensor", 1)
    corner = swap(across, "tensor", 1)
    return jnp.concatenate([piece, beside, across, corner], axis=0)


def scatter_rows(partial_sums):
    rows = partial_sums.shape[0] // 4
    own, beside, across, corner = (partial_sums[k * rows : (k + 1) * rows] for k in range(4))
    far = across + swap(corner.astype(jnp.bfloat16), "tensor", 1).astype(jnp.float32)
    near = own + swap(beside.astype(jnp.bfloat16), "tensor", 1).astype(jnp.float32)
    return near + swap(far.astype(jnp.bfloat16), "tensor", 2).astype(jnp.float32)


def sum_rows_ranks(vector):
    vector = vector + swap(vector, "tensor", 1)
    return vector + swap(vector, "tensor", 2)


def stage_offsets(count):
    bits = count.bit_length() - 1
    stages, bit = [], 1
    while bit < bits:
        width = min(2, bits - bit)
        stages.append([k << bit for k in range(1, 1 << width)])
        bit += width
    return stages


def slot_order(count):
    return list(range(0, count, 2)) + list(range(1, count, 2))


def gather_even(shard):
    held = [([0], shard)]
    for stage in stage_offsets(lax.axis_size("dp")):
        offsets = [o for some, _ in held for o in some]
        block = held[0][1] if len(held) == 1 else jnp.concatenate([b for _, b in held], axis=0)
        for offset in stage:
            held.append(([o ^ offset for o in offsets], swap(block, "dp", offset)))
    return held


def gather_odd(held):
    return [([o ^ 1 for o in offsets], swap(block, "dp", 1)) for offsets, block in held]


def whole_of(even, odd):
    return jnp.concatenate([block for _, block in even + odd], axis=0)


def scatter_shards(partial_sums):
    half = partial_sums.shape[0] // 2
    sums = partial_sums[:half] + swap(
        partial_sums[half:].astype(jnp.bfloat16), "dp", 1
    ).astype(jnp.float32)
    for stage in reversed(stage_offsets(lax.axis_size("dp"))):
        rows = sums.shape[0] // (len(stage) + 1)
        kept = sums[:rows]
        for place, offset in enumerate(stage, 1):
            piece = sums[place * rows : (place + 1) * rows].astype(jnp.bfloat16)
            kept = kept + swap(piece, "dp", offset).astype(jnp.float32)
        sums = kept
    return sums


def sum_dp_ranks(vector):
    offset = 1
    while offset < lax.axis_size("dp"):
        vector = vector + swap(vector, "dp", offset)
        offset *= 2
    return vector


def to_slots(array):
    count, rank = lax.axis_size("dp"), lax.axis_index("dp")
    width = array.shape[-1] // count
    return jnp.concatenate(
        [
            lax.dynamic_slice_in_dim(array, (rank ^ o) * width, width, array.ndim - 1)
            for o in slot_order(count)
        ],
        axis=-1,
    )


def from_slots(array):
    count, rank = lax.axis_size("dp"), lax.axis_index("dp")
    width = array.shape[-1] // count
    pieces = []
    for block in range(count):
        offset = rank ^ block
        place = offset // 2 + (count // 2) * (offset % 2)
        pieces.append(lax.dynamic_slice_in_dim(array, place * width, width, array.ndim - 1))
    return jnp.concatenate(pieces, axis=-1)


def masked_scores(query_heads, key_heads, allowed):
    scores = jnp.einsum("qhd,khd->hqk", query_heads, key_heads, preferred_element_type=jnp.float32)
    return jnp.where(allowed[None], scores, masked_fill)


def on_device(
    tokens,
    key_mask,
    seq_lengths,
    w_query,
    b_query,
    w_key,
    w_value,
    b_value,
    w_proj,
    b_proj,
    gain_attn,
    shift_attn,
    w_inner,
    b_inner,
    w_outer,
    b_outer,
    gain_ffn,
    shift_ffn,
    out_grad,
):
    tensor_count = lax.axis_size("tensor")
    tensor_rank = lax.axis_index("tensor")
    piece_rows = tokens.shape[0]
    group_rows = piece_rows * tensor_count
    slot_count = seq_lengths.shape[1]
    head_width = b_query.shape[0]
    local_heads = head_width // HEAD_DIM
    inner_width = b_inner.shape[0]
    head_scale = HEAD_DIM ** (-0.5)

    qkv_even = gather_even(jnp.concatenate([w_query, w_key, w_value], axis=1))
    tokens = to_slots(tokens)
    token_rows = gather_rows(tokens)
    qkv_odd = gather_odd(qkv_even)
    qkv_full = whole_of(qkv_even, qkv_odd)
    ffn_shards = jnp.concatenate([w_proj.T, w_inner, w_outer.T], axis=1)
    ffn_even = gather_even(after(ffn_shards, [block for _, block in qkv_even]))
    ffn_odd = gather_odd(ffn_even)
    ffn_full = whole_of(ffn_even, ffn_odd)
    proj_full_t = ffn_full[:, :head_width]
    inner_full = ffn_full[:, head_width : head_width + inner_width]
    outer_full_t = ffn_full[:, head_width + inner_width :]

    out_grad = to_slots(out_grad)
    small = to_slots(jnp.stack([b_proj, gain_attn, shift_attn, b_outer, gain_ffn, shift_ffn]))
    b_proj, gain_attn, shift_attn, b_outer, gain_ffn, shift_ffn = (small[k] for k in range(6))

    steps = jnp.arange(piece_rows, dtype=jnp.int32)
    places = jnp.concatenate([(tensor_rank ^ k) * piece_rows + steps for k in range(tensor_count)])
    key_rows = jnp.concatenate(
        [
            lax.dynamic_slice_in_dim(key_mask, (tensor_rank ^ k) * piece_rows, piece_rows, 0)
            for k in range(tensor_count)
        ]
    )
    slot_ends = jnp.cumsum(seq_lengths[0])
    segment = jnp.sum((places[:, None] >= slot_ends[None, :]).astype(jnp.int32), axis=1)
    allowed = (segment[:, None] == segment[None, :]) & (
        (key_rows[None, :] == 1) | (places[:, None] == places[None, :])
    )
    valid_piece = (segment[:piece_rows] < slot_count).astype(jnp.float32)[:, None]

    qkv = matmul(token_rows, qkv_full)
    query_low = ((qkv[:, :head_width] + b_query) * head_scale).astype(jnp.bfloat16)
    key_low = qkv[:, head_width : 2 * head_width].astype(jnp.bfloat16)
    value_low = (qkv[:, 2 * head_width :] + b_value).astype(jnp.bfloat16)
    query_heads = query_low.reshape(group_rows, local_heads, HEAD_DIM)
    key_heads = key_low.reshape(group_rows, local_heads, HEAD_DIM)
    value_heads = value_low.reshape(group_rows, local_heads, HEAD_DIM)
    scores = masked_scores(query_heads, key_heads, allowed)
    row_top = jnp.max(scores, axis=2, keepdims=True)
    weights = jnp.exp(scores - row_top)
    row_total = jnp.sum(weights, axis=2, keepdims=True)
    probs_low = (weights / row_total).astype(jnp.bfloat16)
    context = jnp.einsum("hqk,khd->qhd", probs_low, value_heads, preferred_element_type=jnp.float32)
    context = context.reshape(group_rows, head_width).astype(jnp.bfloat16)
    attended = scatter_rows(matmul_nt(context, proj_full_t)) + b_proj
    first_in = tokens.astype(jnp.float32) + attended
    first_norm = layer_norm(first_in, gain_attn, shift_attn)
    first_low = first_norm.astype(jnp.bfloat16)
    norm_rows = gather_rows(first_low)
    hidden = matmul(norm_rows, inner_full) + b_inner
    active_low = jax.nn.gelu(hidden, approximate=False).astype(jnp.bfloat16)
    branch = scatter_rows(matmul_nt(active_low, outer_full_t)) + b_outer
    second_in = first_norm + branch
    second, second_pull = jax.vjp(layer_norm, second_in, gain_ffn, shift_ffn)
    layer_out = from_slots((second * valid_piece).astype(jnp.bfloat16))
    out_cot = out_grad.astype(jnp.float32) * valid_piece
    second_grad, dgain_ffn, dshift_ffn = second_pull(out_cot)
    branch_grad = second_grad.astype(jnp.bfloat16)
    db_outer = jnp.sum(branch_grad.astype(jnp.float32), axis=0)
    branch_rows = gather_rows(branch_grad)
    active_grad = matmul(branch_rows, outer_full_t)
    gelu_pull = jax.vjp(partial(jax.nn.gelu, approximate=False), hidden)[1]
    hidden_grad = gelu_pull(active_grad)[0].astype(jnp.bfloat16)
    norm_back = scatter_rows(matmul_nt(hidden_grad, inner_full))
    dw_outer_t = scatter_shards(matmul_tn(branch_rows, active_low))
    dw_inner = scatter_shards(matmul_tn(norm_rows, hidden_grad))
    db_inner = jnp.sum(hidden_grad.astype(jnp.float32), axis=0)
    first_pull = jax.vjp(layer_norm, first_in, gain_attn, shift_attn)[1]
    mix_grad, dgain_attn, dshift_attn = first_pull(second_grad + norm_back)
    proj_grad = mix_grad.astype(jnp.bfloat16)
    db_proj = jnp.sum(proj_grad.astype(jnp.float32), axis=0)
    proj_rows = gather_rows(proj_grad)
    whole_sums = sum_rows_ranks(
        from_slots(jnp.stack([db_proj, dgain_attn, dshift_attn, db_outer, dgain_ffn, dshift_ffn]))
    )
    context_grad = matmul(proj_rows, proj_full_t).astype(jnp.bfloat16)
    dw_proj_t = scatter_shards(matmul_tn(proj_rows, context))
    context_heads = context_grad.reshape(group_rows, local_heads, HEAD_DIM)
    scores = masked_scores(query_heads, key_heads, allowed)
    probs_exact = jnp.exp(scores - row_top) / row_total
    probs_again = probs_exact.astype(jnp.bfloat16)
    prob_grad = jnp.einsum(
        "qhd,khd->hqk", context_heads, value_heads, preferred_element_type=jnp.float32
    )
    row_delta = jnp.sum(prob_grad * probs_exact, axis=2, keepdims=True)
    score_grad = (probs_exact * (prob_grad - row_delta)).astype(jnp.bfloat16)
    query_grad = jnp.einsum(
        "hqk,khd->qhd", score_grad, key_heads, preferred_element_type=jnp.float32
    )
    query_grad = (query_grad.astype(jnp.bfloat16) * head_scale).reshape(group_rows, head_width)
    key_grad = jnp.einsum(
        "hqk,qhd->khd", score_grad, query_heads, preferred_element_type=jnp.float32
    )
    key_grad = key_grad.astype(jnp.bfloat16).reshape(group_rows, head_width)
    value_grad = jnp.einsum(
        "hqk,qhd->khd", probs_again, context_heads, preferred_element_type=jnp.float32
    )
    value_grad = value_grad.astype(jnp.bfloat16).reshape(group_rows, head_width)
    qkv_grad = jnp.concatenate([query_grad, key_grad, value_grad], axis=1)
    dw_qkv = scatter_shards(matmul_tn(token_rows, qkv_grad))
    tokens_grad = from_slots(mix_grad + scatter_rows(matmul_nt(qkv_grad, qkv_full)))
    db_query = jnp.sum(query_grad.astype(jnp.float32), axis=0)
    db_value = jnp.sum(value_grad.astype(jnp.float32), axis=0)
    sums = sum_dp_ranks(jnp.concatenate([whole_sums.reshape(-1), db_inner, db_query, db_value]))
    whole_width = whole_sums.size
    shared = sums[:whole_width].reshape(whole_sums.shape)
    db_inner = sums[whole_width : whole_width + inner_width]
    db_query = sums[whole_width + inner_width : whole_width + inner_width + head_width]
    db_value = sums[whole_width + inner_width + head_width :]
    return (
        layer_out,
        tokens_grad,
        dw_qkv[:, :head_width],
        db_query,
        dw_qkv[:, head_width : 2 * head_width],
        dw_qkv[:, 2 * head_width :],
        db_value,
        dw_proj_t.T,
        shared[0],
        shared[1],
        shared[2],
        dw_inner,
        db_inner,
        dw_outer_t.T,
        shared[3],
        shared[4],
        shared[5],
    )


def solution(mesh):
    in_specs = (
        P(("dp", "tensor"), None),
        P("dp"),
        P("dp", None),
        P("dp", "tensor"),
        P("tensor"),
        P("dp", "tensor"),
        P("dp", "tensor"),
        P("tensor"),
        P("tensor", "dp"),
        P(),
        P(),
        P(),
        P("dp", "tensor"),
        P("tensor"),
        P("tensor", "dp"),
        P(),
        P(),
        P(),
        P(("dp", "tensor"), None),
    )
    out_specs = (
        P(("dp", "tensor"), None),
        P(("dp", "tensor"), None),
        P("dp", "tensor"),
        P("tensor"),
        P("dp", "tensor"),
        P("dp", "tensor"),
        P("tensor"),
        P("tensor", "dp"),
        P(),
        P(),
        P(),
        P("dp", "tensor"),
        P("tensor"),
        P("tensor", "dp"),
        P(),
        P(),
        P(),
    )
    return jax.shard_map(
        on_device, mesh=mesh, in_specs=in_specs, out_specs=out_specs, check_vma=False
    )
```

```python
from functools import partial

import jax
import jax.numpy as jnp
from jax import lax
from jax.experimental import pallas as pl
from jax.experimental.pallas import tpu as pltpu
from jax.sharding import PartitionSpec as P

HEAD_DIM = 64


epsilon = 1e-12
masked_fill = -1e30

row_slots = (0, 2, 1, 3)
slot_offsets = (0, 4, 6, 5, 7, 3, 2, 1)


def matmul(left_side, right_side):
    return jnp.dot(left_side, right_side, preferred_element_type=jnp.float32)


def matmul_nt(left_side, right_side):
    return lax.dot_general(
        left_side, right_side, (((1,), (1,)), ((), ())), preferred_element_type=jnp.float32
    )


def matmul_tn(left_side, right_side):
    return lax.dot_general(
        left_side, right_side, (((0,), (0,)), ((), ())), preferred_element_type=jnp.float32
    )


def low(value):
    return value.astype(jnp.bfloat16)


def wide(value):
    return value.astype(jnp.float32)


def shaped(shape, dtype=jnp.bfloat16):
    return jax.ShapeDtypeStruct(shape, dtype)


def paired():
    return lax.axis_size("dp") == len(slot_offsets)


def swap(block, axis_name, offset):
    count = lax.axis_size(axis_name)
    return lax.ppermute(block, axis_name, [(i, i ^ offset) for i in range(count)])


def part(array, start, rows):
    return array, start, rows


def kernel_call(body, out_shape, whole=(), pieces=(), scalars=(), marks=(), scratch=()):
    pieces = [
        [p if isinstance(p, tuple) else (p, 0, p.shape[0]) for p in some] for some in pieces
    ]
    buffers = [
        pltpu.VMEM((sum(p[2] for p in some), *some[0][0].shape[1:]), some[0][0].dtype)
        for some in pieces
    ]
    flat = [p for some in pieces for p in some]
    flat_out, tree = jax.tree.flatten(list(out_shape))
    counts = (len(scalars), len(whole), len(flat), len(marks), len(flat_out), len(buffers))

    def run(*refs):
        groups, start = [], 0
        for count in counts:
            groups.append(refs[start : start + count])
            start += count
        scalar_refs, whole_refs, piece_refs, _, out_refs, buffer_refs = groups
        rest = refs[start:]
        copies = []
        if flat:
            done, rest = rest[0], rest[1:]
            k = 0
            for some, buffer in zip(pieces, buffer_refs):
                row, mine = 0, []
                for _, first, rows in some:
                    mine.append(
                        pltpu.make_async_copy(
                            piece_refs[k].at[pl.ds(first, rows)],
                            buffer.at[pl.ds(row, rows)],
                            done.at[k],
                        )
                    )
                    row += rows
                    k += 1
                copies.append(mine)
            for copy in (c for mine in copies for c in mine):
                copy.start()

        def need(number):
            for copy in copies[number]:
                copy.wait()

        outs = jax.tree.unflatten(tree, out_refs)
        body(need, *scalar_refs, *whole_refs, *buffer_refs, *outs, *rest)

    anywhere = pl.BlockSpec(memory_space=pl.ANY)
    inside = pl.BlockSpec(memory_space=pltpu.VMEM)
    semaphores = [pltpu.SemaphoreType.DMA((len(flat),))] if flat else []
    results = pl.pallas_call(
        run,
        out_shape=flat_out,
        in_specs=[pl.BlockSpec(memory_space=pltpu.SMEM)] * len(scalars)
        + [inside] * len(whole)
        + [anywhere] * (len(flat) + len(marks)),
        out_specs=[inside] * len(flat_out),
        scratch_shapes=buffers + semaphores + list(scratch),
        compiler_params=pltpu.CompilerParams(vmem_limit_bytes=VMEM_LIMIT),
        cost_estimate=pl.CostEstimate(
            flops=int(QUICK * 1.1e9), bytes_accessed=int(QUICK * 3.5e6), transcendentals=0
        ),
    )(*scalars, *whole, *[p[0] for p in flat], *marks)
    return jax.tree.unflatten(tree, results)


VMEM_LIMIT = 63 << 20
QUICK = 0.01
PARTS = 1


def part_shapes(rows, columns):
    return [shaped((rows // PARTS, columns))] * PARTS


def write_parts(refs, value, columns=slice(None)):
    rows = refs[0].shape[0]
    for k, ref in enumerate(refs):
        ref[:, columns] = low(value[k * rows : (k + 1) * rows])


def region(flag, body, *operands):
    def nothing(*some):
        return jax.tree.map(lambda x: jnp.zeros(x.shape, x.dtype), jax.eval_shape(body, *operands))

    return lax.cond(flag, body, nothing, *operands)


def swap_parts(parts, offset):
    return [swap(p, "tensor", offset) for p in parts]


def gather_rows(parts):
    across = swap_parts(parts, 2)
    beside = swap_parts(parts, 1)
    corner = swap_parts(across, 1)
    return [*parts, *across, *beside, *corner]


def turn_kernel(need, near_ref, arrived_ref, out_refs):
    need(0)
    need(1)
    write_parts(out_refs, near_ref[...] + wide(arrived_ref[...]))


def scatter_rows(near, far, marks=()):
    rows, columns = near.shape
    half = rows // 2
    arrived = swap_parts(far, 1)
    turned = kernel_call(
        turn_kernel,
        [part_shapes(half, columns)],
        pieces=[[part(near, half, half)], arrived[PARTS:]],
        marks=marks,
    )[0]
    return [[part(near, 0, half)], arrived[:PARTS], swap_parts(turned, 2)]


def own_sum(need, near_ref, arrived_ref, across_ref):
    for number in range(3):
        need(number)
    return near_ref[...] + wide(arrived_ref[...]) + wide(across_ref[...])


def gather_first(shard):
    if not paired():
        return [lax.all_gather(shard, "dp", axis=0, tiled=True)]
    beside = swap(shard, "dp", 1)
    farther, far = swap(shard, "dp", 6), swap(shard, "dp", 4)
    above = swap(shard, "dp", 2)
    return [shard, far, farther, swap(beside, "dp", 2), above, beside]


def gather_rest(pieces):
    if not paired():
        return pieces
    shard, far, farther, corner, above, beside = pieces
    return [shard, far, farther, swap(far, "dp", 1), swap(farther, "dp", 1), corner, above, beside]


def far_pieces(pieces):
    return pieces[1:3] if paired() else pieces


def weight_cuts(width, columns):
    if not paired():
        return [shaped((width, columns), jnp.float32)]
    block = width // len(slot_offsets)
    return [shaped((block, columns), jnp.float32)] + [
        shaped((block * n, columns)) for n in (2, 2, 2, 1)
    ]


def weight_grad_into(pairs, out_refs):
    column = 0
    for left_ref, right_ref in pairs:
        right = right_ref[...]
        columns = slice(column, column + right.shape[1])
        column += right.shape[1]
        start = 0
        for out_ref in out_refs:
            for place in range(0, out_ref.shape[0], 128):
                block = left_ref[:, start : start + 128]
                out_ref[place : place + 128, columns] = matmul_tn(block, right).astype(
                    out_ref.dtype
                )
                start += 128


def scatter_first(cuts):
    if not paired():
        return cuts
    kept, far, far_beside, above, beside = cuts
    return kept, far, beside, swap(far_beside, "dp", 1), swap(above, "dp", 2)


def combine_kernel(
    need, far_ref, far_in_ref, beside_ref, above_ref, far_out, farther_out, beside_out
):
    block = far_out.shape[0]
    need(0)
    need(1)
    farther_out[...] = low(wide(far_ref[block:]) + wide(far_in_ref[block:]))
    far_out[...] = low(wide(far_ref[:block]) + wide(far_in_ref[:block]))
    need(2)
    need(3)
    beside_out[...] = low(wide(beside_ref[...]) + wide(above_ref[...]))


def scatter_second(state, marks=()):
    if not paired():
        return state, marks
    kept, far, beside, far_in, above = state
    block = kept.shape[0]
    far_out, farther_out, beside_out = kernel_call(
        combine_kernel,
        [shaped(kept.shape)] * 3,
        pieces=[[far], [far_in], [beside], [part(above, 0, block)]],
        marks=marks,
    )
    state = [
        kept,
        part(above, block, block),
        swap(farther_out, "dp", 6),
        swap(far_out, "dp", 4),
        swap(beside_out, "dp", 1),
    ]
    return state, [beside_out]


def last_kernel(write, count, need, *refs):
    total = None
    for number, ref in enumerate(refs[:count]):
        need(number)
        total = wide(ref[...]) if total is None else total + wide(ref[...])
    write(total, *refs[count:])


def scatter_last(state, write, out_shape, marks=()):
    if not paired():
        state = [lax.psum_scatter(state[0], "dp", scatter_dimension=0, tiled=True)]
    return kernel_call(
        partial(last_kernel, write, len(state)),
        out_shape,
        pieces=[[term] for term in state],
        marks=marks,
    )


def sum_dp_ranks(value):
    if paired():
        value = value + swap(value, "dp", 1)
        farther, far = swap(value, "dp", 6), swap(value, "dp", 4)
        return (value + swap(value, "dp", 2)) + (far + farther)
    offset = 1
    while offset < lax.axis_size("dp"):
        value = value + swap(value, "dp", offset)
        offset *= 2
    return value


def to_slots(array_ref, rank, in_slots):
    if not in_slots:
        return array_ref[...]
    width = array_ref.shape[-1] // len(slot_offsets)
    return jnp.concatenate(
        [
            array_ref[:, pl.ds(pl.multiple_of((rank ^ o) * width, width), width)]
            for o in slot_offsets
        ],
        axis=1,
    )


def from_slots(value, rank, in_slots, out_ref):
    if not in_slots:
        out_ref[...] = value.astype(out_ref.dtype)
        return
    width = out_ref.shape[-1] // len(slot_offsets)
    for place, o in enumerate(slot_offsets):
        out_ref[:, pl.ds(pl.multiple_of((rank ^ o) * width, width), width)] = value[
            :, place * width : (place + 1) * width
        ].astype(out_ref.dtype)


def segments(lengths_ref, places):
    total = jnp.int32(0)
    found = jnp.zeros(places.shape, jnp.int32)
    for k in range(lengths_ref.shape[1]):
        total = total + lengths_ref[0, k]
        found = found + jnp.where(places >= total, 1, 0)
    return found


def prepare_kernel(need, query_ref, key_ref, value_ref, proj_ref, out_ref):
    width = query_ref.shape[1]
    for place, ref in enumerate((query_ref, key_ref, value_ref)):
        out_ref[:, place * width : (place + 1) * width] = ref[...]
    out_ref[:, 3 * width :] = proj_ref[...].T


def place_kernel(in_slots, need, ranks_ref, tokens_ref, grad_ref, small_ref, *out_refs):
    write_parts(out_refs[0], to_slots(tokens_ref, ranks_ref[0], in_slots))
    for ref, out_ref in zip((grad_ref, small_ref), out_refs[1:]):
        out_ref[...] = to_slots(ref, ranks_ref[0], in_slots)


def pass_kernel(need, in_ref, out_ref):
    need(0)
    out_ref[...] = in_ref[...]


def turn_over_kernel(need, in_ref, out_ref):
    need(0)
    out_ref[...] = in_ref[...].T


def back_into(left_ref, right_ref, inner, near_ref, far_ref):
    half = near_ref.shape[0]
    for start in range(0, near_ref.shape[1], 256):
        columns = slice(start, start + 256)
        total = matmul_nt(left_ref[...], right_ref[columns, inner])
        near_ref[:, columns] = total[:half]
        write_parts(far_ref, total[half:], columns)


def attention_kernel(
    scale,
    need,
    ranks_ref,
    lengths_ref,
    key_ref,
    bias_ref,
    tokens_ref,
    weights_ref,
    qkv_ref,
    probs_ref,
    context_ref,
    fill_ref,
):
    rows = tokens_ref.shape[0]
    piece = rows // len(row_slots)
    head_width = context_ref.shape[1]
    rank = ranks_ref[1]
    down = lax.broadcasted_iota(jnp.int32, (rows, 1), 0)
    along = lax.broadcasted_iota(jnp.int32, (1, rows), 1)

    def places(index):
        slot, step = index // piece, index % piece
        owner = jnp.where(slot == 0, row_slots[0], 0)
        for k in range(1, len(row_slots)):
            owner = jnp.where(slot == k, row_slots[k], owner)
        return (owner ^ rank) * piece + step

    segment_down = segments(lengths_ref, places(down))
    segment_along = segments(lengths_ref, places(along))
    keys = jnp.concatenate([key_ref[pl.ds(rank ^ o, 1), :] for o in row_slots], axis=1)
    allowed = (segment_down == segment_along) & ((keys == 1) | (down == along))
    fill_ref[...] = jnp.where(allowed, 0.0, masked_fill)

    need(0)
    need(1)
    qkv = matmul(tokens_ref[...], weights_ref[:, : 3 * head_width]) + bias_ref[...]
    qkv_ref[:, :head_width] = low(qkv[:, :head_width] * scale)
    qkv_ref[:, head_width:] = low(qkv[:, head_width:])
    for head in range(head_width // HEAD_DIM):
        columns = [
            slice(part * head_width + head * HEAD_DIM, part * head_width + (head + 1) * HEAD_DIM)
            for part in range(3)
        ]
        query, key, value = (qkv_ref[:, c] for c in columns)
        scores = matmul_nt(query, key) + fill_ref[...]
        weights = jnp.exp(scores - jnp.max(scores, axis=1, keepdims=True))
        probs = low(weights * (1.0 / jnp.sum(weights, axis=1, keepdims=True)))
        probs_ref[head] = probs
        context_ref[:, columns[0]] = low(matmul(probs, value))


def project_kernel(need, context_ref, weights_ref, shard_ref, near_ref, far_ref, out_ref):
    need(2)
    out_ref[...] = shard_ref[...]
    need(0)
    need(1)
    width = context_ref.shape[1]
    back_into(context_ref, weights_ref, slice(3 * width, None), near_ref, far_ref)


def first_norm_kernel(
    need,
    small_ref,
    near_ref,
    arrived_ref,
    across_ref,
    tokens_ref,
    first_ref,
    unit_ref,
    scale_ref,
    low_ref,
):
    need(3)
    total = (
        wide(tokens_ref[...])
        + own_sum(need, near_ref, arrived_ref, across_ref)
        + small_ref[0:1]
    )
    centred = total - jnp.mean(total, axis=1, keepdims=True)
    scale = lax.rsqrt(jnp.mean(centred * centred, axis=1, keepdims=True) + epsilon)
    unit = centred * scale
    first = unit * small_ref[1:2] + small_ref[2:3]
    unit_ref[...] = unit
    scale_ref[...] = scale
    first_ref[...] = first
    write_parts(low_ref, first)


def inner_kernel(need, bias_ref, rows_ref, weights_ref, active_ref, slope_ref):
    need(0)
    need(1)
    for start in range(0, active_ref.shape[1], 256):
        columns = slice(start, start + 256)
        hidden = matmul(rows_ref[...], weights_ref[:, columns]) + bias_ref[:, columns]
        share = 0.5 + 0.5 * lax.erf(hidden * (0.5**0.5))
        active_ref[:, columns] = low(hidden * share)
        slope_ref[:, columns] = share + hidden * jnp.exp(-0.5 * hidden * hidden) * (
            0.3989422804014327
        )


def outer_kernel(need, active_ref, weights_ref, near_ref, far_ref):
    need(0)
    need(1)
    back_into(active_ref, weights_ref, slice(None), near_ref, far_ref)


def second_norm_kernel(
    in_slots,
    need,
    ranks_ref,
    lengths_ref,
    small_ref,
    near_ref,
    arrived_ref,
    across_ref,
    first_ref,
    grad_ref,
    out_ref,
    second_grad_ref,
    low_ref,
    sums_ref,
):
    rows, _ = first_ref.shape
    need(3)
    need(4)
    total = first_ref[...] + own_sum(need, near_ref, arrived_ref, across_ref) + small_ref[3:4]
    centred = total - jnp.mean(total, axis=1, keepdims=True)
    scale = lax.rsqrt(jnp.mean(centred * centred, axis=1, keepdims=True) + epsilon)
    unit = centred * scale
    place = ranks_ref[1] * rows + lax.broadcasted_iota(jnp.int32, (rows, 1), 0)
    valid = jnp.where(segments(lengths_ref, place) < lengths_ref.shape[1], 1.0, 0.0)
    gain = small_ref[4:5]
    second = (unit * gain + small_ref[5:6]) * valid
    from_slots(second, ranks_ref[0], in_slots, out_ref)
    cot = wide(grad_ref[...]) * valid
    pulled = cot * gain
    second_grad = scale * (
        pulled
        - jnp.mean(pulled, axis=1, keepdims=True)
        - unit * jnp.mean(pulled * unit, axis=1, keepdims=True)
    )
    second_grad_ref[...] = second_grad
    rounded = low(second_grad)
    write_parts(low_ref, rounded)
    sums_ref[0:1] = jnp.sum(wide(rounded), axis=0, keepdims=True)
    sums_ref[1:2] = jnp.sum(cot * unit, axis=0, keepdims=True)
    sums_ref[2:3] = jnp.sum(cot, axis=0, keepdims=True)
    sums_ref[3:8] = jnp.zeros_like(sums_ref[3:8])


def hidden_grad_kernel(
    need, rows_ref, outer_ref, slope_ref, inner_ref, hidden_grad_ref, near_ref, far_ref, sums_ref
):
    for number in range(3):
        need(number)
    for start in range(0, hidden_grad_ref.shape[1], 256):
        columns = slice(start, start + 256)
        grad = low(matmul(rows_ref[...], outer_ref[:, columns]) * slope_ref[:, columns])
        hidden_grad_ref[:, columns] = grad
        sums_ref[0:1, columns] = jnp.sum(wide(grad), axis=0, keepdims=True)
    need(3)
    back_into(hidden_grad_ref, inner_ref, slice(None), near_ref, far_ref)


def single_grad_kernel(need, left_ref, right_ref, *out_refs):
    need(0)
    need(1)
    weight_grad_into([(left_ref, right_ref)], out_refs)


def first_back_kernel(
    in_slots,
    need,
    ranks_ref,
    scale_ref,
    small_ref,
    second_sums_ref,
    near_ref,
    arrived_ref,
    across_ref,
    second_grad_ref,
    unit_ref,
    mix_ref,
    low_ref,
    sums_ref,
):
    need(3)
    need(4)
    cot = second_grad_ref[...] + own_sum(need, near_ref, arrived_ref, across_ref)
    unit = unit_ref[...]
    pulled = cot * small_ref[1:2]
    mix = scale_ref[...] * (
        pulled
        - jnp.mean(pulled, axis=1, keepdims=True)
        - unit * jnp.mean(pulled * unit, axis=1, keepdims=True)
    )
    mix_ref[...] = mix
    rounded = low(mix)
    write_parts(low_ref, rounded)
    sums = jnp.concatenate(
        [
            jnp.sum(wide(rounded), axis=0, keepdims=True),
            jnp.sum(cot * unit, axis=0, keepdims=True),
            jnp.sum(cot, axis=0, keepdims=True),
            second_sums_ref[0:3],
            jnp.zeros((2, mix.shape[1]), jnp.float32),
        ],
        axis=0,
    )
    from_slots(sums, ranks_ref[0], in_slots, sums_ref)


def attention_back_kernel(
    scale,
    need,
    rows_ref,
    weights_ref,
    qkv_ref,
    probs_ref,
    grads_ref,
    near_ref,
    far_ref,
    sums_ref,
    context_grad_ref,
):
    head_width = context_grad_ref.shape[1]
    need(0)
    need(1)
    context_grad_ref[...] = low(matmul(rows_ref[...], weights_ref[:, 3 * head_width :]))
    need(2)
    need(3)
    for head in range(head_width // HEAD_DIM):
        columns = [
            slice(part * head_width + head * HEAD_DIM, part * head_width + (head + 1) * HEAD_DIM)
            for part in range(3)
        ]
        query, key, value = (qkv_ref[:, c] for c in columns)
        probs = probs_ref[head]
        context_grad = context_grad_ref[:, columns[0]]
        prob_grad = matmul_nt(context_grad, value)
        exact = wide(probs)
        product = prob_grad * exact
        score_grad = low(product - exact * jnp.sum(product, axis=1, keepdims=True))
        query_grad = low(matmul(score_grad, key)) * jnp.asarray(scale, jnp.bfloat16)
        key_grad = low(matmul_tn(score_grad, query))
        value_grad = low(matmul_tn(probs, context_grad))
        for place, grad in zip(columns, (query_grad, key_grad, value_grad)):
            grads_ref[:, place] = grad
    sums_ref[...] = jnp.zeros_like(sums_ref)
    sums_ref[0:1, : 3 * head_width] = jnp.sum(wide(grads_ref[...]), axis=0, keepdims=True)
    back_into(grads_ref, weights_ref, slice(0, 3 * head_width), near_ref, far_ref)


def attention_grad_kernel(need, tokens_ref, qkv_grad_ref, rows_ref, context_ref, *out_refs):
    for number in range(4):
        need(number)
    weight_grad_into([(tokens_ref, qkv_grad_ref), (rows_ref, context_ref)], out_refs)


def tokens_grad_kernel(
    in_slots, need, ranks_ref, near_ref, arrived_ref, across_ref, mix_ref, out_ref
):
    need(3)
    total = mix_ref[...] + own_sum(need, near_ref, arrived_ref, across_ref)
    from_slots(total, ranks_ref[0], in_slots, out_ref)


def write_turned(total, out_ref):
    out_ref[...] = total.T


def write_plain(total, out_ref):
    out_ref[...] = total


def write_attention(total, query_ref, key_ref, value_ref, proj_ref):
    width = query_ref.shape[1]
    for place, ref in enumerate((query_ref, key_ref, value_ref)):
        ref[...] = total[:, place * width : (place + 1) * width]
    proj_ref[...] = total[:, 3 * width :].T


def on_device(
    tokens,
    key_mask,
    seq_lengths,
    w_query,
    b_query,
    w_key,
    w_value,
    b_value,
    w_proj,
    b_proj,
    gain_attn,
    shift_attn,
    w_inner,
    b_inner,
    w_outer,
    b_outer,
    gain_ffn,
    shift_ffn,
    out_grad,
):
    in_slots = paired()
    flag = seq_lengths[0, 0] >= 0
    ranks = jnp.stack([lax.axis_index("dp"), lax.axis_index("tensor")]).astype(jnp.int32)
    piece_rows, model_width = tokens.shape
    group_rows = piece_rows * lax.axis_size("tensor")
    half_rows = group_rows // 2
    shard_rows = w_query.shape[0]
    head_width = b_query.shape[0]
    heads = head_width // HEAD_DIM
    inner_width = b_inner.shape[0]
    scale = HEAD_DIM ** (-0.5)
    own = (piece_rows, model_width)
    own_parts = part_shapes(*own)
    partial_sums = [shaped((half_rows, model_width), jnp.float32), own_parts + own_parts]

    attn_shard = kernel_call(
        prepare_kernel,
        [shaped((shard_rows, 4 * head_width))],
        whole=[w_query, w_key, w_value, w_proj],
    )[0]
    attn_pieces = gather_first(attn_shard)
    small = jnp.stack(
        [b_proj, gain_attn, shift_attn, b_outer, gain_ffn, shift_ffn, b_proj, b_proj]
    )
    tokens, out_grad, small = kernel_call(
        partial(place_kernel, in_slots),
        [own_parts, shaped(own), shaped(small.shape, jnp.float32)],
        whole=[tokens, out_grad, small],
        scalars=[ranks],
    )
    token_rows = gather_rows(tokens)
    outer_shard = kernel_call(
        turn_over_kernel, [shaped(w_outer.shape[::-1])], pieces=[[w_outer]], marks=tokens[:1]
    )[0]
    inner_shard = kernel_call(
        pass_kernel, [shaped(w_inner.shape)], pieces=[[w_inner]], marks=far_pieces(attn_pieces)
    )[0]
    inner_pieces = gather_first(inner_shard)
    attn_weights = gather_rest(attn_pieces)
    qkv_bias = jnp.concatenate([b_query, jnp.zeros_like(b_query), b_value])[None, :]
    qkv, probs, context = kernel_call(
        partial(attention_kernel, scale),
        [
            shaped((group_rows, 3 * head_width)),
            shaped((heads, group_rows, group_rows)),
            shaped((group_rows, head_width)),
        ],
        scalars=[ranks, seq_lengths],
        whole=[key_mask.reshape(lax.axis_size("tensor"), piece_rows), qkv_bias],
        pieces=[token_rows, attn_weights],
        marks=[inner_shard],
        scratch=[pltpu.VMEM((group_rows, group_rows), jnp.float32)],
    )
    near, far, outer_shard = kernel_call(
        project_kernel,
        [*partial_sums, shaped(outer_shard.shape)],
        pieces=[[context], attn_weights, [outer_shard]],
        marks=far_pieces(inner_pieces),
    )
    outer_pieces = gather_first(outer_shard)
    inner_weights = gather_rest(inner_pieces)
    def first_part(near, far, tokens, small):
        terms = scatter_rows(near, far)
        return kernel_call(
            first_norm_kernel,
            [
                shaped(own, jnp.float32),
                shaped(own, jnp.float32),
                shaped((piece_rows, 1), jnp.float32),
                own_parts,
            ],
            whole=[small],
            pieces=[*terms, tokens],
        )

    first, unit, unit_scale, first_low = region(flag, first_part, near, far, tokens, small)
    outer_weights = gather_rest(outer_pieces)
    norm_rows = gather_rows(first_low)
    active, slope = kernel_call(
        inner_kernel,
        [shaped((group_rows, inner_width)), shaped((group_rows, inner_width), jnp.float32)],
        whole=[b_inner[None, :]],
        pieces=[norm_rows, inner_weights],
    )
    near, far = kernel_call(
        outer_kernel, partial_sums, pieces=[[active], outer_weights]
    )
    terms = scatter_rows(near, far)
    layer_out, second_grad, branch_grad, second_sums = kernel_call(
        partial(second_norm_kernel, in_slots),
        [
            shaped(own),
            shaped(own, jnp.float32),
            own_parts,
            shaped((8, model_width), jnp.float32),
        ],
        scalars=[ranks, seq_lengths],
        whole=[small],
        pieces=[*terms, [first], [out_grad]],
    )

    branch_rows = gather_rows(branch_grad)
    outer_cuts = kernel_call(
        single_grad_kernel,
        weight_cuts(model_width, inner_width),
        pieces=[branch_rows, [active]],
    )
    outer_state = scatter_first(outer_cuts)
    hidden_grad, near, far, inner_sums = kernel_call(
        hidden_grad_kernel,
        [
            shaped((group_rows, inner_width)),
            *partial_sums,
            shaped((1, inner_width), jnp.float32),
        ],
        pieces=[branch_rows, outer_weights, [slope], inner_weights],
        marks=[outer_cuts[0]],
    )
    terms = scatter_rows(near, far)
    inner_state = scatter_first(
        kernel_call(
            single_grad_kernel,
            weight_cuts(model_width, inner_width),
            pieces=[norm_rows, [hidden_grad]],
            marks=[outer_state[0], terms[1][0]],
        )
    )
    mix_grad, proj_grad, sums = kernel_call(
        partial(first_back_kernel, in_slots),
        [shaped(own, jnp.float32), own_parts, shaped((8, model_width), jnp.float32)],
        scalars=[ranks],
        whole=[unit_scale, small, second_sums],
        pieces=[*terms, [second_grad], [unit]],
    )
    proj_rows = gather_rows(proj_grad)
    outer_state, outer_mark = scatter_second(outer_state, proj_grad[:1])
    sums = sums + swap(sums, "tensor", 1)
    sums = sums + swap(sums, "tensor", 2)
    qkv_grad, near, far, attn_sums = kernel_call(
        partial(attention_back_kernel, scale),
        [
            shaped((group_rows, 3 * head_width)),
            *partial_sums,
            shaped((1, model_width), jnp.float32),
        ],
        pieces=[proj_rows, attn_weights, [qkv], [probs]],
        marks=[*outer_mark, sums],
        scratch=[pltpu.VMEM((group_rows, head_width), jnp.bfloat16)],
    )
    attn_state = scatter_first(
        kernel_call(
            attention_grad_kernel,
            weight_cuts(model_width, 4 * head_width),
            pieces=[token_rows, [qkv_grad], proj_rows, [context]],
        )
    )
    inner_state, inner_mark = scatter_second(inner_state, [attn_state[0], *outer_state[2:]])
    terms = scatter_rows(near, far, inner_mark)
    dw_outer = scatter_last(
        outer_state, write_turned, [shaped(w_outer.shape, jnp.float32)], inner_mark
    )[0]
    attn_state, attn_mark = scatter_second(attn_state, inner_mark)
    tokens_grad = kernel_call(
        partial(tokens_grad_kernel, in_slots),
        [shaped(own, jnp.float32)],
        scalars=[ranks],
        pieces=[*terms, [mix_grad]],
        marks=attn_mark,
    )[0]
    dw_inner = scatter_last(
        inner_state, write_plain, [shaped(w_inner.shape, jnp.float32)], [tokens_grad]
    )[0]
    dw_query, dw_key, dw_value, dw_proj = scatter_last(
        attn_state,
        write_attention,
        [shaped(w.shape, jnp.float32) for w in (w_query, w_key, w_value, w_proj)],
    )

    sums = sum_dp_ranks(jnp.concatenate([sums[:6], inner_sums, attn_sums], axis=0))
    return (
        layer_out,
        tokens_grad,
        dw_query,
        sums[7, :head_width],
        dw_key,
        dw_value,
        sums[7, 2 * head_width : 3 * head_width],
        dw_proj,
        sums[0],
        sums[1],
        sums[2],
        dw_inner,
        sums[6],
        dw_outer,
        sums[3],
        sums[4],
        sums[5],
    )


def solution(mesh):
    in_specs = (
        P(("dp", "tensor"), None),
        P("dp"),
        P("dp", None),
        P("dp", "tensor"),
        P("tensor"),
        P("dp", "tensor"),
        P("dp", "tensor"),
        P("tensor"),
        P("tensor", "dp"),
        P(),
        P(),
        P(),
        P("dp", "tensor"),
        P("tensor"),
        P("tensor", "dp"),
        P(),
        P(),
        P(),
        P(("dp", "tensor"), None),
    )
    out_specs = (
        P(("dp", "tensor"), None),
        P(("dp", "tensor"), None),
        P("dp", "tensor"),
        P("tensor"),
        P("dp", "tensor"),
        P("dp", "tensor"),
        P("tensor"),
        P("tensor", "dp"),
        P(),
        P(),
        P(),
        P("dp", "tensor"),
        P("tensor"),
        P("tensor", "dp"),
        P(),
        P(),
        P(),
    )
    return jax.shard_map(
        on_device, mesh=mesh, in_specs=in_specs, out_specs=out_specs, check_vma=False
    )
```

```python
from functools import partial

import jax
import jax.numpy as jnp
from jax import lax
from jax.experimental import pallas as pl
from jax.experimental.pallas import tpu as pltpu
from jax.sharding import PartitionSpec as P

HEAD_DIM = 64


epsilon = 1e-12
masked_fill = -1e30

row_slots = (0, 2, 1, 3)
slot_offsets = (0, 4, 6, 5, 7, 3, 2, 1)


def matmul(left_side, right_side):
    return jnp.dot(left_side, right_side, preferred_element_type=jnp.float32)


def matmul_nt(left_side, right_side):
    return lax.dot_general(
        left_side, right_side, (((1,), (1,)), ((), ())), preferred_element_type=jnp.float32
    )


def matmul_tn(left_side, right_side):
    return lax.dot_general(
        left_side, right_side, (((0,), (0,)), ((), ())), preferred_element_type=jnp.float32
    )


def low(value):
    return value.astype(jnp.bfloat16)


def wide(value):
    return value.astype(jnp.float32)


def shaped(shape, dtype=jnp.bfloat16):
    return jax.ShapeDtypeStruct(shape, dtype)


def paired():
    return lax.axis_size("dp") == len(slot_offsets)


def swap(block, axis_name, offset):
    count = lax.axis_size(axis_name)
    return lax.ppermute(block, axis_name, [(i, i ^ offset) for i in range(count)])


def part(array, start, rows):
    return array, start, rows


def kernel_call(body, out_shape, whole=(), pieces=(), scalars=(), marks=(), scratch=()):
    pieces = [
        [p if isinstance(p, tuple) else (p, 0, p.shape[0]) for p in some] for some in pieces
    ]
    buffers = [
        pltpu.VMEM((sum(p[2] for p in some), *some[0][0].shape[1:]), some[0][0].dtype)
        for some in pieces
    ]
    flat = [p for some in pieces for p in some]
    flat_out, tree = jax.tree.flatten(list(out_shape))
    counts = (len(scalars), len(whole), len(flat), len(marks), len(flat_out), len(buffers))

    def run(*refs):
        groups, start = [], 0
        for count in counts:
            groups.append(refs[start : start + count])
            start += count
        scalar_refs, whole_refs, piece_refs, _, out_refs, buffer_refs = groups
        rest = refs[start:]
        copies = []
        if flat:
            done, rest = rest[0], rest[1:]
            k = 0
            for some, buffer in zip(pieces, buffer_refs):
                row, mine = 0, []
                for _, first, rows in some:
                    mine.append(
                        pltpu.make_async_copy(
                            piece_refs[k].at[pl.ds(first, rows)],
                            buffer.at[pl.ds(row, rows)],
                            done.at[k],
                        )
                    )
                    row += rows
                    k += 1
                copies.append(mine)
            for copy in (c for mine in copies for c in mine):
                copy.start()

        def need(number):
            for copy in copies[number]:
                copy.wait()

        outs = jax.tree.unflatten(tree, out_refs)
        body(need, *scalar_refs, *whole_refs, *buffer_refs, *outs, *rest)

    anywhere = pl.BlockSpec(memory_space=pl.ANY)
    inside = pl.BlockSpec(memory_space=pltpu.VMEM)
    semaphores = [pltpu.SemaphoreType.DMA((len(flat),))] if flat else []
    results = pl.pallas_call(
        run,
        out_shape=flat_out,
        in_specs=[pl.BlockSpec(memory_space=pltpu.SMEM)] * len(scalars)
        + [inside] * len(whole)
        + [anywhere] * (len(flat) + len(marks)),
        out_specs=[inside] * len(flat_out),
        scratch_shapes=buffers + semaphores + list(scratch),
        compiler_params=pltpu.CompilerParams(vmem_limit_bytes=VMEM_LIMIT),
        cost_estimate=pl.CostEstimate(
            flops=int(QUICK * 1.1e9), bytes_accessed=int(QUICK * 3.5e6), transcendentals=0
        ),
    )(*scalars, *whole, *[p[0] for p in flat], *marks)
    return jax.tree.unflatten(tree, results)


VMEM_LIMIT = 63 << 20
QUICK = 0.01


def region(flag, body, *operands):
    def nothing(*some):
        return jax.tree.map(lambda x: jnp.zeros(x.shape, x.dtype), jax.eval_shape(body, *operands))

    return lax.cond(flag, body, nothing, *operands)


def join_kernel(need, own_ref, across_ref, out_ref):
    rows = own_ref.shape[0]
    need(0)
    out_ref[:rows] = own_ref[...]
    need(1)
    out_ref[rows:] = across_ref[...]


def gather_rows(piece, joined=True):
    across = swap(piece, "tensor", 2)
    if not joined:
        return [piece, across, swap(piece, "tensor", 1), swap(across, "tensor", 1)]
    rows, columns = piece.shape
    pair = kernel_call(join_kernel, [shaped((2 * rows, columns))], pieces=[[piece], [across]])[0]
    return [pair, swap(pair, "tensor", 1)]


def scatter_rows(near, far):
    half = near.shape[0] // 2
    arrived = swap(far, "tensor", 1)
    turned = low(near[half:] + wide(arrived[half:]))
    return [[part(near, 0, half)], [part(arrived, 0, half)], [swap(turned, "tensor", 2)]]


def own_sum(need, near_ref, arrived_ref, across_ref):
    for number in range(3):
        need(number)
    return near_ref[...] + wide(arrived_ref[...]) + wide(across_ref[...])


def far_of(shard):
    return [swap(shard, "dp", 4), swap(shard, "dp", 6)] if paired() else []


def above_of(shard):
    return [swap(shard, "dp", 2)] if paired() else []


def rest_of(pieces):
    return [swap(p, "dp", 1) for p in pieces]


def weight_pieces(shard, far, rest, above, beside):
    if not paired():
        return [lax.all_gather(shard, "dp", axis=0, tiled=True)]
    return [shard, *far, *rest, *above, *beside]


def weight_cuts(width, columns):
    if not paired():
        return [shaped((width, columns), jnp.float32)]
    block = width // len(slot_offsets)
    return [shaped((block, columns), jnp.float32)] + [
        shaped((block * n, columns)) for n in (2, 2, 2, 1)
    ]


def weight_grad_into(pairs, out_refs):
    column = 0
    for left_ref, right_ref in pairs:
        right = right_ref[...]
        columns = slice(column, column + right.shape[1])
        column += right.shape[1]
        start = 0
        for out_ref in out_refs:
            for place in range(0, out_ref.shape[0], 128):
                block = left_ref[:, start : start + 128]
                out_ref[place : place + 128, columns] = matmul_tn(block, right).astype(
                    out_ref.dtype
                )
                start += 128


def scatter_first(cuts):
    if not paired():
        return cuts
    kept, far, far_beside, above, beside = cuts
    return kept, far, beside, swap(far_beside, "dp", 1), swap(above, "dp", 2)


def combine_kernel(
    need, far_ref, far_in_ref, beside_ref, above_ref, *rest
):
    *waiting, far_out, farther_out, beside_out = rest
    block = far_out.shape[0]
    need(0)
    need(1)
    farther_out[...] = low(wide(far_ref[block:]) + wide(far_in_ref[block:]))
    far_out[...] = low(wide(far_ref[:block]) + wide(far_in_ref[:block]))
    need(2)
    need(3)
    beside_out[:block] = low(wide(beside_ref[...]) + wide(above_ref[...]))
    for number, ref in enumerate(waiting):
        need(4 + number)
        beside_out[(number + 1) * block : (number + 2) * block] = ref[...]


def scatter_second(state, marks, waiting=()):
    if not paired():
        return state, None, list(marks)
    kept, far, beside, far_in, above = state
    block, columns = kept.shape
    far_out, farther_out, beside_out = kernel_call(
        combine_kernel,
        [shaped(kept.shape)] * 2 + [shaped((block * (1 + len(waiting)), columns))],
        pieces=[[far], [far_in], [beside], [part(above, 0, block)], *[[w] for w in waiting]],
        marks=marks,
    )
    terms = [
        kept,
        part(above, block, block),
        swap(farther_out, "dp", 6),
        swap(far_out, "dp", 4),
    ]
    return terms, beside_out, [beside_out]


def last_kernel(write, count, need, *refs):
    total = None
    for number, ref in enumerate(refs[:count]):
        need(number)
        total = wide(ref[...]) if total is None else total + wide(ref[...])
    write(total, *refs[count:])


def scatter_last(state, write, out_shape, marks=()):
    if not paired():
        state = [lax.psum_scatter(state[0], "dp", scatter_dimension=0, tiled=True)]
    return kernel_call(
        partial(last_kernel, write, len(state)),
        out_shape,
        pieces=[[term] for term in state],
        marks=marks,
    )


def to_slots(array_ref, rank, in_slots):
    if not in_slots:
        return array_ref[...]
    width = array_ref.shape[-1] // len(slot_offsets)
    return jnp.concatenate(
        [
            array_ref[:, pl.ds(pl.multiple_of((rank ^ o) * width, width), width)]
            for o in slot_offsets
        ],
        axis=1,
    )


def from_slots(value, rank, in_slots, out_ref):
    if not in_slots:
        out_ref[...] = value.astype(out_ref.dtype)
        return
    width = out_ref.shape[-1] // len(slot_offsets)
    for place, o in enumerate(slot_offsets):
        out_ref[:, pl.ds(pl.multiple_of((rank ^ o) * width, width), width)] = value[
            :, place * width : (place + 1) * width
        ].astype(out_ref.dtype)


def segments(lengths_ref, places):
    total = jnp.int32(0)
    found = jnp.zeros(places.shape, jnp.int32)
    for k in range(lengths_ref.shape[1]):
        total = total + lengths_ref[0, k]
        found = found + jnp.where(places >= total, 1, 0)
    return found


def prepare_kernel(need, query_ref, key_ref, value_ref, proj_ref, out_ref):
    width = query_ref.shape[1]
    for place, ref in enumerate((query_ref, key_ref, value_ref)):
        out_ref[:, place * width : (place + 1) * width] = ref[...]
    out_ref[:, 3 * width :] = proj_ref[...].T


def shards_kernel(need, attn_ref, inner_ref, outer_ref, out_ref):
    rows = attn_ref.shape[0]
    out_ref[:rows] = attn_ref[...]
    out_ref[rows : 2 * rows] = inner_ref[...]
    out_ref[2 * rows :] = outer_ref[...].T


def place_kernel(in_slots, need, ranks_ref, tokens_ref, grad_ref, small_ref, *out_refs):
    for ref, out_ref in zip((tokens_ref, grad_ref, small_ref), out_refs):
        out_ref[...] = to_slots(ref, ranks_ref[0], in_slots)


def pass_kernel(need, *refs):
    half = len(refs) // 2
    for number, (in_ref, out_ref) in enumerate(zip(refs[:half], refs[half:])):
        need(number)
        out_ref[...] = in_ref[...]


def back_into(left_ref, right_ref, inner, near_ref, far_ref):
    half = near_ref.shape[0]
    for start in range(0, near_ref.shape[1], 256):
        columns = slice(start, start + 256)
        total = matmul_nt(left_ref[...], right_ref[columns, inner])
        near_ref[:, columns] = total[:half]
        far_ref[:, columns] = low(total[half:])


def attention_kernel(
    scale,
    need,
    ranks_ref,
    lengths_ref,
    key_ref,
    bias_ref,
    tokens_ref,
    weights_ref,
    qkv_ref,
    probs_ref,
    context_ref,
    fill_ref,
):
    rows = tokens_ref.shape[0]
    piece = rows // len(row_slots)
    head_width = context_ref.shape[1]
    rank = ranks_ref[1]
    down = lax.broadcasted_iota(jnp.int32, (rows, 1), 0)
    along = lax.broadcasted_iota(jnp.int32, (1, rows), 1)

    def places(index):
        slot, step = index // piece, index % piece
        owner = jnp.where(slot == 0, row_slots[0], 0)
        for k in range(1, len(row_slots)):
            owner = jnp.where(slot == k, row_slots[k], owner)
        return (owner ^ rank) * piece + step

    segment_down = segments(lengths_ref, places(down))
    segment_along = segments(lengths_ref, places(along))
    keys = jnp.concatenate([key_ref[pl.ds(rank ^ o, 1), :] for o in row_slots], axis=1)
    allowed = (segment_down == segment_along) & ((keys == 1) | (down == along))
    fill_ref[...] = jnp.where(allowed, 0.0, masked_fill)

    need(0)
    need(1)
    qkv = matmul(tokens_ref[...], weights_ref[:, : 3 * head_width]) + bias_ref[...]
    qkv_ref[:, :head_width] = low(qkv[:, :head_width] * scale)
    qkv_ref[:, head_width:] = low(qkv[:, head_width:])
    for head in range(head_width // HEAD_DIM):
        columns = [
            slice(part * head_width + head * HEAD_DIM, part * head_width + (head + 1) * HEAD_DIM)
            for part in range(3)
        ]
        query, key, value = (qkv_ref[:, c] for c in columns)
        scores = matmul_nt(query, key) + fill_ref[...]
        weights = jnp.exp(scores - jnp.max(scores, axis=1, keepdims=True))
        probs = low(weights * (1.0 / jnp.sum(weights, axis=1, keepdims=True)))
        probs_ref[head] = probs
        context_ref[:, columns[0]] = low(matmul(probs, value))


def project_kernel(need, context_ref, weights_ref, *refs):
    passed = len(refs) // 2 - 1
    near_ref, far_ref = refs[passed : passed + 2]
    for number, (in_ref, out_ref) in enumerate(zip(refs[:passed], refs[passed + 2 :])):
        need(2 + number)
        out_ref[...] = in_ref[...]
    need(0)
    need(1)
    width = context_ref.shape[1]
    back_into(context_ref, weights_ref, slice(3 * width, None), near_ref, far_ref)


def first_norm_kernel(
    need,
    small_ref,
    near_ref,
    arrived_ref,
    across_ref,
    tokens_ref,
    first_ref,
    unit_ref,
    scale_ref,
    low_ref,
):
    need(3)
    total = (
        wide(tokens_ref[...])
        + own_sum(need, near_ref, arrived_ref, across_ref)
        + small_ref[0:1]
    )
    centred = total - jnp.mean(total, axis=1, keepdims=True)
    scale = lax.rsqrt(jnp.mean(centred * centred, axis=1, keepdims=True) + epsilon)
    unit = centred * scale
    first = unit * small_ref[1:2] + small_ref[2:3]
    unit_ref[...] = unit
    scale_ref[...] = scale
    first_ref[...] = first
    low_ref[...] = low(first)


def inner_kernel(need, bias_ref, rows_ref, weights_ref, active_ref, slope_ref):
    need(0)
    need(1)
    for start in range(0, active_ref.shape[1], 256):
        columns = slice(start, start + 256)
        hidden = matmul(rows_ref[...], weights_ref[:, columns]) + bias_ref[:, columns]
        share = 0.5 + 0.5 * lax.erf(hidden * (0.5**0.5))
        active_ref[:, columns] = low(hidden * share)
        slope_ref[:, columns] = share + hidden * jnp.exp(-0.5 * hidden * hidden) * (
            0.3989422804014327
        )


def outer_kernel(need, active_ref, weights_ref, near_ref, far_ref):
    need(0)
    need(1)
    back_into(active_ref, weights_ref, slice(None), near_ref, far_ref)


def second_norm_kernel(
    in_slots,
    need,
    ranks_ref,
    lengths_ref,
    small_ref,
    near_ref,
    arrived_ref,
    across_ref,
    first_ref,
    grad_ref,
    out_ref,
    second_grad_ref,
    low_ref,
    sums_ref,
):
    rows, _ = first_ref.shape
    need(3)
    need(4)
    total = first_ref[...] + own_sum(need, near_ref, arrived_ref, across_ref) + small_ref[3:4]
    centred = total - jnp.mean(total, axis=1, keepdims=True)
    scale = lax.rsqrt(jnp.mean(centred * centred, axis=1, keepdims=True) + epsilon)
    unit = centred * scale
    place = ranks_ref[1] * rows + lax.broadcasted_iota(jnp.int32, (rows, 1), 0)
    valid = jnp.where(segments(lengths_ref, place) < lengths_ref.shape[1], 1.0, 0.0)
    gain = small_ref[4:5]
    second = (unit * gain + small_ref[5:6]) * valid
    from_slots(second, ranks_ref[0], in_slots, out_ref)
    cot = wide(grad_ref[...]) * valid
    pulled = cot * gain
    second_grad = scale * (
        pulled
        - jnp.mean(pulled, axis=1, keepdims=True)
        - unit * jnp.mean(pulled * unit, axis=1, keepdims=True)
    )
    second_grad_ref[...] = second_grad
    rounded = low(second_grad)
    low_ref[...] = rounded
    sums_ref[0:1] = jnp.sum(wide(rounded), axis=0, keepdims=True)
    sums_ref[1:2] = jnp.sum(cot * unit, axis=0, keepdims=True)
    sums_ref[2:3] = jnp.sum(cot, axis=0, keepdims=True)
    sums_ref[3:8] = jnp.zeros_like(sums_ref[3:8])


def hidden_grad_kernel(
    need, rows_ref, outer_ref, slope_ref, inner_ref, hidden_grad_ref, near_ref, far_ref, sums_ref
):
    for number in range(3):
        need(number)
    for start in range(0, hidden_grad_ref.shape[1], 256):
        columns = slice(start, start + 256)
        grad = low(matmul(rows_ref[...], outer_ref[:, columns]) * slope_ref[:, columns])
        hidden_grad_ref[:, columns] = grad
        sums_ref[0:1, columns] = jnp.sum(wide(grad), axis=0, keepdims=True)
    need(3)
    back_into(hidden_grad_ref, inner_ref, slice(None), near_ref, far_ref)


def single_grad_kernel(need, left_ref, right_ref, *out_refs):
    need(0)
    need(1)
    weight_grad_into([(left_ref, right_ref)], out_refs)


def first_back_kernel(
    in_slots,
    need,
    ranks_ref,
    scale_ref,
    small_ref,
    second_sums_ref,
    near_ref,
    arrived_ref,
    across_ref,
    second_grad_ref,
    unit_ref,
    mix_ref,
    low_ref,
    sums_ref,
):
    need(3)
    need(4)
    cot = second_grad_ref[...] + own_sum(need, near_ref, arrived_ref, across_ref)
    unit = unit_ref[...]
    pulled = cot * small_ref[1:2]
    mix = scale_ref[...] * (
        pulled
        - jnp.mean(pulled, axis=1, keepdims=True)
        - unit * jnp.mean(pulled * unit, axis=1, keepdims=True)
    )
    mix_ref[...] = mix
    rounded = low(mix)
    low_ref[...] = rounded
    sums = jnp.concatenate(
        [
            jnp.sum(wide(rounded), axis=0, keepdims=True),
            jnp.sum(cot * unit, axis=0, keepdims=True),
            jnp.sum(cot, axis=0, keepdims=True),
            second_sums_ref[0:3],
            jnp.zeros((2, mix.shape[1]), jnp.float32),
        ],
        axis=0,
    )
    from_slots(sums, ranks_ref[0], in_slots, sums_ref)


def attention_back_kernel(
    scale,
    need,
    rows_ref,
    weights_ref,
    qkv_ref,
    probs_ref,
    grads_ref,
    near_ref,
    far_ref,
    sums_ref,
    context_grad_ref,
):
    head_width = context_grad_ref.shape[1]
    need(0)
    need(1)
    context_grad_ref[...] = low(matmul(rows_ref[...], weights_ref[:, 3 * head_width :]))
    need(2)
    need(3)
    for head in range(head_width // HEAD_DIM):
        columns = [
            slice(part * head_width + head * HEAD_DIM, part * head_width + (head + 1) * HEAD_DIM)
            for part in range(3)
        ]
        query, key, value = (qkv_ref[:, c] for c in columns)
        probs = probs_ref[head]
        context_grad = context_grad_ref[:, columns[0]]
        prob_grad = matmul_nt(context_grad, value)
        exact = wide(probs)
        product = prob_grad * exact
        score_grad = low(product - exact * jnp.sum(product, axis=1, keepdims=True))
        query_grad = low(matmul(score_grad, key)) * jnp.asarray(scale, jnp.bfloat16)
        key_grad = low(matmul_tn(score_grad, query))
        value_grad = low(matmul_tn(probs, context_grad))
        for place, grad in zip(columns, (query_grad, key_grad, value_grad)):
            grads_ref[:, place] = grad
    sums_ref[...] = jnp.zeros_like(sums_ref)
    sums_ref[0:1, : 3 * head_width] = jnp.sum(wide(grads_ref[...]), axis=0, keepdims=True)
    back_into(grads_ref, weights_ref, slice(0, 3 * head_width), near_ref, far_ref)


def attention_grad_kernel(need, tokens_ref, qkv_grad_ref, rows_ref, context_ref, *out_refs):
    for number in range(4):
        need(number)
    weight_grad_into([(tokens_ref, qkv_grad_ref), (rows_ref, context_ref)], out_refs)


def tokens_grad_kernel(
    in_slots, need, ranks_ref, near_ref, arrived_ref, across_ref, mix_ref, out_ref
):
    need(3)
    total = mix_ref[...] + own_sum(need, near_ref, arrived_ref, across_ref)
    from_slots(total, ranks_ref[0], in_slots, out_ref)


def finish_kernel(need, sums_ref, arrived_ref, *out_refs):
    *row_refs, query_ref, value_ref = out_refs
    for k, ref in enumerate(row_refs):
        ref[...] = sums_ref[k, :] + arrived_ref[k, :]
    width = query_ref.shape[0]
    k = len(row_refs)
    query_ref[...] = sums_ref[k, :width] + arrived_ref[k, :width]
    value_ref[...] = sums_ref[k, 2 * width : 3 * width] + arrived_ref[k, 2 * width : 3 * width]


def write_turned(total, out_ref):
    out_ref[...] = total.T


def write_plain(total, out_ref):
    out_ref[...] = total


def write_attention(total, query_ref, key_ref, value_ref, proj_ref):
    width = query_ref.shape[1]
    for place, ref in enumerate((query_ref, key_ref, value_ref)):
        ref[...] = total[:, place * width : (place + 1) * width]
    proj_ref[...] = total[:, 3 * width :].T


def on_device(
    tokens,
    key_mask,
    seq_lengths,
    w_query,
    b_query,
    w_key,
    w_value,
    b_value,
    w_proj,
    b_proj,
    gain_attn,
    shift_attn,
    w_inner,
    b_inner,
    w_outer,
    b_outer,
    gain_ffn,
    shift_ffn,
    out_grad,
):
    in_slots = paired()
    flag = seq_lengths[0, 0] >= 0
    ranks = jnp.stack([lax.axis_index("dp"), lax.axis_index("tensor")]).astype(jnp.int32)
    piece_rows, model_width = tokens.shape
    group_rows = piece_rows * lax.axis_size("tensor")
    half_rows = group_rows // 2
    shard_rows = w_query.shape[0]
    head_width = b_query.shape[0]
    heads = head_width // HEAD_DIM
    inner_width = b_inner.shape[0]
    scale = HEAD_DIM ** (-0.5)
    own = (piece_rows, model_width)
    partial_sums = [shaped((half_rows, model_width), jnp.float32), shaped((half_rows, model_width))]

    attn_shard = kernel_call(
        prepare_kernel,
        [shaped((shard_rows, 4 * head_width))],
        whole=[w_query, w_key, w_value, w_proj],
    )[0]
    shards = kernel_call(
        shards_kernel,
        [shaped((3 * shard_rows, 4 * head_width))],
        whole=[attn_shard, w_inner, w_outer],
    )[0]
    attn_beside, inner_beside, outer_beside = [], [], []
    if in_slots:
        beside = swap(shards, "dp", 1)
        attn_beside, inner_beside, outer_beside = (
            [part(beside, k * shard_rows, shard_rows)] for k in range(3)
        )
    attn_far = far_of(attn_shard)
    attn_above = above_of(attn_shard)
    small = jnp.stack(
        [b_proj, gain_attn, shift_attn, b_outer, gain_ffn, shift_ffn, b_proj, b_proj]
    )

    def tokens_in_part(tokens, out_grad, small):
        tokens, out_grad, small = kernel_call(
            partial(place_kernel, in_slots),
            [shaped(own), shaped(own), shaped(small.shape, jnp.float32)],
            whole=[tokens, out_grad, small],
            scalars=[ranks],
        )
        return tokens, out_grad, small, gather_rows(tokens)

    tokens, out_grad, small, token_rows = region(flag, tokens_in_part, tokens, out_grad, small)
    joined = [shaped((3 * shard_rows, model_width))] if in_slots else []
    inner_shard, *attn_joined = kernel_call(
        pass_kernel,
        [shaped(w_inner.shape), *joined],
        pieces=[[part(shards, shard_rows, shard_rows)]] + [attn_far + attn_above] * in_slots,
        marks=[tokens],
    )
    attn_weights = weight_pieces(
        attn_shard, attn_far, rest_of(attn_joined), attn_above, attn_beside
    )
    inner_far = far_of(inner_shard)
    inner_above = above_of(inner_shard)
    qkv_bias = jnp.concatenate([b_query, jnp.zeros_like(b_query), b_value])[None, :]
    qkv, probs, context = kernel_call(
        partial(attention_kernel, scale),
        [
            shaped((group_rows, 3 * head_width)),
            shaped((heads, group_rows, group_rows)),
            shaped((group_rows, head_width)),
        ],
        scalars=[ranks, seq_lengths],
        whole=[key_mask.reshape(lax.axis_size("tensor"), piece_rows), qkv_bias],
        pieces=[token_rows, attn_weights],
        marks=[inner_shard],
        scratch=[pltpu.VMEM((group_rows, group_rows), jnp.float32)],
    )
    near, far, outer_shard, *inner_joined = kernel_call(
        project_kernel,
        [*partial_sums, shaped(inner_shard.shape), *joined],
        pieces=[[context], attn_weights, [part(shards, 2 * shard_rows, shard_rows)]]
        + [inner_far + inner_above] * in_slots,
    )
    inner_weights = weight_pieces(
        inner_shard, inner_far, rest_of(inner_joined), inner_above, inner_beside
    )
    outer_far = far_of(outer_shard)
    outer_corner = above_of(beside[2 * shard_rows :]) if in_slots else []
    def first_part(near, far, tokens, small):
        terms = scatter_rows(near, far)
        return kernel_call(
            first_norm_kernel,
            [
                shaped(own, jnp.float32),
                shaped(own, jnp.float32),
                shaped((piece_rows, 1), jnp.float32),
                shaped(own),
            ],
            whole=[small],
            pieces=[*terms, [tokens]],
        )

    first, unit, unit_scale, first_low = region(flag, first_part, near, far, tokens, small)
    outer_weights = weight_pieces(
        outer_shard,
        outer_far,
        rest_of(outer_far),
        outer_corner + above_of(outer_shard),
        outer_beside,
    )

    def inner_part(first_low, arrived, marks):
        norm_rows = gather_rows(first_low)
        return norm_rows, kernel_call(
            inner_kernel,
            [shaped((group_rows, inner_width)), shaped((group_rows, inner_width), jnp.float32)],
            whole=[b_inner[None, :]],
            pieces=[norm_rows, arrived + inner_beside],
            marks=marks,
        )

    norm_rows, (active, slope) = region(
        flag,
        inner_part,
        first_low,
        inner_weights[: len(inner_weights) - len(inner_beside)],
        outer_far + outer_corner,
    )
    near, far = kernel_call(
        outer_kernel, partial_sums, pieces=[[active], outer_weights]
    )
    terms = scatter_rows(near, far)
    layer_out, second_grad, branch_grad, second_sums = kernel_call(
        partial(second_norm_kernel, in_slots),
        [
            shaped(own),
            shaped(own, jnp.float32),
            shaped(own),
            shaped((8, model_width), jnp.float32),
        ],
        scalars=[ranks, seq_lengths],
        whole=[small],
        pieces=[*terms, [first], [out_grad]],
    )

    branch_rows = gather_rows(branch_grad, joined=False)
    outer_cuts = kernel_call(
        single_grad_kernel,
        weight_cuts(model_width, inner_width),
        pieces=[branch_rows, [active]],
    )
    outer_state = scatter_first(outer_cuts)
    hidden_grad, near, far, inner_sums = kernel_call(
        hidden_grad_kernel,
        [
            shaped((group_rows, inner_width)),
            *partial_sums,
            shaped((1, inner_width), jnp.float32),
        ],
        pieces=[branch_rows, outer_weights, [slope], inner_weights],
        marks=[outer_cuts[0]],
    )

    def first_back_part(near, far, norm_rows, hidden_grad, rest):
        terms = scatter_rows(near, far)
        inner_cuts = kernel_call(
            single_grad_kernel,
            weight_cuts(model_width, inner_width),
            pieces=[norm_rows, [hidden_grad]],
            marks=[terms[1][0][0]],
        )
        second_grad, unit, *small_operands = rest
        return inner_cuts, kernel_call(
            partial(first_back_kernel, in_slots),
            [shaped(own, jnp.float32), shaped(own), shaped((8, model_width), jnp.float32)],
            scalars=[ranks],
            whole=small_operands,
            pieces=[*terms, [second_grad], [unit]],
            marks=inner_cuts[:1],
        )

    inner_cuts, (mix_grad, proj_grad, sums) = region(
        flag,
        first_back_part,
        near,
        far,
        norm_rows,
        hidden_grad,
        [second_grad, unit, unit_scale, small, second_sums],
    )
    outer_terms, outer_beside, outer_mark = scatter_second(outer_state, [proj_grad])
    inner_state = scatter_first(inner_cuts)

    def attention_back_part(proj_grad, qkv, probs, marks):
        proj_rows = gather_rows(proj_grad)
        return (
            proj_rows,
            kernel_call(
                partial(attention_back_kernel, scale),
                [
                    shaped((group_rows, 3 * head_width)),
                    *partial_sums,
                    shaped((1, model_width), jnp.float32),
                ],
                pieces=[proj_rows, attn_weights, [qkv], [probs]],
                marks=marks,
                scratch=[pltpu.VMEM((group_rows, head_width), jnp.bfloat16)],
            ),
        )

    proj_rows, (qkv_grad, near, far, attn_sums) = region(
        flag, attention_back_part, proj_grad, qkv, probs, outer_mark
    )
    attn_state = scatter_first(
        kernel_call(
            attention_grad_kernel,
            weight_cuts(model_width, 4 * head_width),
            pieces=[token_rows, [qkv_grad], proj_rows, [context]],
        )
    )
    inner_terms, inner_beside, _ = scatter_second(
        inner_state, [attn_state[0], *outer_terms[2:]]
    )

    offsets = [1 << bit for bit in range(lax.axis_size("dp").bit_length() - 1)]

    def sums_part(sums, inner_sums, attn_sums, mark):
        sums = sums + swap(sums, "tensor", 1)
        sums = sums + swap(sums, "tensor", 2)
        sums = jnp.concatenate([sums[:6], inner_sums, attn_sums], axis=0)
        for offset in offsets[:-1]:
            sums = sums + swap(sums, "dp", offset)
        return sums

    sums = region(flag, sums_part, sums, inner_sums, attn_sums, attn_state[0])
    waiting = [outer_beside, inner_beside] if in_slots else []
    attn_terms, beside, attn_mark = scatter_second(
        attn_state, [sums, *inner_terms[2:]], waiting
    )
    besides = [[]] * 3
    if in_slots:
        besides = swap(beside, "dp", 1)
        besides = [[part(besides, k * shard_rows, shard_rows)] for k in range(3)]

    def tokens_part(near, far, mix_grad, mark):
        terms = scatter_rows(near, far)
        return kernel_call(
            partial(tokens_grad_kernel, in_slots),
            [shaped(own, jnp.float32)],
            scalars=[ranks],
            pieces=[*terms, [mix_grad]],
            marks=[mark],
        )[0]

    tokens_grad = region(flag, tokens_part, near, far, mix_grad, attn_mark[0])
    *shared, db_inner, db_query, db_value = kernel_call(
        finish_kernel,
        [shaped((model_width,), jnp.float32)] * 6
        + [shaped(b.shape, jnp.float32) for b in (b_inner, b_query, b_value)],
        whole=[sums, swap(sums, "dp", offsets[-1])],
        marks=[tokens_grad],
    )
    dw_query, dw_key, dw_value, dw_proj = scatter_last(
        attn_terms + besides[0],
        write_attention,
        [shaped(w.shape, jnp.float32) for w in (w_query, w_key, w_value, w_proj)],
        [tokens_grad],
    )
    dw_outer = scatter_last(
        outer_terms + besides[1], write_turned, [shaped(w_outer.shape, jnp.float32)], [tokens_grad]
    )[0]
    dw_inner = scatter_last(
        inner_terms + besides[2], write_plain, [shaped(w_inner.shape, jnp.float32)], [tokens_grad]
    )[0]
    db_proj, dgain_attn, dshift_attn, db_outer, dgain_ffn, dshift_ffn = shared
    return (
        layer_out,
        tokens_grad,
        dw_query,
        db_query,
        dw_key,
        dw_value,
        db_value,
        dw_proj,
        db_proj,
        dgain_attn,
        dshift_attn,
        dw_inner,
        db_inner,
        dw_outer,
        db_outer,
        dgain_ffn,
        dshift_ffn,
    )


def solution(mesh):
    in_specs = (
        P(("dp", "tensor"), None),
        P("dp"),
        P("dp", None),
        P("dp", "tensor"),
        P("tensor"),
        P("dp", "tensor"),
        P("dp", "tensor"),
        P("tensor"),
        P("tensor", "dp"),
        P(),
        P(),
        P(),
        P("dp", "tensor"),
        P("tensor"),
        P("tensor", "dp"),
        P(),
        P(),
        P(),
        P(("dp", "tensor"), None),
    )
    out_specs = (
        P(("dp", "tensor"), None),
        P(("dp", "tensor"), None),
        P("dp", "tensor"),
        P("tensor"),
        P("dp", "tensor"),
        P("dp", "tensor"),
        P("tensor"),
        P("tensor", "dp"),
        P(),
        P(),
        P(),
        P("dp", "tensor"),
        P("tensor"),
        P("tensor", "dp"),
        P(),
        P(),
        P(),
    )
    return jax.shard_map(
        on_device, mesh=mesh, in_specs=in_specs, out_specs=out_specs, check_vma=False
    )
```

```python
from functools import partial

import jax
import jax.numpy as jnp
from jax import lax
from jax.experimental import pallas as pl
from jax.experimental.pallas import tpu as pltpu
from jax.sharding import PartitionSpec as P

HEAD_DIM = 64


epsilon = 1e-12
masked_fill = -1e30

row_slots = (0, 2, 1, 3)
slot_offsets = (0, 4, 6, 5, 7, 3, 2, 1)


def matmul(left_side, right_side):
    return jnp.dot(left_side, right_side, preferred_element_type=jnp.float32)


def matmul_nt(left_side, right_side):
    return lax.dot_general(
        left_side, right_side, (((1,), (1,)), ((), ())), preferred_element_type=jnp.float32
    )


def matmul_tn(left_side, right_side):
    return lax.dot_general(
        left_side, right_side, (((0,), (0,)), ((), ())), preferred_element_type=jnp.float32
    )


def low(value):
    return value.astype(jnp.bfloat16)


def wide(value):
    return value.astype(jnp.float32)


VMEM_LIMIT = 63 << 20
QUICK, SLOW = 0.01, 2


def shaped(shape, dtype=jnp.bfloat16):
    return jax.ShapeDtypeStruct(shape, dtype)


def paired():
    return lax.axis_size("dp") == len(slot_offsets)


def swap(block, axis_name, offset):
    count = lax.axis_size(axis_name)
    return lax.ppermute(block, axis_name, [(i, i ^ offset) for i in range(count)])


def part(array, start, rows):
    return array, start, rows


def kernel_call(body, out_shape, whole=(), pieces=(), scalars=(), marks=(), scratch=(), us=QUICK):
    pieces = [
        [p if isinstance(p, tuple) else (p, 0, p.shape[0]) for p in some] for some in pieces
    ]
    buffers = [
        pltpu.VMEM((sum(p[2] for p in some), *some[0][0].shape[1:]), some[0][0].dtype)
        for some in pieces
    ]
    flat = [p for some in pieces for p in some]
    flat_out, tree = jax.tree.flatten(list(out_shape))
    counts = (len(scalars), len(whole), len(flat), len(marks), len(flat_out), len(buffers))

    def run(*refs):
        groups, start = [], 0
        for count in counts:
            groups.append(refs[start : start + count])
            start += count
        scalar_refs, whole_refs, piece_refs, _, out_refs, buffer_refs = groups
        rest = refs[start:]
        copies = []
        if flat:
            done, rest = rest[0], rest[1:]
            k = 0
            for some, buffer in zip(pieces, buffer_refs):
                row, mine = 0, []
                for _, first, rows in some:
                    mine.append(
                        pltpu.make_async_copy(
                            piece_refs[k].at[pl.ds(first, rows)],
                            buffer.at[pl.ds(row, rows)],
                            done.at[k],
                        )
                    )
                    row += rows
                    k += 1
                copies.append(mine)
            for copy in (c for mine in copies for c in mine):
                copy.start()

        def need(number):
            for copy in copies[number]:
                copy.wait()

        outs = jax.tree.unflatten(tree, out_refs)
        body(need, *scalar_refs, *whole_refs, *buffer_refs, *outs, *rest)

    anywhere = pl.BlockSpec(memory_space=pl.ANY)
    inside = pl.BlockSpec(memory_space=pltpu.VMEM)
    semaphores = [pltpu.SemaphoreType.DMA((len(flat),))] if flat else []
    results = pl.pallas_call(
        run,
        out_shape=flat_out,
        in_specs=[pl.BlockSpec(memory_space=pltpu.SMEM)] * len(scalars)
        + [inside] * len(whole)
        + [pl.BlockSpec(memory_space=pltpu.HBM)] * len(flat)
        + [anywhere] * len(marks),
        out_specs=[inside] * len(flat_out),
        scratch_shapes=buffers + semaphores + list(scratch),
        compiler_params=pltpu.CompilerParams(vmem_limit_bytes=VMEM_LIMIT),
        cost_estimate=pl.CostEstimate(
            flops=int(us * 1.1e9), bytes_accessed=int(us * 3.5e6), transcendentals=0
        ),
    )(*scalars, *whole, *[p[0] for p in flat], *marks)
    return jax.tree.unflatten(tree, results)


def region(flag, body, *operands):
    def nothing(*some):
        return jax.tree.map(lambda x: jnp.zeros(x.shape, x.dtype), jax.eval_shape(body, *operands))

    return lax.cond(flag, body, nothing, *operands)


RIDERS = 8


def pack(value):
    high = wide(low(value))
    return low(jnp.concatenate([high, value - high], axis=0))


def unpack(packed):
    value = wide(packed[...])
    return value[:RIDERS] + value[RIDERS:]


def join_kernel(need, own_ref, across_ref, out_ref):
    rows = own_ref.shape[0]
    need(0)
    out_ref[:rows] = own_ref[...]
    need(1)
    out_ref[rows:] = across_ref[...]


def gather_rows(piece, joined=True):
    across = swap(piece, "tensor", 2)
    if not joined:
        return [piece, across, swap(piece, "tensor", 1), swap(across, "tensor", 1)]
    rows, columns = piece.shape
    pair = kernel_call(join_kernel, [shaped((2 * rows, columns))], pieces=[[piece], [across]])[0]
    return [pair, swap(pair, "tensor", 1)]


def scatter_rows(near, far):
    half = near.shape[0] // 2
    arrived = swap(far, "tensor", 1)
    turned = low(near[half:] + wide(arrived[half:]))
    return [[part(near, 0, half)], [part(arrived, 0, half)], [swap(turned, "tensor", 2)]]


def own_sum(need, near_ref, arrived_ref, across_ref):
    for number in range(3):
        need(number)
    return near_ref[...] + wide(arrived_ref[...]) + wide(across_ref[...])


def far_of(shard):
    return [swap(shard, "dp", 4), swap(shard, "dp", 6)] if paired() else []


def above_of(shard):
    return [swap(shard, "dp", 2)] if paired() else []


def rest_of(pieces):
    return [swap(p, "dp", 1) for p in pieces]


def weight_pieces(shard, far, rest, above, beside):
    if not paired():
        return [lax.all_gather(shard, "dp", axis=0, tiled=True)]
    return [shard, *far, *rest, *above, *beside]


def weight_cuts(width, columns):
    if not paired():
        return [shaped((width, columns), jnp.float32)]
    block = width // len(slot_offsets)
    return [shaped((block, columns), jnp.float32)] + [
        shaped((block * n, columns)) for n in (2, 2, 2, 1)
    ]


def weight_cuts_with_sums(width, columns):
    cuts = weight_cuts(width, columns)
    for k in (2, 3):
        if paired():
            cuts[k] = shaped((cuts[k].shape[0] + 2 * RIDERS, columns))
    return cuts + [shaped((2 * RIDERS, columns))]


def weight_grad_into(pairs, out_refs):
    places, start = [], 0
    for out_ref in out_refs:
        rows = out_ref.shape[0] // 128 * 128
        places.append((out_ref, start, start + rows))
        start += rows
    for first in range(0, start, 512):
        last, column = min(first + 512, start), 0
        for left_ref, right_ref in pairs:
            columns = slice(column, column + right_ref.shape[1])
            column += right_ref.shape[1]
            block = matmul_tn(left_ref[:, first:last], right_ref[...])
            for out_ref, low_row, high_row in places:
                begin, end = max(first, low_row), min(last, high_row)
                if begin < end:
                    out_ref[begin - low_row : end - low_row, columns] = block[
                        begin - first : end - first
                    ].astype(out_ref.dtype)


def scatter_first(cuts):
    if not paired():
        return cuts
    kept, far, far_beside, above, beside = cuts
    return kept, far, beside, swap(far_beside, "dp", 1), swap(above, "dp", 2)


def combine_kernel(with_sums, need, far_ref, far_in_ref, beside_ref, above_ref, *rest):
    *waiting, far_out, farther_out, beside_out = rest
    block = far_ref.shape[0] // 2
    need(0)
    need(1)
    farther_out[:block] = low(wide(far_ref[block:]) + wide(far_in_ref[block : 2 * block]))
    far_out[:block] = low(wide(far_ref[:block]) + wide(far_in_ref[:block]))
    need(2)
    need(3)
    beside_out[:block] = low(wide(beside_ref[...]) + wide(above_ref[:block]))
    sums, waiting = waiting[:with_sums], waiting[with_sums:]
    place = block
    for number, ref in enumerate(waiting):
        need(4 + with_sums + number)
        beside_out[place : place + block] = ref[...]
        place += block
    if with_sums:
        need(4)
        packed = pack(unpack(sums[0]) + unpack(far_in_ref[2 * block :]))
        far_out[block:] = packed
        farther_out[block:] = packed
        beside_out[place:] = above_ref[block:]


def scatter_second(state, marks, waiting=(), sums=(), us=QUICK):
    if not paired():
        return state, None, []
    kept, far, beside, far_in, above = state
    block, columns = kept.shape
    extra = 2 * RIDERS * len(sums)
    first = [part(above, 0, block)] + [part(above, 2 * block, extra)] * len(sums)
    far_out, farther_out, beside_out = kernel_call(
        partial(combine_kernel, len(sums)),
        [shaped((block + extra, columns))] * 2
        + [shaped((block * (1 + len(waiting)) + extra, columns))],
        pieces=[[far], [far_in], [beside], first, *[[x] for x in (*sums, *waiting)]],
        marks=marks,
        us=us,
    )
    arrived = [swap(farther_out, "dp", 6), swap(far_out, "dp", 4)]
    terms = [kept, part(above, block, block), *[part(x, 0, block) for x in arrived]]
    riders = [part(x, block, extra) for x in (far_out, *arrived)]
    return terms, beside_out, [*riders, part(above, 2 * block, extra)] if sums else []


def last_kernel(write, count, riders, need, *refs):
    total = None
    for number, ref in enumerate(refs[:count]):
        need(number)
        total = wide(ref[...]) if total is None else total + wide(ref[...])
    for number in range(riders):
        need(count + number)
    write(total, *refs[count:])


def scatter_last(state, write, out_shape, marks=(), riders=()):
    if not paired():
        state = [lax.psum_scatter(state[0], "dp", scatter_dimension=0, tiled=True)]
    return kernel_call(
        partial(last_kernel, write, len(state), len(riders)),
        out_shape,
        pieces=[[term] for term in [*state, *riders]],
        marks=marks,
    )


def to_slots(array_ref, rank, in_slots):
    if not in_slots:
        return array_ref[...]
    width = array_ref.shape[-1] // len(slot_offsets)
    return jnp.concatenate(
        [
            array_ref[:, pl.ds(pl.multiple_of((rank ^ o) * width, width), width)]
            for o in slot_offsets
        ],
        axis=1,
    )


def from_slots(value, rank, in_slots, out_ref):
    if not in_slots:
        out_ref[...] = value.astype(out_ref.dtype)
        return
    width = out_ref.shape[-1] // len(slot_offsets)
    for place, o in enumerate(slot_offsets):
        out_ref[:, pl.ds(pl.multiple_of((rank ^ o) * width, width), width)] = value[
            :, place * width : (place + 1) * width
        ].astype(out_ref.dtype)


def segments(lengths_ref, places):
    total = jnp.int32(0)
    found = jnp.zeros(places.shape, jnp.int32)
    for k in range(lengths_ref.shape[1]):
        total = total + lengths_ref[0, k]
        found = found + jnp.where(places >= total, 1, 0)
    return found


def prepare_kernel(need, query_ref, key_ref, value_ref, proj_ref, out_ref):
    width = query_ref.shape[1]
    for place, ref in enumerate((query_ref, key_ref, value_ref)):
        out_ref[:, place * width : (place + 1) * width] = ref[...]
    out_ref[:, 3 * width :] = proj_ref[...].T


def shards_kernel(need, attn_ref, inner_ref, outer_ref, out_ref):
    rows = attn_ref.shape[0]
    out_ref[:rows] = attn_ref[...]
    out_ref[rows : 2 * rows] = inner_ref[...]
    out_ref[2 * rows :] = outer_ref[...].T


def place_kernel(in_slots, need, ranks_ref, tokens_ref, grad_ref, small_ref, *out_refs):
    for ref, out_ref in zip((tokens_ref, grad_ref, small_ref), out_refs):
        out_ref[...] = to_slots(ref, ranks_ref[0], in_slots)


def pass_kernel(need, *refs):
    half = len(refs) // 2
    for number, (in_ref, out_ref) in enumerate(zip(refs[:half], refs[half:])):
        need(number)
        out_ref[...] = in_ref[...]


def back_into(left_ref, right_ref, inner, near_ref, far_ref):
    half = near_ref.shape[0]
    for start in range(0, near_ref.shape[1], 256):
        columns = slice(start, start + 256)
        total = matmul_nt(left_ref[...], right_ref[columns, inner])
        near_ref[:, columns] = total[:half]
        far_ref[:, columns] = low(total[half:])


def attention_kernel(
    scale,
    need,
    ranks_ref,
    lengths_ref,
    key_ref,
    bias_ref,
    tokens_ref,
    weights_ref,
    qkv_ref,
    probs_ref,
    context_ref,
    fill_ref,
):
    rows = tokens_ref.shape[0]
    piece = rows // len(row_slots)
    head_width = context_ref.shape[1]
    rank = ranks_ref[1]
    down = lax.broadcasted_iota(jnp.int32, (rows, 1), 0)
    along = lax.broadcasted_iota(jnp.int32, (1, rows), 1)

    def places(index):
        slot, step = index // piece, index % piece
        owner = jnp.where(slot == 0, row_slots[0], 0)
        for k in range(1, len(row_slots)):
            owner = jnp.where(slot == k, row_slots[k], owner)
        return (owner ^ rank) * piece + step

    segment_down = segments(lengths_ref, places(down))
    segment_along = segments(lengths_ref, places(along))
    keys = jnp.concatenate([key_ref[pl.ds(rank ^ o, 1), :] for o in row_slots], axis=1)
    allowed = (segment_down == segment_along) & ((keys == 1) | (down == along))
    fill_ref[...] = jnp.where(allowed, 0.0, masked_fill)

    need(0)
    need(1)
    qkv = matmul(tokens_ref[...], weights_ref[:, : 3 * head_width]) + bias_ref[...]
    qkv_ref[:, :head_width] = low(qkv[:, :head_width] * scale)
    qkv_ref[:, head_width:] = low(qkv[:, head_width:])
    for head in range(head_width // HEAD_DIM):
        columns = [
            slice(part * head_width + head * HEAD_DIM, part * head_width + (head + 1) * HEAD_DIM)
            for part in range(3)
        ]
        query, key, value = (qkv_ref[:, c] for c in columns)
        scores = matmul_nt(query, key) + fill_ref[...]
        weights = jnp.exp(scores - jnp.max(scores, axis=1, keepdims=True))
        probs = low(weights * (1.0 / jnp.sum(weights, axis=1, keepdims=True)))
        probs_ref[head] = probs
        context_ref[:, columns[0]] = low(matmul(probs, value))


def project_kernel(need, context_ref, weights_ref, *refs):
    passed = len(refs) // 2 - 1
    near_ref, far_ref = refs[passed : passed + 2]
    for number, (in_ref, out_ref) in enumerate(zip(refs[:passed], refs[passed + 2 :])):
        need(2 + number)
        out_ref[...] = in_ref[...]
    need(0)
    need(1)
    width = context_ref.shape[1]
    back_into(context_ref, weights_ref, slice(3 * width, None), near_ref, far_ref)


def first_norm_kernel(
    need,
    small_ref,
    near_ref,
    arrived_ref,
    across_ref,
    tokens_ref,
    first_ref,
    unit_ref,
    scale_ref,
    low_ref,
):
    need(3)
    total = (
        wide(tokens_ref[...])
        + own_sum(need, near_ref, arrived_ref, across_ref)
        + small_ref[0:1]
    )
    centred = total - jnp.mean(total, axis=1, keepdims=True)
    scale = lax.rsqrt(jnp.mean(centred * centred, axis=1, keepdims=True) + epsilon)
    unit = centred * scale
    first = unit * small_ref[1:2] + small_ref[2:3]
    unit_ref[...] = unit
    scale_ref[...] = scale
    first_ref[...] = first
    low_ref[...] = low(first)


def inner_kernel(need, bias_ref, rows_ref, weights_ref, active_ref, slope_ref):
    need(0)
    need(1)
    for start in range(0, active_ref.shape[1], 256):
        columns = slice(start, start + 256)
        hidden = matmul(rows_ref[...], weights_ref[:, columns]) + bias_ref[:, columns]
        share = 0.5 + 0.5 * lax.erf(hidden * (0.5**0.5))
        active_ref[:, columns] = low(hidden * share)
        slope_ref[:, columns] = share + hidden * jnp.exp(-0.5 * hidden * hidden) * (
            0.3989422804014327
        )


def outer_kernel(need, active_ref, weights_ref, near_ref, far_ref):
    need(0)
    need(1)
    back_into(active_ref, weights_ref, slice(None), near_ref, far_ref)


def second_norm_kernel(
    in_slots,
    need,
    ranks_ref,
    lengths_ref,
    small_ref,
    near_ref,
    arrived_ref,
    across_ref,
    first_ref,
    grad_ref,
    out_ref,
    second_grad_ref,
    low_ref,
    sums_ref,
):
    rows, _ = first_ref.shape
    need(3)
    need(4)
    total = first_ref[...] + own_sum(need, near_ref, arrived_ref, across_ref) + small_ref[3:4]
    centred = total - jnp.mean(total, axis=1, keepdims=True)
    scale = lax.rsqrt(jnp.mean(centred * centred, axis=1, keepdims=True) + epsilon)
    unit = centred * scale
    place = ranks_ref[1] * rows + lax.broadcasted_iota(jnp.int32, (rows, 1), 0)
    valid = jnp.where(segments(lengths_ref, place) < lengths_ref.shape[1], 1.0, 0.0)
    gain = small_ref[4:5]
    second = (unit * gain + small_ref[5:6]) * valid
    from_slots(second, ranks_ref[0], in_slots, out_ref)
    cot = wide(grad_ref[...]) * valid
    pulled = cot * gain
    second_grad = scale * (
        pulled
        - jnp.mean(pulled, axis=1, keepdims=True)
        - unit * jnp.mean(pulled * unit, axis=1, keepdims=True)
    )
    second_grad_ref[...] = second_grad
    rounded = low(second_grad)
    low_ref[...] = rounded
    sums_ref[0:1] = jnp.sum(wide(rounded), axis=0, keepdims=True)
    sums_ref[1:2] = jnp.sum(cot * unit, axis=0, keepdims=True)
    sums_ref[2:3] = jnp.sum(cot, axis=0, keepdims=True)
    sums_ref[3:8] = jnp.zeros_like(sums_ref[3:8])


def hidden_grad_kernel(
    need, rows_ref, outer_ref, slope_ref, inner_ref, hidden_grad_ref, near_ref, far_ref, sums_ref
):
    need(0)
    need(1)
    for start in range(0, hidden_grad_ref.shape[1], 256):
        columns = slice(start, start + 256)
        product = matmul(rows_ref[...], outer_ref[:, columns])
        if start == 0:
            need(2)
        grad = low(product * slope_ref[:, columns])
        hidden_grad_ref[:, columns] = grad
        sums_ref[0:1, columns] = jnp.sum(wide(grad), axis=0, keepdims=True)
    need(3)
    back_into(hidden_grad_ref, inner_ref, slice(None), near_ref, far_ref)


def single_grad_kernel(need, left_ref, right_ref, *out_refs):
    need(0)
    need(1)
    weight_grad_into([(left_ref, right_ref)], out_refs)


def first_back_kernel(
    in_slots,
    need,
    ranks_ref,
    scale_ref,
    small_ref,
    second_sums_ref,
    near_ref,
    arrived_ref,
    across_ref,
    second_grad_ref,
    unit_ref,
    mix_ref,
    low_ref,
    sums_ref,
):
    rows = mix_ref.shape[0]
    need(3)
    need(4)
    cot = second_grad_ref[...] + own_sum(need, near_ref, arrived_ref, across_ref)
    unit = unit_ref[...]
    pulled = cot * small_ref[1:2]
    mix = scale_ref[...] * (
        pulled
        - jnp.mean(pulled, axis=1, keepdims=True)
        - unit * jnp.mean(pulled * unit, axis=1, keepdims=True)
    )
    mix_ref[...] = mix
    rounded = low(mix)
    low_ref[:rows] = rounded
    sums = jnp.concatenate(
        [
            jnp.sum(wide(rounded), axis=0, keepdims=True),
            jnp.sum(cot * unit, axis=0, keepdims=True),
            jnp.sum(cot, axis=0, keepdims=True),
            second_sums_ref[0:3],
            jnp.zeros((2, mix.shape[1]), jnp.float32),
        ],
        axis=0,
    )
    from_slots(sums, ranks_ref[0], in_slots, sums_ref)
    low_ref[rows:] = pack(sums_ref[...])


def attention_back_kernel(
    scale,
    need,
    inner_sums_ref,
    rows_ref,
    weights_ref,
    qkv_ref,
    probs_ref,
    tokens_ref,
    context_ref,
    riders_ref,
    grads_ref,
    near_ref,
    far_ref,
    *rest,
):
    *cut_refs, context_grad_ref = rest
    head_width = context_grad_ref.shape[1]
    need(0)
    need(1)
    context_grad_ref[...] = low(matmul(rows_ref[...], weights_ref[:, 3 * head_width :]))
    need(2)
    need(3)
    for head in range(head_width // HEAD_DIM):
        columns = [
            slice(part * head_width + head * HEAD_DIM, part * head_width + (head + 1) * HEAD_DIM)
            for part in range(3)
        ]
        query, key, value = (qkv_ref[:, c] for c in columns)
        probs = probs_ref[head]
        context_grad = context_grad_ref[:, columns[0]]
        prob_grad = matmul_nt(context_grad, value)
        exact = wide(probs)
        product = prob_grad * exact
        score_grad = low(product - exact * jnp.sum(product, axis=1, keepdims=True))
        query_grad = low(matmul(score_grad, key)) * jnp.asarray(scale, jnp.bfloat16)
        key_grad = low(matmul_tn(score_grad, query))
        value_grad = low(matmul_tn(probs, context_grad))
        for place, grad in zip(columns, (query_grad, key_grad, value_grad)):
            grads_ref[:, place] = grad
    for number in range(4, 7):
        need(number)
    *cut_refs, packed_ref = cut_refs
    own, across, beside, corner = (
        unpack(riders_ref[k * 2 * RIDERS : (k + 1) * 2 * RIDERS]) for k in range(4)
    )
    sums = (own + across) + (beside + corner)
    mine = jnp.sum(wide(grads_ref[...]), axis=0, keepdims=True)
    mine = jnp.concatenate([mine, jnp.zeros((1, head_width), jnp.float32)], axis=1)
    packed = pack(jnp.concatenate([sums[: RIDERS - 2], inner_sums_ref[...], mine], axis=0))
    packed_ref[...] = packed
    for ref in cut_refs[2:4]:
        ref[ref.shape[0] - 2 * RIDERS :] = packed
    weight_grad_into([(tokens_ref, grads_ref), (rows_ref, context_ref)], cut_refs)
    back_into(grads_ref, weights_ref, slice(0, 3 * head_width), near_ref, far_ref)


def tokens_grad_kernel(
    in_slots, need, ranks_ref, near_ref, arrived_ref, across_ref, mix_ref, out_ref
):
    need(3)
    total = mix_ref[...] + own_sum(need, near_ref, arrived_ref, across_ref)
    from_slots(total, ranks_ref[0], in_slots, out_ref)


def write_turned(total, out_ref):
    out_ref[...] = total.T


def write_plain(total, out_ref):
    out_ref[...] = total


def write_attention(total, *refs):
    riders, refs = refs[: len(refs) - 13], refs[len(refs) - 13 :]
    query_ref, key_ref, value_ref, proj_ref, inner_sum_ref, query_sum_ref, value_sum_ref = refs[:7]
    width = query_ref.shape[1]
    for place, ref in enumerate((query_ref, key_ref, value_ref)):
        ref[...] = total[:, place * width : (place + 1) * width]
    proj_ref[...] = total[:, 3 * width :].T
    if len(riders) > 1:
        own, farther, far, above, beside = (unpack(ref) for ref in riders)
        above = unpack(pack(above + beside))
        sums = (own + above) + (far + farther)
    else:
        sums = unpack(riders[0])
    for k, ref in enumerate(refs[7:]):
        ref[...] = sums[k, :]
    inner_sum_ref[...] = sums[6, :]
    query_sum_ref[...] = sums[7, :width]
    value_sum_ref[...] = sums[7, 2 * width : 3 * width]


def on_device(
    tokens,
    key_mask,
    seq_lengths,
    w_query,
    b_query,
    w_key,
    w_value,
    b_value,
    w_proj,
    b_proj,
    gain_attn,
    shift_attn,
    w_inner,
    b_inner,
    w_outer,
    b_outer,
    gain_ffn,
    shift_ffn,
    out_grad,
):
    in_slots = paired()
    flag = seq_lengths[0, 0] >= 0
    ranks = jnp.stack([lax.axis_index("dp"), lax.axis_index("tensor")]).astype(jnp.int32)
    piece_rows, model_width = tokens.shape
    group_rows = piece_rows * lax.axis_size("tensor")
    half_rows = group_rows // 2
    shard_rows = w_query.shape[0]
    head_width = b_query.shape[0]
    heads = head_width // HEAD_DIM
    inner_width = b_inner.shape[0]
    scale = HEAD_DIM ** (-0.5)
    own = (piece_rows, model_width)
    partial_sums = [shaped((half_rows, model_width), jnp.float32), shaped((half_rows, model_width))]

    attn_shard = kernel_call(
        prepare_kernel,
        [shaped((shard_rows, 4 * head_width))],
        whole=[w_query, w_key, w_value, w_proj],
    )[0]
    shards = kernel_call(
        shards_kernel,
        [shaped((3 * shard_rows, 4 * head_width))],
        whole=[attn_shard, w_inner, w_outer],
    )[0]
    attn_beside, inner_beside, outer_beside = [], [], []
    if in_slots:
        beside = swap(shards, "dp", 1)
        attn_beside, inner_beside, outer_beside = (
            [part(beside, k * shard_rows, shard_rows)] for k in range(3)
        )
    attn_far = far_of(attn_shard)
    attn_above = above_of(attn_shard)
    small = jnp.stack(
        [b_proj, gain_attn, shift_attn, b_outer, gain_ffn, shift_ffn, b_proj, b_proj]
    )

    def tokens_in_part(tokens, out_grad, small):
        tokens, out_grad, small = kernel_call(
            partial(place_kernel, in_slots),
            [shaped(own), shaped(own), shaped(small.shape, jnp.float32)],
            whole=[tokens, out_grad, small],
            scalars=[ranks],
        )
        return tokens, out_grad, small, gather_rows(tokens)

    tokens, out_grad, small, token_rows = region(flag, tokens_in_part, tokens, out_grad, small)
    joined = [shaped((3 * shard_rows, model_width))] if in_slots else []
    inner_shard, *attn_joined = kernel_call(
        pass_kernel,
        [shaped(w_inner.shape), *joined],
        pieces=[[part(shards, shard_rows, shard_rows)]] + [attn_far + attn_above] * in_slots,
        marks=[tokens],
    )
    attn_weights = weight_pieces(
        attn_shard, attn_far, rest_of(attn_joined), attn_above, attn_beside
    )
    inner_far = far_of(inner_shard)
    inner_above = above_of(inner_shard)
    qkv_bias = jnp.concatenate([b_query, jnp.zeros_like(b_query), b_value])[None, :]
    qkv, probs, context = kernel_call(
        partial(attention_kernel, scale),
        [
            shaped((group_rows, 3 * head_width)),
            shaped((heads, group_rows, group_rows)),
            shaped((group_rows, head_width)),
        ],
        scalars=[ranks, seq_lengths],
        whole=[key_mask.reshape(lax.axis_size("tensor"), piece_rows), qkv_bias],
        pieces=[token_rows, attn_weights],
        marks=[inner_shard],
        scratch=[pltpu.VMEM((group_rows, group_rows), jnp.float32)],
    )
    near, far, outer_shard, *inner_joined = kernel_call(
        project_kernel,
        [*partial_sums, shaped(inner_shard.shape), *joined],
        pieces=[[context], attn_weights, [part(shards, 2 * shard_rows, shard_rows)]]
        + [inner_far + inner_above] * in_slots,
    )
    inner_weights = weight_pieces(
        inner_shard, inner_far, rest_of(inner_joined), inner_above, inner_beside
    )
    outer_far = far_of(outer_shard)
    outer_corner = above_of(beside[2 * shard_rows :]) if in_slots else []
    def first_part(near, far, tokens, small):
        terms = scatter_rows(near, far)
        return kernel_call(
            first_norm_kernel,
            [
                shaped(own, jnp.float32),
                shaped(own, jnp.float32),
                shaped((piece_rows, 1), jnp.float32),
                shaped(own),
            ],
            whole=[small],
            pieces=[*terms, [tokens]],
        )

    first, unit, unit_scale, first_low = region(flag, first_part, near, far, tokens, small)
    outer_weights = weight_pieces(
        outer_shard,
        outer_far,
        rest_of(outer_far),
        outer_corner + above_of(outer_shard),
        outer_beside,
    )

    def inner_part(first_low, arrived, marks):
        norm_rows = gather_rows(first_low, joined=False)
        return norm_rows[1:], kernel_call(
            inner_kernel,
            [shaped((group_rows, inner_width)), shaped((group_rows, inner_width), jnp.float32)],
            whole=[b_inner[None, :]],
            pieces=[norm_rows, arrived + inner_beside],
            marks=marks,
        )

    other_rows, (active, slope) = region(
        flag,
        inner_part,
        first_low,
        inner_weights[: len(inner_weights) - len(inner_beside)],
        outer_far + outer_corner,
    )
    norm_rows = [first_low, *other_rows]
    near, far = kernel_call(
        outer_kernel, partial_sums, pieces=[[active], outer_weights]
    )
    terms = scatter_rows(near, far)
    layer_out, second_grad, branch_grad, second_sums = kernel_call(
        partial(second_norm_kernel, in_slots),
        [
            shaped(own),
            shaped(own, jnp.float32),
            shaped(own),
            shaped((8, model_width), jnp.float32),
        ],
        scalars=[ranks, seq_lengths],
        whole=[small],
        pieces=[*terms, [first], [out_grad]],
    )

    branch_rows = gather_rows(branch_grad, joined=False)
    outer_cuts = kernel_call(
        single_grad_kernel,
        weight_cuts(model_width, inner_width),
        pieces=[branch_rows, [active]],
    )
    outer_state = scatter_first(outer_cuts)
    hidden_grad, near, far, inner_sums = kernel_call(
        hidden_grad_kernel,
        [
            shaped((group_rows, inner_width)),
            *partial_sums,
            shaped((1, inner_width), jnp.float32),
        ],
        pieces=[branch_rows, outer_weights, [slope], inner_weights],
        marks=[outer_cuts[0]],
    )

    def inner_grad_part(near, far, norm_rows, hidden_grad):
        terms = scatter_rows(near, far)
        inner_cuts = kernel_call(
            single_grad_kernel,
            weight_cuts(model_width, inner_width),
            pieces=[norm_rows, [hidden_grad]],
            marks=[terms[1][0][0]],
        )
        return inner_cuts, [some[0][0] if isinstance(some[0], tuple) else some[0] for some in terms[1:]]

    inner_cuts, (arrived, across) = region(
        flag, inner_grad_part, near, far, norm_rows, hidden_grad
    )
    outer_terms, outer_beside, _ = scatter_second(outer_state, [across])
    outer_mark = [outer_beside] if in_slots else []
    mix_grad, proj_grad = kernel_call(
        partial(first_back_kernel, in_slots),
        [shaped(own, jnp.float32), shaped((piece_rows + 2 * RIDERS, model_width))],
        scalars=[ranks],
        whole=[unit_scale, small, second_sums],
        pieces=[
            [part(near, 0, piece_rows)],
            [part(arrived, 0, piece_rows)],
            [across],
            [second_grad],
            [unit],
        ],
        scratch=[pltpu.VMEM((RIDERS, model_width), jnp.float32)],
    )
    inner_state = scatter_first(inner_cuts)

    def row_parts(gathered, first, rows):
        whole = gathered[0].shape[0] // 2
        return [part(g, k * whole + first, rows) for g in gathered for k in range(2)]

    def attention_back_part(proj_grad, marks):
        gathered = gather_rows(proj_grad)
        return kernel_call(
            partial(attention_back_kernel, scale),
            [
                shaped((group_rows, 3 * head_width)),
                *partial_sums,
                *weight_cuts_with_sums(model_width, 4 * head_width),
            ],
            whole=[inner_sums],
            pieces=[
                row_parts(gathered, 0, piece_rows),
                attn_weights,
                [qkv],
                [probs],
                token_rows,
                [context],
                row_parts(gathered, piece_rows, 2 * RIDERS),
            ],
            marks=marks,
            scratch=[pltpu.VMEM((group_rows, head_width), jnp.bfloat16)],
        )[1:]

    near, far, *attn_cuts, sums = region(flag, attention_back_part, proj_grad, outer_mark)
    attn_state = scatter_first(attn_cuts)
    inner_terms, inner_beside, _ = scatter_second(
        inner_state, [attn_state[0], *[t[0] for t in outer_terms[2:]]], us=SLOW
    )

    def tokens_part(near, far, mix_grad, mark):
        terms = scatter_rows(near, far)
        return kernel_call(
            partial(tokens_grad_kernel, in_slots),
            [shaped(own, jnp.float32)],
            scalars=[ranks],
            pieces=[*terms, [mix_grad]],
            marks=[mark],
        )[0]

    tokens_grad = region(flag, tokens_part, near, far, mix_grad, attn_state[0])
    waiting = [outer_beside, inner_beside] if in_slots else []
    attn_terms, beside, riders = scatter_second(
        attn_state, [tokens_grad, *[t[0] for t in inner_terms[2:]]], waiting, [sums] * in_slots
    )
    besides = [[]] * 3
    if in_slots:
        besides = swap(beside, "dp", 1)
        riders.append(part(besides, 3 * shard_rows, 2 * RIDERS))
        besides = [[part(besides, k * shard_rows, shard_rows)] for k in range(3)]
    else:
        riders = [pack(lax.psum(unpack(sums), "dp"))]
    dw_outer = scatter_last(
        outer_terms + besides[1], write_turned, [shaped(w_outer.shape, jnp.float32)]
    )[0]
    dw_inner = scatter_last(
        inner_terms + besides[2], write_plain, [shaped(w_inner.shape, jnp.float32)]
    )[0]
    dw_query, dw_key, dw_value, dw_proj, db_inner, db_query, db_value, *shared = scatter_last(
        attn_terms + besides[0],
        write_attention,
        [shaped(w.shape, jnp.float32) for w in (w_query, w_key, w_value, w_proj)]
        + [shaped(b.shape, jnp.float32) for b in (b_inner, b_query, b_value)]
        + [shaped((model_width,), jnp.float32)] * 6,
        [dw_outer, dw_inner],
        riders,
    )
    db_proj, dgain_attn, dshift_attn, db_outer, dgain_ffn, dshift_ffn = shared
    return (
        layer_out,
        tokens_grad,
        dw_query,
        db_query,
        dw_key,
        dw_value,
        db_value,
        dw_proj,
        db_proj,
        dgain_attn,
        dshift_attn,
        dw_inner,
        db_inner,
        dw_outer,
        db_outer,
        dgain_ffn,
        dshift_ffn,
    )


def solution(mesh):
    in_specs = (
        P(("dp", "tensor"), None),
        P("dp"),
        P("dp", None),
        P("dp", "tensor"),
        P("tensor"),
        P("dp", "tensor"),
        P("dp", "tensor"),
        P("tensor"),
        P("tensor", "dp"),
        P(),
        P(),
        P(),
        P("dp", "tensor"),
        P("tensor"),
        P("tensor", "dp"),
        P(),
        P(),
        P(),
        P(("dp", "tensor"), None),
    )
    out_specs = (
        P(("dp", "tensor"), None),
        P(("dp", "tensor"), None),
        P("dp", "tensor"),
        P("tensor"),
        P("dp", "tensor"),
        P("dp", "tensor"),
        P("tensor"),
        P("tensor", "dp"),
        P(),
        P(),
        P(),
        P("dp", "tensor"),
        P("tensor"),
        P("tensor", "dp"),
        P(),
        P(),
        P(),
    )
    return jax.shard_map(
        on_device, mesh=mesh, in_specs=in_specs, out_specs=out_specs, check_vma=False
    )
```

```python
from functools import partial

import jax
import jax.numpy as jnp
from jax import lax
from jax.experimental import pallas as pl
from jax.experimental.pallas import tpu as pltpu
from jax.sharding import PartitionSpec as P

HEAD_DIM = 64


epsilon = 1e-12
masked_fill = -1e30

row_slots = (0, 2, 1, 3)
slot_offsets = (0, 4, 6, 5, 7, 3, 2, 1)


def matmul(left_side, right_side):
    return jnp.dot(left_side, right_side, preferred_element_type=jnp.float32)


def matmul_nt(left_side, right_side):
    return lax.dot_general(
        left_side, right_side, (((1,), (1,)), ((), ())), preferred_element_type=jnp.float32
    )


def matmul_tn(left_side, right_side):
    return lax.dot_general(
        left_side, right_side, (((0,), (0,)), ((), ())), preferred_element_type=jnp.float32
    )


def low(value):
    return value.astype(jnp.bfloat16)


def wide(value):
    return value.astype(jnp.float32)


VMEM_LIMIT = 63 << 20
QUICK, SLOW = 0.01, 2


def shaped(shape, dtype=jnp.bfloat16):
    return jax.ShapeDtypeStruct(shape, dtype)


def paired():
    return lax.axis_size("dp") == len(slot_offsets)


def swap(block, axis_name, offset):
    count = lax.axis_size(axis_name)
    return lax.ppermute(block, axis_name, [(i, i ^ offset) for i in range(count)])


def part(array, start, rows, columns=None):
    return array, start, rows, columns


def kernel_call(body, out_shape, whole=(), pieces=(), scalars=(), marks=(), scratch=(), us=QUICK, pinned=True):
    pieces = [
        [p if isinstance(p, tuple) else part(p, 0, p.shape[0]) for p in some] for some in pieces
    ]
    buffers = [
        pltpu.VMEM(
            (sum(p[2] for p in some), *((some[0][3][1],) if some[0][3] else some[0][0].shape[1:])),
            some[0][0].dtype,
        )
        for some in pieces
    ]
    flat = [p for some in pieces for p in some]
    flat_out, tree = jax.tree.flatten(list(out_shape))
    counts = (len(scalars), len(whole), len(flat), len(marks), len(flat_out), len(buffers))

    def run(*refs):
        groups, start = [], 0
        for count in counts:
            groups.append(refs[start : start + count])
            start += count
        scalar_refs, whole_refs, piece_refs, _, out_refs, buffer_refs = groups
        rest = refs[start:]
        copies = []
        if flat:
            done, rest = rest[0], rest[1:]
            k = 0
            for some, buffer in zip(pieces, buffer_refs):
                row, mine = 0, []
                for _, first, rows, columns in some:
                    place = (pl.ds(first, rows), pl.ds(*columns)) if columns else pl.ds(first, rows)
                    mine.append(
                        pltpu.make_async_copy(
                            piece_refs[k].at[place],
                            buffer.at[pl.ds(row, rows)],
                            done.at[k],
                        )
                    )
                    row += rows
                    k += 1
                copies.append(mine)
            for copy in (c for mine in copies for c in mine):
                copy.start()

        def need(number):
            for copy in copies[number]:
                copy.wait()

        outs = jax.tree.unflatten(tree, out_refs)
        body(need, *scalar_refs, *whole_refs, *buffer_refs, *outs, *rest)

    anywhere = pl.BlockSpec(memory_space=pl.ANY)
    inside = pl.BlockSpec(memory_space=pltpu.VMEM)
    semaphores = [pltpu.SemaphoreType.DMA((len(flat),))] if flat else []
    results = pl.pallas_call(
        run,
        out_shape=flat_out,
        in_specs=[pl.BlockSpec(memory_space=pltpu.SMEM)] * len(scalars)
        + [inside] * len(whole)
        + [pl.BlockSpec(memory_space=pltpu.HBM) if pinned else anywhere] * len(flat)
        + [anywhere] * len(marks),
        out_specs=[inside] * len(flat_out),
        scratch_shapes=buffers + semaphores + list(scratch),
        compiler_params=pltpu.CompilerParams(vmem_limit_bytes=VMEM_LIMIT),
        cost_estimate=pl.CostEstimate(
            flops=int(us * 1.1e9), bytes_accessed=int(us * 3.5e6), transcendentals=0
        ),
    )(*scalars, *whole, *[p[0] for p in flat], *marks)
    return jax.tree.unflatten(tree, results)


def tie(blocks, marks):
    pinned = pl.BlockSpec(memory_space=pltpu.HBM)
    return pl.pallas_call(
        lambda *refs: None,
        out_shape=[shaped(b.shape, b.dtype) for b in blocks],
        in_specs=[pinned] * len(blocks) + [pl.BlockSpec(memory_space=pl.ANY)] * len(marks),
        out_specs=[pinned] * len(blocks),
        input_output_aliases={k: k for k in range(len(blocks))},
        cost_estimate=pl.CostEstimate(flops=0, bytes_accessed=0, transcendentals=0),
    )(*blocks, *marks)


def region(flag, body, *operands):
    def nothing(*some):
        return jax.tree.map(lambda x: jnp.zeros(x.shape, x.dtype), jax.eval_shape(body, *operands))

    return lax.cond(flag, body, nothing, *operands)


RIDERS = 8


def pack(value):
    high = wide(low(value))
    return low(jnp.concatenate([high, value - high], axis=0))


def unpack(packed):
    value = wide(packed[...])
    return value[:RIDERS] + value[RIDERS:]


def join_kernel(need, own_ref, across_ref, out_ref):
    rows = own_ref.shape[0]
    need(0)
    out_ref[:rows] = own_ref[...]
    need(1)
    out_ref[rows:] = across_ref[...]


def gather_rows(piece, joined=True):
    across = swap(piece, "tensor", 2)
    if not joined:
        return [piece, across, swap(piece, "tensor", 1), swap(across, "tensor", 1)]
    rows, columns = piece.shape
    pair = kernel_call(join_kernel, [shaped((2 * rows, columns))], pieces=[[piece], [across]])[0]
    return [pair, swap(pair, "tensor", 1)]


def turn_kernel(need, near_ref, arrived_ref, out_ref):
    need(0)
    need(1)
    out_ref[...] = low(near_ref[...] + wide(arrived_ref[...]))


def scatter_rows(near, far):
    half = near.shape[0] // 2
    if isinstance(far, list):
        beside, corner = (swap(f, "tensor", 1) for f in far)
        turned = kernel_call(
            turn_kernel, [shaped(corner.shape)], pieces=[[part(near, half, half)], [corner]]
        )[0]
    else:
        arrived = swap(far, "tensor", 1)
        beside = part(arrived, 0, half)
        turned = low(near[half:] + wide(arrived[half:]))
    return [[part(near, 0, half)], [beside], [swap(turned, "tensor", 2)]]


def own_sum(need, near_ref, arrived_ref, across_ref):
    for number in range(3):
        need(number)
    return near_ref[...] + wide(arrived_ref[...]) + wide(across_ref[...])


def far_of(shard):
    return [swap(shard, "dp", 4), swap(shard, "dp", 6)] if paired() else []


def above_of(shard):
    return [swap(shard, "dp", 2)] if paired() else []


def rest_of(pieces):
    return [swap(p, "dp", 1) for p in pieces]


def weight_pieces(shard, far, rest, above, beside):
    if not paired():
        return [lax.all_gather(shard, "dp", axis=0, tiled=True)]
    return [shard, *far, *rest, *above, *beside]


def weight_cuts(width, columns):
    if not paired():
        return [shaped((width, columns), jnp.float32)]
    block = width // len(slot_offsets)
    return [shaped((block, columns), jnp.float32)] + [
        shaped((block * n, columns)) for n in (2, 2, 2, 1)
    ]


def weight_cuts_with_sums(width, columns):
    cuts = weight_cuts(width, columns)
    for k in (2, 3):
        if paired():
            cuts[k] = shaped((cuts[k].shape[0] + 2 * RIDERS, columns))
    return cuts + [shaped((2 * RIDERS, columns))]


def weight_grad_into(pairs, out_refs):
    places, start = [], 0
    for out_ref in out_refs:
        rows = out_ref.shape[0] // 128 * 128
        places.append((out_ref, start, start + rows))
        start += rows
    for first in range(0, start, 512):
        last, column = min(first + 512, start), 0
        for left_ref, right_ref in pairs:
            columns = slice(column, column + right_ref.shape[1])
            column += right_ref.shape[1]
            block = matmul_tn(left_ref[:, first:last], right_ref[...])
            for out_ref, low_row, high_row in places:
                begin, end = max(first, low_row), min(last, high_row)
                if begin < end:
                    out_ref[begin - low_row : end - low_row, columns] = block[
                        begin - first : end - first
                    ].astype(out_ref.dtype)


def scatter_first(cuts):
    if not paired():
        return cuts
    kept, far, far_beside, above, beside = cuts
    return kept, far, beside, swap(far_beside, "dp", 1), swap(above, "dp", 2)


def combine_kernel(with_sums, need, far_ref, far_in_ref, beside_ref, above_ref, *rest):
    *waiting, far_out, farther_out, beside_out = rest
    block = far_ref.shape[0] // 2
    need(0)
    need(1)
    farther_out[:block] = low(wide(far_ref[block:]) + wide(far_in_ref[block : 2 * block]))
    far_out[:block] = low(wide(far_ref[:block]) + wide(far_in_ref[:block]))
    need(2)
    need(3)
    beside_out[:block] = low(wide(beside_ref[...]) + wide(above_ref[:block]))
    sums, waiting = waiting[:with_sums], waiting[with_sums:]
    place = block
    for number, ref in enumerate(waiting):
        need(4 + with_sums + number)
        beside_out[place : place + block] = ref[...]
        place += block
    if with_sums:
        need(4)
        packed = pack(unpack(sums[0]) + unpack(far_in_ref[2 * block :]))
        far_out[block:] = packed
        farther_out[block:] = packed
        beside_out[place:] = above_ref[block:]


def scatter_second(state, marks, waiting=(), sums=(), us=QUICK):
    if not paired():
        return state, None, []
    kept, far, beside, far_in, above = state
    block, columns = kept.shape
    extra = 2 * RIDERS * len(sums)
    first = [part(above, 0, block)] + [part(above, 2 * block, extra)] * len(sums)
    far_out, farther_out, beside_out = kernel_call(
        partial(combine_kernel, len(sums)),
        [shaped((block + extra, columns))] * 2
        + [shaped((block * (1 + len(waiting)) + extra, columns))],
        pieces=[[far], [far_in], [beside], first, *[[x] for x in (*sums, *waiting)]],
        marks=marks,
        us=us,
        pinned=not sums,
    )
    arrived = [swap(farther_out, "dp", 6), swap(far_out, "dp", 4)]
    terms = [kept, part(above, block, block), *[part(x, 0, block) for x in arrived]]
    riders = [part(x, block, extra) for x in (far_out, *arrived)]
    return terms, beside_out, [*riders, part(above, 2 * block, extra)] if sums else []


def last_kernel(write, count, riders, need, *refs):
    total = None
    for number, ref in enumerate(refs[:count]):
        need(number)
        total = wide(ref[...]) if total is None else total + wide(ref[...])
    for number in range(riders):
        need(count + number)
    write(total, *refs[count:])


def scatter_last(state, write, out_shape, marks=(), riders=(), pinned=True):
    if not paired():
        state = [lax.psum_scatter(state[0], "dp", scatter_dimension=0, tiled=True)]
    return kernel_call(
        partial(last_kernel, write, len(state), len(riders)),
        out_shape,
        pieces=[[term] for term in [*state, *riders]],
        marks=marks,
        pinned=pinned,
    )


def to_slots(array_ref, rank, in_slots):
    if not in_slots:
        return array_ref[...]
    width = array_ref.shape[-1] // len(slot_offsets)
    return jnp.concatenate(
        [
            array_ref[:, pl.ds(pl.multiple_of((rank ^ o) * width, width), width)]
            for o in slot_offsets
        ],
        axis=1,
    )


def from_slots(value, rank, in_slots, out_ref):
    if not in_slots:
        out_ref[...] = value.astype(out_ref.dtype)
        return
    width = out_ref.shape[-1] // len(slot_offsets)
    for place, o in enumerate(slot_offsets):
        out_ref[:, pl.ds(pl.multiple_of((rank ^ o) * width, width), width)] = value[
            :, place * width : (place + 1) * width
        ].astype(out_ref.dtype)


def segments(lengths_ref, places):
    total = jnp.int32(0)
    found = jnp.zeros(places.shape, jnp.int32)
    for k in range(lengths_ref.shape[1]):
        total = total + lengths_ref[0, k]
        found = found + jnp.where(places >= total, 1, 0)
    return found


def prepare_kernel(need, query_ref, key_ref, value_ref, proj_ref, out_ref):
    width = query_ref.shape[1]
    for place, ref in enumerate((query_ref, key_ref, value_ref)):
        out_ref[:, place * width : (place + 1) * width] = ref[...]
    out_ref[:, 3 * width :] = proj_ref[...].T


def shards_kernel(need, attn_ref, inner_ref, outer_ref, out_ref):
    rows = attn_ref.shape[0]
    out_ref[:rows] = attn_ref[...]
    out_ref[rows : 2 * rows] = inner_ref[...]
    out_ref[2 * rows :] = outer_ref[...].T


def place_kernel(in_slots, need, ranks_ref, tokens_ref, grad_ref, small_ref, *out_refs):
    for ref, out_ref in zip((tokens_ref, grad_ref, small_ref), out_refs):
        out_ref[...] = to_slots(ref, ranks_ref[0], in_slots)


def pass_kernel(need, *refs):
    half = len(refs) // 2
    for number, (in_ref, out_ref) in enumerate(zip(refs[:half], refs[half:])):
        need(number)
        out_ref[...] = in_ref[...]


def back_into(left_ref, right_ref, inner, near_ref, far_ref):
    half = near_ref.shape[0]
    for start in range(0, near_ref.shape[1], 256):
        columns = slice(start, start + 256)
        total = matmul_nt(left_ref[...], right_ref[columns, inner])
        near_ref[:, columns] = total[:half]
        fars = far_ref if isinstance(far_ref, list) else [far_ref]
        rows = half // len(fars)
        for k, ref in enumerate(fars):
            ref[:, columns] = low(total[half + k * rows : half + (k + 1) * rows])


def attention_kernel(
    scale,
    need,
    ranks_ref,
    lengths_ref,
    key_ref,
    bias_ref,
    tokens_ref,
    weights_ref,
    qkv_ref,
    probs_ref,
    context_ref,
    fill_ref,
):
    rows = tokens_ref.shape[0]
    piece = rows // len(row_slots)
    head_width = context_ref.shape[1]
    rank = ranks_ref[1]
    down = lax.broadcasted_iota(jnp.int32, (rows, 1), 0)
    along = lax.broadcasted_iota(jnp.int32, (1, rows), 1)

    def places(index):
        slot, step = index // piece, index % piece
        owner = jnp.where(slot == 0, row_slots[0], 0)
        for k in range(1, len(row_slots)):
            owner = jnp.where(slot == k, row_slots[k], owner)
        return (owner ^ rank) * piece + step

    segment_down = segments(lengths_ref, places(down))
    segment_along = segments(lengths_ref, places(along))
    keys = jnp.concatenate([key_ref[pl.ds(rank ^ o, 1), :] for o in row_slots], axis=1)
    allowed = (segment_down == segment_along) & ((keys == 1) | (down == along))
    fill_ref[...] = jnp.where(allowed, 0.0, masked_fill)

    need(0)
    need(1)
    qkv = matmul(tokens_ref[...], weights_ref[:, : 3 * head_width]) + bias_ref[...]
    qkv_ref[:, :head_width] = low(qkv[:, :head_width] * scale)
    qkv_ref[:, head_width:] = low(qkv[:, head_width:])
    for head in range(head_width // HEAD_DIM):
        columns = [
            slice(part * head_width + head * HEAD_DIM, part * head_width + (head + 1) * HEAD_DIM)
            for part in range(3)
        ]
        query, key, value = (qkv_ref[:, c] for c in columns)
        scores = matmul_nt(query, key) + fill_ref[...]
        weights = jnp.exp(scores - jnp.max(scores, axis=1, keepdims=True))
        probs = low(weights * (1.0 / jnp.sum(weights, axis=1, keepdims=True)))
        probs_ref[head] = probs
        context_ref[:, columns[0]] = low(matmul(probs, value))


def project_kernel(need, context_ref, weights_ref, *refs):
    passed = len(refs) // 2 - 1
    near_ref, far_ref = refs[passed : passed + 2]
    for number, (in_ref, out_ref) in enumerate(zip(refs[:passed], refs[passed + 2 :])):
        need(2 + number)
        out_ref[...] = in_ref[...]
    need(0)
    need(1)
    back_into(context_ref, weights_ref, slice(None), near_ref, far_ref)


def first_norm_kernel(
    need,
    small_ref,
    near_ref,
    arrived_ref,
    across_ref,
    tokens_ref,
    first_ref,
    unit_ref,
    scale_ref,
    low_ref,
):
    need(3)
    total = (
        wide(tokens_ref[...])
        + own_sum(need, near_ref, arrived_ref, across_ref)
        + small_ref[0:1]
    )
    centred = total - jnp.mean(total, axis=1, keepdims=True)
    scale = lax.rsqrt(jnp.mean(centred * centred, axis=1, keepdims=True) + epsilon)
    unit = centred * scale
    first = unit * small_ref[1:2] + small_ref[2:3]
    unit_ref[...] = unit
    scale_ref[...] = scale
    first_ref[...] = first
    low_ref[...] = low(first)


def inner_kernel(need, bias_ref, rows_ref, weights_ref, active_ref, slope_ref):
    need(0)
    need(1)
    for start in range(0, active_ref.shape[1], 256):
        columns = slice(start, start + 256)
        hidden = matmul(rows_ref[...], weights_ref[:, columns]) + bias_ref[:, columns]
        share = 0.5 + 0.5 * lax.erf(hidden * (0.5**0.5))
        active_ref[:, columns] = low(hidden * share)
        slope_ref[:, columns] = share + hidden * jnp.exp(-0.5 * hidden * hidden) * (
            0.3989422804014327
        )


def outer_kernel(need, active_ref, weights_ref, near_ref, far_ref):
    need(0)
    need(1)
    back_into(active_ref, weights_ref, slice(None), near_ref, far_ref)


def second_norm_kernel(
    in_slots,
    need,
    ranks_ref,
    lengths_ref,
    small_ref,
    near_ref,
    arrived_ref,
    across_ref,
    first_ref,
    grad_ref,
    out_ref,
    second_grad_ref,
    low_ref,
    sums_ref,
):
    rows, _ = first_ref.shape
    need(3)
    need(4)
    total = first_ref[...] + own_sum(need, near_ref, arrived_ref, across_ref) + small_ref[3:4]
    centred = total - jnp.mean(total, axis=1, keepdims=True)
    scale = lax.rsqrt(jnp.mean(centred * centred, axis=1, keepdims=True) + epsilon)
    unit = centred * scale
    place = ranks_ref[1] * rows + lax.broadcasted_iota(jnp.int32, (rows, 1), 0)
    valid = jnp.where(segments(lengths_ref, place) < lengths_ref.shape[1], 1.0, 0.0)
    gain = small_ref[4:5]
    second = (unit * gain + small_ref[5:6]) * valid
    from_slots(second, ranks_ref[0], in_slots, out_ref)
    cot = wide(grad_ref[...]) * valid
    pulled = cot * gain
    second_grad = scale * (
        pulled
        - jnp.mean(pulled, axis=1, keepdims=True)
        - unit * jnp.mean(pulled * unit, axis=1, keepdims=True)
    )
    second_grad_ref[...] = second_grad
    rounded = low(second_grad)
    low_ref[...] = rounded
    sums_ref[0:1] = jnp.sum(wide(rounded), axis=0, keepdims=True)
    sums_ref[1:2] = jnp.sum(cot * unit, axis=0, keepdims=True)
    sums_ref[2:3] = jnp.sum(cot, axis=0, keepdims=True)
    sums_ref[3:8] = jnp.zeros_like(sums_ref[3:8])


def hidden_grad_kernel(
    need, rows_ref, outer_ref, slope_ref, inner_ref, hidden_grad_ref, near_ref, far_ref, sums_ref
):
    need(0)
    need(1)
    for start in range(0, hidden_grad_ref.shape[1], 256):
        columns = slice(start, start + 256)
        product = matmul(rows_ref[...], outer_ref[:, columns])
        if start == 0:
            need(2)
        grad = low(product * slope_ref[:, columns])
        hidden_grad_ref[:, columns] = grad
        sums_ref[0:1, columns] = jnp.sum(wide(grad), axis=0, keepdims=True)
    need(3)
    back_into(hidden_grad_ref, inner_ref, slice(None), near_ref, far_ref)


def single_grad_kernel(need, left_ref, right_ref, *out_refs):
    need(0)
    need(1)
    weight_grad_into([(left_ref, right_ref)], out_refs)


def first_back_kernel(
    in_slots,
    need,
    ranks_ref,
    scale_ref,
    small_ref,
    second_sums_ref,
    near_ref,
    arrived_ref,
    across_ref,
    second_grad_ref,
    unit_ref,
    mix_ref,
    low_ref,
    sums_ref,
):
    rows = mix_ref.shape[0]
    need(3)
    need(4)
    cot = second_grad_ref[...] + own_sum(need, near_ref, arrived_ref, across_ref)
    unit = unit_ref[...]
    pulled = cot * small_ref[1:2]
    mix = scale_ref[...] * (
        pulled
        - jnp.mean(pulled, axis=1, keepdims=True)
        - unit * jnp.mean(pulled * unit, axis=1, keepdims=True)
    )
    mix_ref[...] = mix
    rounded = low(mix)
    low_ref[:rows] = rounded
    sums = jnp.concatenate(
        [
            jnp.sum(wide(rounded), axis=0, keepdims=True),
            jnp.sum(cot * unit, axis=0, keepdims=True),
            jnp.sum(cot, axis=0, keepdims=True),
            second_sums_ref[0:3],
            jnp.zeros((2, mix.shape[1]), jnp.float32),
        ],
        axis=0,
    )
    from_slots(sums, ranks_ref[0], in_slots, sums_ref)
    low_ref[rows:] = pack(sums_ref[...])


def attention_back_kernel(
    scale,
    need,
    inner_sums_ref,
    rows_ref,
    weights_ref,
    qkv_ref,
    probs_ref,
    tokens_ref,
    context_ref,
    riders_ref,
    grads_ref,
    near_ref,
    far_ref,
    *rest,
):
    *cut_refs, context_grad_ref = rest
    head_width = context_grad_ref.shape[1]
    need(0)
    need(1)
    context_grad_ref[...] = low(matmul(rows_ref[...], weights_ref[:, 3 * head_width :]))
    need(2)
    need(3)
    for head in range(head_width // HEAD_DIM):
        columns = [
            slice(part * head_width + head * HEAD_DIM, part * head_width + (head + 1) * HEAD_DIM)
            for part in range(3)
        ]
        query, key, value = (qkv_ref[:, c] for c in columns)
        probs = probs_ref[head]
        context_grad = context_grad_ref[:, columns[0]]
        prob_grad = matmul_nt(context_grad, value)
        exact = wide(probs)
        product = prob_grad * exact
        score_grad = low(product - exact * jnp.sum(product, axis=1, keepdims=True))
        query_grad = low(matmul(score_grad, key)) * jnp.asarray(scale, jnp.bfloat16)
        key_grad = low(matmul_tn(score_grad, query))
        value_grad = low(matmul_tn(probs, context_grad))
        for place, grad in zip(columns, (query_grad, key_grad, value_grad)):
            grads_ref[:, place] = grad
    for number in range(4, 7):
        need(number)
    *cut_refs, packed_ref = cut_refs
    own, across, beside, corner = (
        unpack(riders_ref[k * 2 * RIDERS : (k + 1) * 2 * RIDERS]) for k in range(4)
    )
    sums = (own + across) + (beside + corner)
    mine = jnp.sum(wide(grads_ref[...]), axis=0, keepdims=True)
    mine = jnp.concatenate([mine, jnp.zeros((1, head_width), jnp.float32)], axis=1)
    packed = pack(jnp.concatenate([sums[: RIDERS - 2], inner_sums_ref[...], mine], axis=0))
    packed_ref[...] = packed
    for ref in cut_refs[2:4]:
        ref[ref.shape[0] - 2 * RIDERS :] = packed
    weight_grad_into([(tokens_ref, grads_ref), (rows_ref, context_ref)], cut_refs)
    back_into(grads_ref, weights_ref, slice(0, 3 * head_width), near_ref, far_ref)


def tokens_grad_kernel(
    in_slots, need, ranks_ref, near_ref, arrived_ref, across_ref, mix_ref, out_ref
):
    need(3)
    total = mix_ref[...] + own_sum(need, near_ref, arrived_ref, across_ref)
    from_slots(total, ranks_ref[0], in_slots, out_ref)


def write_turned(total, out_ref):
    out_ref[...] = total.T


def write_plain(total, out_ref):
    out_ref[...] = total


def write_attention(total, *refs):
    riders, refs = refs[: len(refs) - 13], refs[len(refs) - 13 :]
    query_ref, key_ref, value_ref, proj_ref, inner_sum_ref, query_sum_ref, value_sum_ref = refs[:7]
    width = query_ref.shape[1]
    for place, ref in enumerate((query_ref, key_ref, value_ref)):
        ref[...] = total[:, place * width : (place + 1) * width]
    proj_ref[...] = total[:, 3 * width :].T
    if len(riders) > 1:
        own, farther, far, above, beside = (unpack(ref) for ref in riders)
        above = unpack(pack(above + beside))
        sums = (own + above) + (far + farther)
    else:
        sums = unpack(riders[0])
    for k, ref in enumerate(refs[7:]):
        ref[...] = sums[k, :]
    inner_sum_ref[...] = sums[6, :]
    query_sum_ref[...] = sums[7, :width]
    value_sum_ref[...] = sums[7, 2 * width : 3 * width]


def on_device(
    tokens,
    key_mask,
    seq_lengths,
    w_query,
    b_query,
    w_key,
    w_value,
    b_value,
    w_proj,
    b_proj,
    gain_attn,
    shift_attn,
    w_inner,
    b_inner,
    w_outer,
    b_outer,
    gain_ffn,
    shift_ffn,
    out_grad,
):
    in_slots = paired()
    flag = seq_lengths[0, 0] >= 0
    ranks = jnp.stack([lax.axis_index("dp"), lax.axis_index("tensor")]).astype(jnp.int32)
    piece_rows, model_width = tokens.shape
    group_rows = piece_rows * lax.axis_size("tensor")
    half_rows = group_rows // 2
    shard_rows = w_query.shape[0]
    head_width = b_query.shape[0]
    heads = head_width // HEAD_DIM
    inner_width = b_inner.shape[0]
    scale = HEAD_DIM ** (-0.5)
    own = (piece_rows, model_width)
    partial_sums = [shaped((half_rows, model_width), jnp.float32), shaped((half_rows, model_width))]

    attn_shard = kernel_call(
        prepare_kernel,
        [shaped((shard_rows, 4 * head_width))],
        whole=[w_query, w_key, w_value, w_proj],
    )[0]
    shards = kernel_call(
        shards_kernel,
        [shaped((3 * shard_rows, 4 * head_width))],
        whole=[attn_shard, w_inner, w_outer],
    )[0]
    attn_beside, inner_beside, outer_beside = [], [], []
    if in_slots:
        beside = swap(shards, "dp", 1)
        attn_beside, inner_beside, outer_beside = (
            [part(beside, k * shard_rows, shard_rows)] for k in range(3)
        )
    attn_far = far_of(attn_shard)
    attn_above = above_of(attn_shard)
    small = jnp.stack(
        [b_proj, gain_attn, shift_attn, b_outer, gain_ffn, shift_ffn, b_proj, b_proj]
    )

    def tokens_in_part(tokens, out_grad, small):
        tokens, out_grad, small = kernel_call(
            partial(place_kernel, in_slots),
            [shaped(own), shaped(own), shaped(small.shape, jnp.float32)],
            whole=[tokens, out_grad, small],
            scalars=[ranks],
        )
        return tokens, out_grad, small, gather_rows(tokens)

    tokens, out_grad, small, token_rows = region(flag, tokens_in_part, tokens, out_grad, small)
    joined = [shaped((3 * shard_rows, model_width))] if in_slots else []
    inner_shard, *attn_joined = kernel_call(
        pass_kernel,
        [shaped(w_inner.shape), *joined],
        pieces=[[part(shards, shard_rows, shard_rows)]] + [attn_far + attn_above] * in_slots,
        marks=[tokens],
    )
    attn_weights = weight_pieces(
        attn_shard, attn_far, rest_of(attn_joined), attn_above, attn_beside
    )
    inner_far = far_of(inner_shard)
    inner_above = above_of(inner_shard)
    outer_corner = above_of(beside[2 * shard_rows :]) if in_slots else []
    qkv_bias = jnp.concatenate([b_query, jnp.zeros_like(b_query), b_value])[None, :]
    qkv, probs, context = kernel_call(
        partial(attention_kernel, scale),
        [
            shaped((group_rows, 3 * head_width)),
            shaped((heads, group_rows, group_rows)),
            shaped((group_rows, head_width)),
        ],
        scalars=[ranks, seq_lengths],
        whole=[key_mask.reshape(lax.axis_size("tensor"), piece_rows), qkv_bias],
        pieces=[token_rows, attn_weights],
        marks=[inner_shard],
        scratch=[pltpu.VMEM((group_rows, group_rows), jnp.float32)],
    )
    proj_columns = (3 * head_width, head_width)
    proj_weights = [
        part(*p[:3], proj_columns) if isinstance(p, tuple) else part(p, 0, p.shape[0], proj_columns)
        for p in attn_weights
    ]
    near, far, outer_shard, *inner_joined = kernel_call(
        project_kernel,
        [*partial_sums, shaped(inner_shard.shape), *joined],
        pieces=[[context], proj_weights, [part(shards, 2 * shard_rows, shard_rows)]]
        + [inner_far + inner_above] * in_slots,
        marks=outer_corner,
    )
    inner_weights = weight_pieces(
        inner_shard, inner_far, rest_of(inner_joined), inner_above, inner_beside
    )
    outer_far = far_of(outer_shard)
    def first_part(near, far, tokens, small):
        terms = scatter_rows(near, far)
        return kernel_call(
            first_norm_kernel,
            [
                shaped(own, jnp.float32),
                shaped(own, jnp.float32),
                shaped((piece_rows, 1), jnp.float32),
                shaped(own),
            ],
            whole=[small],
            pieces=[*terms, [tokens]],
        )

    first, unit, unit_scale, first_low = region(flag, first_part, near, far, tokens, small)
    *outer_far, outer_shard = tie([*outer_far, outer_shard], [first_low])
    outer_weights = weight_pieces(
        outer_shard,
        outer_far,
        rest_of(outer_far),
        outer_corner + above_of(outer_shard),
        outer_beside,
    )

    def inner_part(first_low, arrived, marks):
        norm_rows = gather_rows(first_low, joined=False)
        return norm_rows[1:], kernel_call(
            inner_kernel,
            [shaped((group_rows, inner_width)), shaped((group_rows, inner_width), jnp.float32)],
            whole=[b_inner[None, :]],
            pieces=[norm_rows, arrived + inner_beside],
            marks=marks,
        )

    other_rows, (active, slope) = region(
        flag,
        inner_part,
        first_low,
        inner_weights[: len(inner_weights) - len(inner_beside)],
        [],
    )
    norm_rows = [first_low, *other_rows]
    near, far = kernel_call(
        outer_kernel, partial_sums, pieces=[[active], outer_weights]
    )
    terms = scatter_rows(near, far)
    layer_out, second_grad, branch_grad, second_sums = kernel_call(
        partial(second_norm_kernel, in_slots),
        [
            shaped(own),
            shaped(own, jnp.float32),
            shaped(own),
            shaped((8, model_width), jnp.float32),
        ],
        scalars=[ranks, seq_lengths],
        whole=[small],
        pieces=[*terms, [first], [out_grad]],
    )

    branch_rows = gather_rows(branch_grad, joined=False)
    outer_cuts = kernel_call(
        single_grad_kernel,
        weight_cuts(model_width, inner_width),
        pieces=[branch_rows, [active]],
    )
    outer_state = scatter_first(outer_cuts)
    hidden_grad, near, far, inner_sums = kernel_call(
        hidden_grad_kernel,
        [
            shaped((group_rows, inner_width)),
            partial_sums[0],
            [shaped(own)] * 2,
            shaped((1, inner_width), jnp.float32),
        ],
        pieces=[branch_rows, outer_weights, [slope], inner_weights],
        marks=[outer_cuts[0]],
    )

    terms = scatter_rows(near, far)
    inner_cuts = kernel_call(
        single_grad_kernel,
        weight_cuts(model_width, inner_width),
        pieces=[norm_rows, [hidden_grad]],
        marks=terms[1],
    )
    outer_terms, outer_beside, _ = scatter_second(outer_state, [inner_cuts[0]])
    outer_mark = [outer_beside] if in_slots else []
    mix_grad, proj_grad = kernel_call(
        partial(first_back_kernel, in_slots),
        [shaped(own, jnp.float32), shaped((piece_rows + 2 * RIDERS, model_width))],
        scalars=[ranks],
        whole=[unit_scale, small, second_sums],
        pieces=[
            *terms,
            [second_grad],
            [unit],
        ],
        scratch=[pltpu.VMEM((RIDERS, model_width), jnp.float32)],
        us=4 * SLOW,
    )
    inner_state = scatter_first(inner_cuts)

    def row_parts(gathered, first, rows):
        whole = gathered[0].shape[0] // 2
        return [part(g, k * whole + first, rows) for g in gathered for k in range(2)]

    def attention_back_part(proj_grad, marks):
        gathered = gather_rows(proj_grad)
        return kernel_call(
            partial(attention_back_kernel, scale),
            [
                shaped((group_rows, 3 * head_width)),
                *partial_sums,
                *weight_cuts_with_sums(model_width, 4 * head_width),
            ],
            whole=[inner_sums],
            pieces=[
                row_parts(gathered, 0, piece_rows),
                attn_weights,
                [qkv],
                [probs],
                token_rows,
                [context],
                row_parts(gathered, piece_rows, 2 * RIDERS),
            ],
            marks=marks,
            scratch=[pltpu.VMEM((group_rows, head_width), jnp.bfloat16)],
        )[1:]

    near, far, *attn_cuts, sums = region(flag, attention_back_part, proj_grad, outer_mark)
    attn_state = scatter_first(attn_cuts)
    inner_terms, inner_beside, _ = scatter_second(
        inner_state, [attn_state[0], *[t[0] for t in outer_terms[2:]]], us=8 * SLOW
    )

    def tokens_part(near, far, mix_grad, mark):
        terms = scatter_rows(near, far)
        return kernel_call(
            partial(tokens_grad_kernel, in_slots),
            [shaped(own, jnp.float32)],
            scalars=[ranks],
            pieces=[*terms, [mix_grad]],
            marks=[mark],
        )[0]

    tokens_grad = region(flag, tokens_part, near, far, mix_grad, attn_state[0])
    waiting = [outer_beside, inner_beside] if in_slots else []
    attn_terms, beside, riders = scatter_second(
        attn_state, [tokens_grad, *[t[0] for t in inner_terms[2:]]], waiting, [sums] * in_slots
    )
    besides = [[]] * 3
    if in_slots:
        besides = swap(beside, "dp", 1)
        riders.append(part(besides, 3 * shard_rows, 2 * RIDERS))
        besides = [[part(besides, k * shard_rows, shard_rows)] for k in range(3)]
    else:
        riders = [pack(lax.psum(unpack(sums), "dp"))]
    dw_outer = scatter_last(
        outer_terms + besides[1], write_turned, [shaped(w_outer.shape, jnp.float32)]
    )[0]
    dw_inner = scatter_last(
        inner_terms + besides[2], write_plain, [shaped(w_inner.shape, jnp.float32)]
    )[0]
    dw_query, dw_key, dw_value, dw_proj, db_inner, db_query, db_value, *shared = scatter_last(
        attn_terms + besides[0],
        write_attention,
        [shaped(w.shape, jnp.float32) for w in (w_query, w_key, w_value, w_proj)]
        + [shaped(b.shape, jnp.float32) for b in (b_inner, b_query, b_value)]
        + [shaped((model_width,), jnp.float32)] * 6,
        [dw_outer, dw_inner],
        riders,
        False,
    )
    db_proj, dgain_attn, dshift_attn, db_outer, dgain_ffn, dshift_ffn = shared
    return (
        layer_out,
        tokens_grad,
        dw_query,
        db_query,
        dw_key,
        dw_value,
        db_value,
        dw_proj,
        db_proj,
        dgain_attn,
        dshift_attn,
        dw_inner,
        db_inner,
        dw_outer,
        db_outer,
        dgain_ffn,
        dshift_ffn,
    )


def solution(mesh):
    in_specs = (
        P(("dp", "tensor"), None),
        P("dp"),
        P("dp", None),
        P("dp", "tensor"),
        P("tensor"),
        P("dp", "tensor"),
        P("dp", "tensor"),
        P("tensor"),
        P("tensor", "dp"),
        P(),
        P(),
        P(),
        P("dp", "tensor"),
        P("tensor"),
        P("tensor", "dp"),
        P(),
        P(),
        P(),
        P(("dp", "tensor"), None),
    )
    out_specs = (
        P(("dp", "tensor"), None),
        P(("dp", "tensor"), None),
        P("dp", "tensor"),
        P("tensor"),
        P("dp", "tensor"),
        P("dp", "tensor"),
        P("tensor"),
        P("tensor", "dp"),
        P(),
        P(),
        P(),
        P("dp", "tensor"),
        P("tensor"),
        P("tensor", "dp"),
        P(),
        P(),
        P(),
    )
    return jax.shard_map(
        on_device, mesh=mesh, in_specs=in_specs, out_specs=out_specs, check_vma=False
    )
```

```python
from functools import partial

import jax
import jax.numpy as jnp
from jax import lax
from jax.experimental import pallas as pl
from jax.experimental.pallas import tpu as pltpu
from jax.sharding import PartitionSpec as P

HEAD_DIM = 64


epsilon = 1e-12
masked_fill = -1e30

row_slots = (0, 2, 1, 3)
slot_offsets = (0, 4, 6, 5, 7, 3, 2, 1)


def matmul(left_side, right_side):
    return jnp.dot(left_side, right_side, preferred_element_type=jnp.float32)


def matmul_nt(left_side, right_side):
    return lax.dot_general(
        left_side, right_side, (((1,), (1,)), ((), ())), preferred_element_type=jnp.float32
    )


def matmul_tn(left_side, right_side):
    return lax.dot_general(
        left_side, right_side, (((0,), (0,)), ((), ())), preferred_element_type=jnp.float32
    )


def low(value):
    return value.astype(jnp.bfloat16)


def wide(value):
    return value.astype(jnp.float32)


VMEM_LIMIT = 63 << 20
QUICK, SLOW = 0.01, 2


def shaped(shape, dtype=jnp.bfloat16):
    return jax.ShapeDtypeStruct(shape, dtype)


def paired():
    return lax.axis_size("dp") == len(slot_offsets)


def swap(block, axis_name, offset):
    count = lax.axis_size(axis_name)
    return lax.ppermute(block, axis_name, [(i, i ^ offset) for i in range(count)])


def part(array, start, rows, columns=None):
    return array, start, rows, columns


def kernel_call(body, out_shape, whole=(), pieces=(), scalars=(), marks=(), scratch=(), us=QUICK, pinned=True):
    pieces = [
        [p if isinstance(p, tuple) else part(p, 0, p.shape[0]) for p in some] for some in pieces
    ]
    buffers = [
        pltpu.VMEM(
            (sum(p[2] for p in some), *((some[0][3][1],) if some[0][3] else some[0][0].shape[1:])),
            some[0][0].dtype,
        )
        for some in pieces
    ]
    flat = [p for some in pieces for p in some]
    flat_out, tree = jax.tree.flatten(list(out_shape))
    counts = (len(scalars), len(whole), len(flat), len(marks), len(flat_out), len(buffers))

    def run(*refs):
        groups, start = [], 0
        for count in counts:
            groups.append(refs[start : start + count])
            start += count
        scalar_refs, whole_refs, piece_refs, _, out_refs, buffer_refs = groups
        rest = refs[start:]
        copies = []
        if flat:
            done, rest = rest[0], rest[1:]
            k = 0
            for some, buffer in zip(pieces, buffer_refs):
                row, mine = 0, []
                for _, first, rows, columns in some:
                    place = (pl.ds(first, rows), pl.ds(*columns)) if columns else pl.ds(first, rows)
                    mine.append(
                        pltpu.make_async_copy(
                            piece_refs[k].at[place],
                            buffer.at[pl.ds(row, rows)],
                            done.at[k],
                        )
                    )
                    row += rows
                    k += 1
                copies.append(mine)
            for copy in (c for mine in copies for c in mine):
                copy.start()

        def need(number):
            for copy in copies[number]:
                copy.wait()

        outs = jax.tree.unflatten(tree, out_refs)
        body(need, *scalar_refs, *whole_refs, *buffer_refs, *outs, *rest)

    anywhere = pl.BlockSpec(memory_space=pl.ANY)
    inside = pl.BlockSpec(memory_space=pltpu.VMEM)
    semaphores = [pltpu.SemaphoreType.DMA((len(flat),))] if flat else []
    results = pl.pallas_call(
        run,
        out_shape=flat_out,
        in_specs=[pl.BlockSpec(memory_space=pltpu.SMEM)] * len(scalars)
        + [inside] * len(whole)
        + [pl.BlockSpec(memory_space=pltpu.HBM) if pinned else anywhere] * len(flat)
        + [anywhere] * len(marks),
        out_specs=[inside] * len(flat_out),
        scratch_shapes=buffers + semaphores + list(scratch),
        compiler_params=pltpu.CompilerParams(vmem_limit_bytes=VMEM_LIMIT),
        cost_estimate=pl.CostEstimate(
            flops=int(us * 1.1e9), bytes_accessed=int(us * 3.5e6), transcendentals=0
        ),
    )(*scalars, *whole, *[p[0] for p in flat], *marks)
    return jax.tree.unflatten(tree, results)


def tie(blocks, marks):
    pinned = pl.BlockSpec(memory_space=pltpu.HBM)
    return pl.pallas_call(
        lambda *refs: None,
        out_shape=[shaped(b.shape, b.dtype) for b in blocks],
        in_specs=[pinned] * len(blocks) + [pl.BlockSpec(memory_space=pl.ANY)] * len(marks),
        out_specs=[pinned] * len(blocks),
        input_output_aliases={k: k for k in range(len(blocks))},
        cost_estimate=pl.CostEstimate(flops=0, bytes_accessed=0, transcendentals=0),
    )(*blocks, *marks)


def region(flag, body, *operands):
    def nothing(*some):
        return jax.tree.map(lambda x: jnp.zeros(x.shape, x.dtype), jax.eval_shape(body, *operands))

    return lax.cond(flag, body, nothing, *operands)


RIDERS = 8


def pack(value):
    high = wide(low(value))
    return low(jnp.concatenate([high, value - high], axis=0))


def unpack(packed):
    value = wide(packed[...])
    return value[:RIDERS] + value[RIDERS:]


def join_kernel(need, own_ref, across_ref, out_ref):
    rows = own_ref.shape[0]
    need(0)
    out_ref[:rows] = own_ref[...]
    need(1)
    out_ref[rows:] = across_ref[...]


def gather_rows(piece, joined=True):
    across = swap(piece, "tensor", 2)
    if not joined:
        return [piece, across, swap(piece, "tensor", 1), swap(across, "tensor", 1)]
    rows, columns = piece.shape
    pair = kernel_call(join_kernel, [shaped((2 * rows, columns))], pieces=[[piece], [across]])[0]
    return [pair, swap(pair, "tensor", 1)]


def turn_kernel(need, near_ref, arrived_ref, out_ref):
    need(0)
    need(1)
    out_ref[...] = low(near_ref[...] + wide(arrived_ref[...]))


def scatter_rows(near, far):
    half = near.shape[0] // 2
    if isinstance(far, list):
        beside, corner = (swap(f, "tensor", 1) for f in far)
        turned = kernel_call(
            turn_kernel, [shaped(corner.shape)], pieces=[[part(near, half, half)], [corner]]
        )[0]
    else:
        arrived = swap(far, "tensor", 1)
        beside = part(arrived, 0, half)
        turned = low(near[half:] + wide(arrived[half:]))
    return [[part(near, 0, half)], [beside], [swap(turned, "tensor", 2)]]


def own_sum(need, near_ref, arrived_ref, across_ref):
    for number in range(3):
        need(number)
    return near_ref[...] + wide(arrived_ref[...]) + wide(across_ref[...])


def far_of(shard):
    return [swap(shard, "dp", 4), swap(shard, "dp", 6)] if paired() else []


def above_of(shard):
    return [swap(shard, "dp", 2)] if paired() else []


def rest_of(pieces):
    return [swap(p, "dp", 1) for p in pieces]


def weight_pieces(shard, far, rest, above, beside):
    if not paired():
        return [lax.all_gather(shard, "dp", axis=0, tiled=True)]
    return [shard, *far, *rest, *above, *beside]


def weight_cuts(width, columns):
    if not paired():
        return [shaped((width, columns), jnp.float32)]
    block = width // len(slot_offsets)
    return [shaped((block, columns), jnp.float32)] + [
        shaped((block * n, columns)) for n in (2, 2, 2, 1)
    ]


def weight_cuts_with_sums(width, columns):
    cuts = weight_cuts(width, columns)
    for k in (2, 3):
        if paired():
            cuts[k] = shaped((cuts[k].shape[0] + 2 * RIDERS, columns))
    return cuts + [shaped((2 * RIDERS, columns))]


def weight_grad_into(pairs, out_refs):
    places, start = [], 0
    for out_ref in out_refs:
        rows = out_ref.shape[0] // 128 * 128
        places.append((out_ref, start, start + rows))
        start += rows
    for first in range(0, start, 512):
        last, column = min(first + 512, start), 0
        for left_ref, right_ref in pairs:
            columns = slice(column, column + right_ref.shape[1])
            column += right_ref.shape[1]
            block = matmul_tn(left_ref[:, first:last], right_ref[...])
            for out_ref, low_row, high_row in places:
                begin, end = max(first, low_row), min(last, high_row)
                if begin < end:
                    out_ref[begin - low_row : end - low_row, columns] = block[
                        begin - first : end - first
                    ].astype(out_ref.dtype)


def scatter_first(cuts):
    if not paired():
        return cuts
    kept, far, far_beside, above, beside = cuts
    return kept, far, beside, swap(far_beside, "dp", 1), swap(above, "dp", 2)


def combine_kernel(with_sums, need, far_ref, far_in_ref, beside_ref, above_ref, *rest):
    *waiting, far_out, farther_out, beside_out = rest
    block = far_ref.shape[0] // 2
    need(0)
    need(1)
    farther_out[:block] = low(wide(far_ref[block:]) + wide(far_in_ref[block : 2 * block]))
    far_out[:block] = low(wide(far_ref[:block]) + wide(far_in_ref[:block]))
    need(2)
    need(3)
    beside_out[:block] = low(wide(beside_ref[...]) + wide(above_ref[:block]))
    sums, waiting = waiting[:with_sums], waiting[with_sums:]
    place = block
    for number, ref in enumerate(waiting):
        need(4 + with_sums + number)
        beside_out[place : place + block] = ref[...]
        place += block
    if with_sums:
        need(4)
        packed = pack(unpack(sums[0]) + unpack(far_in_ref[2 * block :]))
        far_out[block:] = packed
        farther_out[block:] = packed
        beside_out[place:] = above_ref[block:]


def scatter_second(state, marks, waiting=(), sums=(), us=QUICK):
    if not paired():
        return state, None, []
    kept, far, beside, far_in, above = state
    block, columns = kept.shape
    extra = 2 * RIDERS * len(sums)
    first = [part(above, 0, block)] + [part(above, 2 * block, extra)] * len(sums)
    far_out, farther_out, beside_out = kernel_call(
        partial(combine_kernel, len(sums)),
        [shaped((block + extra, columns))] * 2
        + [shaped((block * (1 + len(waiting)) + extra, columns))],
        pieces=[[far], [far_in], [beside], first, *[[x] for x in (*sums, *waiting)]],
        marks=marks,
        us=us,
        pinned=not sums,
    )
    arrived = [swap(farther_out, "dp", 6), swap(far_out, "dp", 4)]
    terms = [kept, part(above, block, block), *[part(x, 0, block) for x in arrived]]
    riders = [part(x, block, extra) for x in (far_out, *arrived)]
    return terms, beside_out, [*riders, part(above, 2 * block, extra)] if sums else []


def last_kernel(write, count, riders, need, *refs):
    total = None
    for number, ref in enumerate(refs[:count]):
        need(number)
        total = wide(ref[...]) if total is None else total + wide(ref[...])
    for number in range(riders):
        need(count + number)
    write(total, *refs[count:])


def scatter_last(state, write, out_shape, marks=(), riders=(), pinned=True):
    if not paired():
        state = [lax.psum_scatter(state[0], "dp", scatter_dimension=0, tiled=True)]
    return kernel_call(
        partial(last_kernel, write, len(state), len(riders)),
        out_shape,
        pieces=[[term] for term in [*state, *riders]],
        marks=marks,
        pinned=pinned,
    )


def to_slots(array_ref, rank, in_slots):
    if not in_slots:
        return array_ref[...]
    width = array_ref.shape[-1] // len(slot_offsets)
    return jnp.concatenate(
        [
            array_ref[:, pl.ds(pl.multiple_of((rank ^ o) * width, width), width)]
            for o in slot_offsets
        ],
        axis=1,
    )


def from_slots(value, rank, in_slots, out_ref):
    if not in_slots:
        out_ref[...] = value.astype(out_ref.dtype)
        return
    width = out_ref.shape[-1] // len(slot_offsets)
    for place, o in enumerate(slot_offsets):
        out_ref[:, pl.ds(pl.multiple_of((rank ^ o) * width, width), width)] = value[
            :, place * width : (place + 1) * width
        ].astype(out_ref.dtype)


def segments(lengths_ref, places):
    total = jnp.int32(0)
    found = jnp.zeros(places.shape, jnp.int32)
    for k in range(lengths_ref.shape[1]):
        total = total + lengths_ref[0, k]
        found = found + jnp.where(places >= total, 1, 0)
    return found


def prepare_kernel(need, query_ref, key_ref, value_ref, proj_ref, out_ref):
    width = query_ref.shape[1]
    for place, ref in enumerate((query_ref, key_ref, value_ref)):
        out_ref[:, place * width : (place + 1) * width] = ref[...]
    out_ref[:, 3 * width :] = proj_ref[...].T


def shards_kernel(need, attn_ref, inner_ref, outer_ref, out_ref):
    rows = attn_ref.shape[0]
    out_ref[:rows] = attn_ref[...]
    out_ref[rows : 2 * rows] = inner_ref[...]
    out_ref[2 * rows :] = outer_ref[...].T


def place_kernel(in_slots, need, ranks_ref, tokens_ref, grad_ref, small_ref, *out_refs):
    for ref, out_ref in zip((tokens_ref, grad_ref, small_ref), out_refs):
        out_ref[...] = to_slots(ref, ranks_ref[0], in_slots)


def pass_kernel(need, *refs):
    half = len(refs) // 2
    for number, (in_ref, out_ref) in enumerate(zip(refs[:half], refs[half:])):
        need(number)
        out_ref[...] = in_ref[...]


def back_into(left_ref, right_ref, inner, near_ref, far_ref):
    half = near_ref.shape[0]
    for start in range(0, near_ref.shape[1], 256):
        columns = slice(start, start + 256)
        total = matmul_nt(left_ref[...], right_ref[columns, inner])
        near_ref[:, columns] = total[:half]
        fars = far_ref if isinstance(far_ref, list) else [far_ref]
        rows = half // len(fars)
        for k, ref in enumerate(fars):
            ref[:, columns] = low(total[half + k * rows : half + (k + 1) * rows])


def attention_kernel(
    scale,
    need,
    ranks_ref,
    lengths_ref,
    key_ref,
    bias_ref,
    tokens_ref,
    weights_ref,
    qkv_ref,
    probs_ref,
    context_ref,
    fill_ref,
):
    rows = tokens_ref.shape[0]
    piece = rows // len(row_slots)
    head_width = context_ref.shape[1]
    rank = ranks_ref[1]
    down = lax.broadcasted_iota(jnp.int32, (rows, 1), 0)
    along = lax.broadcasted_iota(jnp.int32, (1, rows), 1)

    def places(index):
        slot, step = index // piece, index % piece
        owner = jnp.where(slot == 0, row_slots[0], 0)
        for k in range(1, len(row_slots)):
            owner = jnp.where(slot == k, row_slots[k], owner)
        return (owner ^ rank) * piece + step

    segment_down = segments(lengths_ref, places(down))
    segment_along = segments(lengths_ref, places(along))
    keys = jnp.concatenate([key_ref[pl.ds(rank ^ o, 1), :] for o in row_slots], axis=1)
    allowed = (segment_down == segment_along) & ((keys == 1) | (down == along))
    fill_ref[...] = jnp.where(allowed, 0.0, masked_fill)

    need(0)
    need(1)
    qkv = matmul(tokens_ref[...], weights_ref[:, : 3 * head_width]) + bias_ref[...]
    qkv_ref[:, :head_width] = low(qkv[:, :head_width] * scale)
    qkv_ref[:, head_width:] = low(qkv[:, head_width:])
    for head in range(head_width // HEAD_DIM):
        columns = [
            slice(part * head_width + head * HEAD_DIM, part * head_width + (head + 1) * HEAD_DIM)
            for part in range(3)
        ]
        query, key, value = (qkv_ref[:, c] for c in columns)
        scores = matmul_nt(query, key) + fill_ref[...]
        weights = jnp.exp(scores - jnp.max(scores, axis=1, keepdims=True))
        probs = low(weights * (1.0 / jnp.sum(weights, axis=1, keepdims=True)))
        probs_ref[head] = probs
        context_ref[:, columns[0]] = low(matmul(probs, value))


def project_kernel(need, context_ref, weights_ref, *refs):
    passed = len(refs) // 2 - 1
    near_ref, far_ref = refs[passed : passed + 2]
    for number, (in_ref, out_ref) in enumerate(zip(refs[:passed], refs[passed + 2 :])):
        need(2 + number)
        out_ref[...] = in_ref[...]
    need(0)
    need(1)
    back_into(context_ref, weights_ref, slice(None), near_ref, far_ref)


def first_norm_kernel(
    need,
    small_ref,
    near_ref,
    arrived_ref,
    across_ref,
    tokens_ref,
    first_ref,
    unit_ref,
    scale_ref,
    low_ref,
):
    need(3)
    total = (
        wide(tokens_ref[...])
        + own_sum(need, near_ref, arrived_ref, across_ref)
        + small_ref[0:1]
    )
    centred = total - jnp.mean(total, axis=1, keepdims=True)
    scale = lax.rsqrt(jnp.mean(centred * centred, axis=1, keepdims=True) + epsilon)
    unit = centred * scale
    first = unit * small_ref[1:2] + small_ref[2:3]
    unit_ref[...] = unit
    scale_ref[...] = scale
    first_ref[...] = first
    low_ref[...] = low(first)


def inner_kernel(need, bias_ref, rows_ref, weights_ref, active_ref, slope_ref):
    need(0)
    need(1)
    for start in range(0, active_ref.shape[1], 256):
        columns = slice(start, start + 256)
        hidden = matmul(rows_ref[...], weights_ref[:, columns]) + bias_ref[:, columns]
        share = 0.5 + 0.5 * lax.erf(hidden * (0.5**0.5))
        active_ref[:, columns] = low(hidden * share)
        slope_ref[:, columns] = share + hidden * jnp.exp(-0.5 * hidden * hidden) * (
            0.3989422804014327
        )


def outer_kernel(need, active_ref, weights_ref, near_ref, far_ref):
    need(0)
    need(1)
    back_into(active_ref, weights_ref, slice(None), near_ref, far_ref)


def second_norm_kernel(
    in_slots,
    need,
    ranks_ref,
    lengths_ref,
    small_ref,
    near_ref,
    arrived_ref,
    across_ref,
    first_ref,
    grad_ref,
    out_ref,
    second_grad_ref,
    low_ref,
    sums_ref,
):
    rows, _ = first_ref.shape
    need(3)
    need(4)
    total = first_ref[...] + own_sum(need, near_ref, arrived_ref, across_ref) + small_ref[3:4]
    centred = total - jnp.mean(total, axis=1, keepdims=True)
    scale = lax.rsqrt(jnp.mean(centred * centred, axis=1, keepdims=True) + epsilon)
    unit = centred * scale
    place = ranks_ref[1] * rows + lax.broadcasted_iota(jnp.int32, (rows, 1), 0)
    valid = jnp.where(segments(lengths_ref, place) < lengths_ref.shape[1], 1.0, 0.0)
    gain = small_ref[4:5]
    second = (unit * gain + small_ref[5:6]) * valid
    from_slots(second, ranks_ref[0], in_slots, out_ref)
    cot = wide(grad_ref[...]) * valid
    pulled = cot * gain
    second_grad = scale * (
        pulled
        - jnp.mean(pulled, axis=1, keepdims=True)
        - unit * jnp.mean(pulled * unit, axis=1, keepdims=True)
    )
    second_grad_ref[...] = second_grad
    rounded = low(second_grad)
    low_ref[...] = rounded
    sums_ref[0:1] = jnp.sum(wide(rounded), axis=0, keepdims=True)
    sums_ref[1:2] = jnp.sum(cot * unit, axis=0, keepdims=True)
    sums_ref[2:3] = jnp.sum(cot, axis=0, keepdims=True)
    sums_ref[3:8] = jnp.zeros_like(sums_ref[3:8])


def hidden_grad_kernel(
    need, rows_ref, outer_ref, slope_ref, inner_ref, hidden_grad_ref, near_ref, far_ref, sums_ref
):
    need(0)
    need(1)
    for start in range(0, hidden_grad_ref.shape[1], 256):
        columns = slice(start, start + 256)
        product = matmul(rows_ref[...], outer_ref[:, columns])
        if start == 0:
            need(2)
        grad = low(product * slope_ref[:, columns])
        hidden_grad_ref[:, columns] = grad
        sums_ref[0:1, columns] = jnp.sum(wide(grad), axis=0, keepdims=True)
    need(3)
    back_into(hidden_grad_ref, inner_ref, slice(None), near_ref, far_ref)


def single_grad_kernel(need, left_ref, right_ref, *out_refs):
    need(0)
    need(1)
    weight_grad_into([(left_ref, right_ref)], out_refs)


def first_back_kernel(
    in_slots,
    need,
    ranks_ref,
    scale_ref,
    small_ref,
    second_sums_ref,
    near_ref,
    arrived_ref,
    across_ref,
    second_grad_ref,
    unit_ref,
    mix_ref,
    low_ref,
    sums_ref,
):
    rows = mix_ref.shape[0]
    need(3)
    need(4)
    cot = second_grad_ref[...] + own_sum(need, near_ref, arrived_ref, across_ref)
    unit = unit_ref[...]
    pulled = cot * small_ref[1:2]
    mix = scale_ref[...] * (
        pulled
        - jnp.mean(pulled, axis=1, keepdims=True)
        - unit * jnp.mean(pulled * unit, axis=1, keepdims=True)
    )
    mix_ref[...] = mix
    rounded = low(mix)
    low_ref[:rows] = rounded
    sums = jnp.concatenate(
        [
            jnp.sum(wide(rounded), axis=0, keepdims=True),
            jnp.sum(cot * unit, axis=0, keepdims=True),
            jnp.sum(cot, axis=0, keepdims=True),
            second_sums_ref[0:3],
            jnp.zeros((2, mix.shape[1]), jnp.float32),
        ],
        axis=0,
    )
    from_slots(sums, ranks_ref[0], in_slots, sums_ref)
    low_ref[rows:] = pack(sums_ref[...])


def attention_back_kernel(
    scale,
    need,
    inner_sums_ref,
    rows_ref,
    weights_ref,
    qkv_ref,
    probs_ref,
    tokens_ref,
    context_ref,
    riders_ref,
    grads_ref,
    near_ref,
    far_ref,
    *rest,
):
    *cut_refs, context_grad_ref = rest
    head_width = context_grad_ref.shape[1]
    need(0)
    need(1)
    context_grad_ref[...] = low(matmul(rows_ref[...], weights_ref[:, 3 * head_width :]))
    need(2)
    need(3)
    for head in range(head_width // HEAD_DIM):
        columns = [
            slice(part * head_width + head * HEAD_DIM, part * head_width + (head + 1) * HEAD_DIM)
            for part in range(3)
        ]
        query, key, value = (qkv_ref[:, c] for c in columns)
        probs = probs_ref[head]
        context_grad = context_grad_ref[:, columns[0]]
        prob_grad = matmul_nt(context_grad, value)
        exact = wide(probs)
        product = prob_grad * exact
        score_grad = low(product - exact * jnp.sum(product, axis=1, keepdims=True))
        query_grad = low(matmul(score_grad, key)) * jnp.asarray(scale, jnp.bfloat16)
        key_grad = low(matmul_tn(score_grad, query))
        value_grad = low(matmul_tn(probs, context_grad))
        for place, grad in zip(columns, (query_grad, key_grad, value_grad)):
            grads_ref[:, place] = grad
    for number in range(4, 7):
        need(number)
    *cut_refs, packed_ref = cut_refs
    own, across, beside, corner = (
        unpack(riders_ref[k * 2 * RIDERS : (k + 1) * 2 * RIDERS]) for k in range(4)
    )
    sums = (own + across) + (beside + corner)
    mine = jnp.sum(wide(grads_ref[...]), axis=0, keepdims=True)
    mine = jnp.concatenate([mine, jnp.zeros((1, head_width), jnp.float32)], axis=1)
    packed = pack(jnp.concatenate([sums[: RIDERS - 2], inner_sums_ref[...], mine], axis=0))
    packed_ref[...] = packed
    for ref in cut_refs[2:4]:
        ref[ref.shape[0] - 2 * RIDERS :] = packed
    weight_grad_into([(tokens_ref, grads_ref), (rows_ref, context_ref)], cut_refs)
    back_into(grads_ref, weights_ref, slice(0, 3 * head_width), near_ref, far_ref)


def tokens_grad_kernel(
    in_slots, need, ranks_ref, near_ref, arrived_ref, across_ref, mix_ref, out_ref
):
    need(3)
    total = mix_ref[...] + own_sum(need, near_ref, arrived_ref, across_ref)
    from_slots(total, ranks_ref[0], in_slots, out_ref)


def write_turned(total, out_ref):
    out_ref[...] = total.T


def write_plain(total, out_ref):
    out_ref[...] = total


def write_attention(total, *refs):
    riders, refs = refs[: len(refs) - 13], refs[len(refs) - 13 :]
    query_ref, key_ref, value_ref, proj_ref, inner_sum_ref, query_sum_ref, value_sum_ref = refs[:7]
    width = query_ref.shape[1]
    for place, ref in enumerate((query_ref, key_ref, value_ref)):
        ref[...] = total[:, place * width : (place + 1) * width]
    proj_ref[...] = total[:, 3 * width :].T
    if len(riders) > 1:
        own, farther, far, above, beside = (unpack(ref) for ref in riders)
        above = unpack(pack(above + beside))
        sums = (own + above) + (far + farther)
    else:
        sums = unpack(riders[0])
    for k, ref in enumerate(refs[7:]):
        ref[...] = sums[k, :]
    inner_sum_ref[...] = sums[6, :]
    query_sum_ref[...] = sums[7, :width]
    value_sum_ref[...] = sums[7, 2 * width : 3 * width]


def on_device(
    tokens,
    key_mask,
    seq_lengths,
    w_query,
    b_query,
    w_key,
    w_value,
    b_value,
    w_proj,
    b_proj,
    gain_attn,
    shift_attn,
    w_inner,
    b_inner,
    w_outer,
    b_outer,
    gain_ffn,
    shift_ffn,
    out_grad,
):
    in_slots = paired()
    flag = seq_lengths[0, 0] >= 0
    ranks = jnp.stack([lax.axis_index("dp"), lax.axis_index("tensor")]).astype(jnp.int32)
    piece_rows, model_width = tokens.shape
    group_rows = piece_rows * lax.axis_size("tensor")
    half_rows = group_rows // 2
    shard_rows = w_query.shape[0]
    head_width = b_query.shape[0]
    heads = head_width // HEAD_DIM
    inner_width = b_inner.shape[0]
    scale = HEAD_DIM ** (-0.5)
    own = (piece_rows, model_width)
    partial_sums = [shaped((half_rows, model_width), jnp.float32), shaped((half_rows, model_width))]

    attn_shard = kernel_call(
        prepare_kernel,
        [shaped((shard_rows, 4 * head_width))],
        whole=[w_query, w_key, w_value, w_proj],
    )[0]
    shards = kernel_call(
        shards_kernel,
        [shaped((3 * shard_rows, 4 * head_width))],
        whole=[attn_shard, w_inner, w_outer],
    )[0]
    attn_beside, inner_beside, outer_beside = [], [], []
    if in_slots:
        beside = swap(shards, "dp", 1)
        attn_beside, inner_beside, outer_beside = (
            [part(beside, k * shard_rows, shard_rows)] for k in range(3)
        )
    attn_far = far_of(attn_shard)
    attn_above = above_of(attn_shard)
    small = jnp.stack(
        [b_proj, gain_attn, shift_attn, b_outer, gain_ffn, shift_ffn, b_proj, b_proj]
    )

    def tokens_in_part(tokens, out_grad, small):
        tokens, out_grad, small = kernel_call(
            partial(place_kernel, in_slots),
            [shaped(own), shaped(own), shaped(small.shape, jnp.float32)],
            whole=[tokens, out_grad, small],
            scalars=[ranks],
        )
        return tokens, out_grad, small, gather_rows(tokens)

    tokens, out_grad, small, token_rows = region(flag, tokens_in_part, tokens, out_grad, small)
    joined = [shaped((3 * shard_rows, model_width))] if in_slots else []
    inner_shard, *attn_joined = kernel_call(
        pass_kernel,
        [shaped(w_inner.shape), *joined],
        pieces=[[part(shards, shard_rows, shard_rows)]] + [attn_far + attn_above] * in_slots,
        marks=[tokens],
    )
    attn_weights = weight_pieces(
        attn_shard, attn_far, rest_of(attn_joined), attn_above, attn_beside
    )
    inner_far = far_of(inner_shard)
    inner_above = above_of(inner_shard)
    outer_corner = above_of(beside[2 * shard_rows :]) if in_slots else []
    qkv_bias = jnp.concatenate([b_query, jnp.zeros_like(b_query), b_value])[None, :]
    qkv, probs, context = kernel_call(
        partial(attention_kernel, scale),
        [
            shaped((group_rows, 3 * head_width)),
            shaped((heads, group_rows, group_rows)),
            shaped((group_rows, head_width)),
        ],
        scalars=[ranks, seq_lengths],
        whole=[key_mask.reshape(lax.axis_size("tensor"), piece_rows), qkv_bias],
        pieces=[token_rows, attn_weights],
        marks=[inner_shard],
        scratch=[pltpu.VMEM((group_rows, group_rows), jnp.float32)],
    )
    proj_columns = (3 * head_width, head_width)
    proj_weights = [
        part(*p[:3], proj_columns) if isinstance(p, tuple) else part(p, 0, p.shape[0], proj_columns)
        for p in attn_weights
    ]
    near, far, outer_shard, *inner_joined = kernel_call(
        project_kernel,
        [*partial_sums, shaped(inner_shard.shape), *joined],
        pieces=[[context], proj_weights, [part(shards, 2 * shard_rows, shard_rows)]]
        + [inner_far + inner_above] * in_slots,
        marks=outer_corner,
    )
    inner_weights = weight_pieces(
        inner_shard, inner_far, rest_of(inner_joined), inner_above, inner_beside
    )
    outer_far = far_of(outer_shard)
    def first_part(near, far, tokens, small):
        terms = scatter_rows(near, far)
        return kernel_call(
            first_norm_kernel,
            [
                shaped(own, jnp.float32),
                shaped(own, jnp.float32),
                shaped((piece_rows, 1), jnp.float32),
                shaped(own),
            ],
            whole=[small],
            pieces=[*terms, [tokens]],
        )

    first, unit, unit_scale, first_low = region(flag, first_part, near, far, tokens, small)
    *outer_far, outer_shard = tie([*outer_far, outer_shard], [first_low])
    outer_weights = weight_pieces(
        outer_shard,
        outer_far,
        rest_of(outer_far),
        outer_corner + above_of(outer_shard),
        outer_beside,
    )

    def inner_part(first_low, arrived, marks):
        norm_rows = gather_rows(first_low, joined=False)
        return norm_rows[1:], kernel_call(
            inner_kernel,
            [shaped((group_rows, inner_width)), shaped((group_rows, inner_width), jnp.float32)],
            whole=[b_inner[None, :]],
            pieces=[norm_rows, arrived + inner_beside],
            marks=marks,
        )

    other_rows, (active, slope) = region(
        flag,
        inner_part,
        first_low,
        inner_weights[: len(inner_weights) - len(inner_beside)],
        [],
    )
    norm_rows = [first_low, *other_rows]
    near, far = kernel_call(
        outer_kernel,
        [partial_sums[0], [shaped(own)] * 2],
        pieces=[[active], outer_weights],
    )
    terms = scatter_rows(near, far)
    layer_out, second_grad, branch_grad, second_sums = kernel_call(
        partial(second_norm_kernel, in_slots),
        [
            shaped(own),
            shaped(own, jnp.float32),
            shaped(own),
            shaped((8, model_width), jnp.float32),
        ],
        scalars=[ranks, seq_lengths],
        whole=[small],
        pieces=[*terms, [first], [out_grad]],
    )

    branch_rows = gather_rows(branch_grad, joined=False)
    outer_cuts = kernel_call(
        single_grad_kernel,
        weight_cuts(model_width, inner_width),
        pieces=[branch_rows, [active]],
    )
    outer_state = scatter_first(outer_cuts)
    hidden_grad, near, far, inner_sums = kernel_call(
        hidden_grad_kernel,
        [
            shaped((group_rows, inner_width)),
            partial_sums[0],
            [shaped(own)] * 2,
            shaped((1, inner_width), jnp.float32),
        ],
        pieces=[branch_rows, outer_weights, [slope], inner_weights],
        marks=[outer_cuts[0]],
    )

    terms = scatter_rows(near, far)
    inner_cuts = kernel_call(
        single_grad_kernel,
        weight_cuts(model_width, inner_width),
        pieces=[norm_rows, [hidden_grad]],
        marks=terms[1],
    )
    outer_terms, outer_beside, _ = scatter_second(outer_state, [inner_cuts[0]])
    outer_mark = [outer_beside] if in_slots else []
    mix_grad, proj_grad = kernel_call(
        partial(first_back_kernel, in_slots),
        [shaped(own, jnp.float32), shaped((piece_rows + 2 * RIDERS, model_width))],
        scalars=[ranks],
        whole=[unit_scale, small, second_sums],
        pieces=[
            *terms,
            [second_grad],
            [unit],
        ],
        scratch=[pltpu.VMEM((RIDERS, model_width), jnp.float32)],
        us=4 * SLOW,
    )
    inner_state = scatter_first(inner_cuts)

    def row_parts(gathered, first, rows):
        whole = gathered[0].shape[0] // 2
        return [part(g, k * whole + first, rows) for g in gathered for k in range(2)]

    def attention_back_part(proj_grad, marks):
        gathered = gather_rows(proj_grad)
        return kernel_call(
            partial(attention_back_kernel, scale),
            [
                shaped((group_rows, 3 * head_width)),
                *partial_sums,
                *weight_cuts_with_sums(model_width, 4 * head_width),
            ],
            whole=[inner_sums],
            pieces=[
                row_parts(gathered, 0, piece_rows),
                attn_weights,
                [qkv],
                [probs],
                token_rows,
                [context],
                row_parts(gathered, piece_rows, 2 * RIDERS),
            ],
            marks=marks,
            scratch=[pltpu.VMEM((group_rows, head_width), jnp.bfloat16)],
        )[1:]

    near, far, *attn_cuts, sums = region(flag, attention_back_part, proj_grad, outer_mark)
    attn_state = scatter_first(attn_cuts)
    inner_terms, inner_beside, _ = scatter_second(
        inner_state, [attn_state[0], *[t[0] for t in outer_terms[2:]]], us=8 * SLOW
    )

    def tokens_part(near, far, mix_grad, mark):
        terms = scatter_rows(near, far)
        return kernel_call(
            partial(tokens_grad_kernel, in_slots),
            [shaped(own, jnp.float32)],
            scalars=[ranks],
            pieces=[*terms, [mix_grad]],
            marks=[mark],
        )[0]

    tokens_grad = region(flag, tokens_part, near, far, mix_grad, attn_state[0])
    waiting = [outer_beside, inner_beside] if in_slots else []
    attn_terms, beside, riders = scatter_second(
        attn_state, [tokens_grad, *[t[0] for t in inner_terms[2:]]], waiting, [sums] * in_slots
    )
    besides = [[]] * 3
    if in_slots:
        besides = swap(beside, "dp", 1)
        riders.append(part(besides, 3 * shard_rows, 2 * RIDERS))
        besides = [[part(besides, k * shard_rows, shard_rows)] for k in range(3)]
    else:
        riders = [pack(lax.psum(unpack(sums), "dp"))]
    dw_outer = scatter_last(
        outer_terms + besides[1], write_turned, [shaped(w_outer.shape, jnp.float32)]
    )[0]
    dw_inner = scatter_last(
        inner_terms + besides[2], write_plain, [shaped(w_inner.shape, jnp.float32)]
    )[0]
    dw_query, dw_key, dw_value, dw_proj, db_inner, db_query, db_value, *shared = scatter_last(
        attn_terms + besides[0],
        write_attention,
        [shaped(w.shape, jnp.float32) for w in (w_query, w_key, w_value, w_proj)]
        + [shaped(b.shape, jnp.float32) for b in (b_inner, b_query, b_value)]
        + [shaped((model_width,), jnp.float32)] * 6,
        [dw_outer, dw_inner],
        riders,
        False,
    )
    db_proj, dgain_attn, dshift_attn, db_outer, dgain_ffn, dshift_ffn = shared
    return (
        layer_out,
        tokens_grad,
        dw_query,
        db_query,
        dw_key,
        dw_value,
        db_value,
        dw_proj,
        db_proj,
        dgain_attn,
        dshift_attn,
        dw_inner,
        db_inner,
        dw_outer,
        db_outer,
        dgain_ffn,
        dshift_ffn,
    )


def solution(mesh):
    in_specs = (
        P(("dp", "tensor"), None),
        P("dp"),
        P("dp", None),
        P("dp", "tensor"),
        P("tensor"),
        P("dp", "tensor"),
        P("dp", "tensor"),
        P("tensor"),
        P("tensor", "dp"),
        P(),
        P(),
        P(),
        P("dp", "tensor"),
        P("tensor"),
        P("tensor", "dp"),
        P(),
        P(),
        P(),
        P(("dp", "tensor"), None),
    )
    out_specs = (
        P(("dp", "tensor"), None),
        P(("dp", "tensor"), None),
        P("dp", "tensor"),
        P("tensor"),
        P("dp", "tensor"),
        P("dp", "tensor"),
        P("tensor"),
        P("tensor", "dp"),
        P(),
        P(),
        P(),
        P("dp", "tensor"),
        P("tensor"),
        P("tensor", "dp"),
        P(),
        P(),
        P(),
    )
    return jax.shard_map(
        on_device, mesh=mesh, in_specs=in_specs, out_specs=out_specs, check_vma=False
    )
```
